256 devices in a mesh: side: 2 (over core), grp: 8 (over x, z_hi), tp: 16 (over z_lo, y).
Axes of the slice: x: 4, y: 4, z: 8 (z_hi: 2, z_lo: 4; z = z_hi * 4 + z_lo), core: 2. Of those that a mesh axis runs over, the one named last changes fastest.
Arguments:
- tokens: bfloat16 [8192, 8192], P(('side', 'grp'), 'tp'), may hold values from -8 to 8
- norm_gain: bfloat16 [8192], P('tp'), may hold values from 0.25 to 1.75
- wq: bfloat16 [8192, 8192], P('side', 'tp'), may hold values from -1 to 1
- wk: bfloat16 [8192, 1024], P('side', 'tp'), may hold values from -1 to 1
- wv: bfloat16 [8192, 1024], P('side', 'tp'), may hold values from -0.0625 to 0.0625
- wo: bfloat16 [8192, 8192], P('tp', 'side'), may hold values from -0.0625 to 0.0625
- span_offsets: int32 [16], P(('side', 'grp')), may hold values from 0 to 32767
- shared_pages: int32 [16, 32], P(('side', 'grp')), may hold values 0 or 1
- page_owner: int32 [16, 32, 1], P(('side', 'grp')), may hold values from 0 to 7; in each aligned block of 32 rows (0 to 31, 32 to 63, ..., all dimensions but the last counted through in order) at most 6 rows name the same one
- page_ids: int32 [16, 32], P(('side', 'grp')), may hold values from 0 to 65535
Outputs:
- mixed: bfloat16 [8192, 8192], P(('side', 'grp'), 'tp')
- kv_pool: bfloat16 [768, 32768], P(('side', 'grp'), 'tp')
- pool_ids: int32 [768], P(('side', 'grp'))
The draws below stay inside these ranges and needn't reach their ends.
Inputs may be any that keep to these rules, and one draw needn't show every extreme that they name: `page_owner`: within the pages of one prompt block, at most 6 pages name one owner, a bound that some block reaches.
All inputs are finite; a program needn't handle non-finite values. No bound on the sum of `shared_pages` on one device may be relied on, other than what follows from the above.
Results may differ from the reference program's by a relative error of at most 0.02.
Values may be sent and summed in bfloat16 or wider, within the bound.
A program may use at most 128 MiB of HBM per device.

```python
import math
import jax
import jax.numpy as jnp
import numpy as np
from jax import lax

D = 8192
HEADS = 64
KVH = 8
HD = 128
TOK_DEV = 512
PAGE = 16
PROMPTS = 16
TOKENS = 8192
PAGES_DEV = 32
CAP = 6
SLOTS = 768
N_GRP = 8
N_TP = 16


def draw_tokens(key, part):
    own_key = jax.random.fold_in(key, 11)
    return jax.random.truncated_normal(own_key, -6.0, 6.0, (TOKENS, D), jnp.float32).astype(jnp.bfloat16)


def draw_wq(key, part):
    own_key = jax.random.fold_in(key, 21)
    return (jax.random.truncated_normal(own_key, -6.0, 6.0, (D, HEADS * HD), jnp.float32) / math.sqrt(D)).astype(jnp.bfloat16)


def draw_wk(key, part):
    own_key = jax.random.fold_in(key, 31)
    return (jax.random.truncated_normal(own_key, -6.0, 6.0, (D, KVH * HD), jnp.float32) / math.sqrt(D)).astype(jnp.bfloat16)


def with_ends(entries, stream_key, least, top_value):
    shape = entries.shape
    spot = [jax.random.randint(jax.random.fold_in(stream_key, axis), (), 0, shape[axis]) for axis in range(len(shape))]
    entries = entries.at[tuple(spot)].set(least)
    longest = shape.index(max(shape))
    spot[longest] = (spot[longest] + 1) % shape[longest]
    return entries.at[tuple(spot)].set(top_value)


def block_scale(rng, dims, pieces, least, top_value):
    def one(position, blocks):
        draws = jax.random.uniform(jax.random.fold_in(jax.random.fold_in(rng, 6), position), (blocks,), jnp.float32, least / len(pieces), top_value / len(pieces))
        return jnp.repeat(jnp.exp(draws), dims[position] // blocks).reshape((-1,) + (1,) * (len(dims) - position - 1))

    level = one(*pieces[0])
    for cut in pieces[1:]:
        level = level * one(*cut)
    return level


def deal_out(rng, own, number, rows, count, top, reach, slope):
    ranking = jax.random.permutation(rng, count)
    crowded, usual = shares(count, rows * top, reach, slope, True), shares(count, rows * top, reach, slope, False)
    places = jnp.arange(count)

    def named(lengths, turn):
        used = int((lengths > 0).sum())
        fixed = max(1, used // 4)
        shifted = fixed + (places - fixed + turn * (used - fixed)) % max(1, count - fixed)
        return jnp.zeros((count,), jnp.int32).at[ranking[jnp.where(places < fixed, places, shifted)]].set(jnp.asarray(lengths, jnp.int32))

    lengths = jnp.where(number % 4 == 0, named(crowded, number // 4), named(usual, number - number // 4 - 1))
    mixed = jax.random.permutation(jax.random.fold_in(own, 3), count)
    donor, receiver = mixed[0:count // 2 * 2:2], mixed[1:count // 2 * 2:2]
    margin = jnp.minimum(lengths[donor] - 1, reach - lengths[receiver]) // 2
    margin = jnp.where((donor == ranking[0]) | (receiver == ranking[0]) | (lengths[receiver] == 0), 0, jnp.maximum(margin, 0))
    shifted = jax.random.randint(jax.random.fold_in(own, 4), (count // 2,), 0, 1 << 20) % (margin + 1)
    lengths = lengths.at[donor].add(-shifted).at[receiver].add(shifted)
    members = jnp.searchsorted(jnp.cumsum(lengths), jnp.arange(rows * top), side="right").astype(jnp.int32)
    grid = members.reshape(top, rows).T
    grid = grid[jax.random.permutation(jax.random.fold_in(own, 1), rows)]
    turn = jax.random.randint(jax.random.fold_in(own, 2), (rows, 1), 0, top)
    return jnp.take_along_axis(grid, (jnp.arange(top)[None, :] + turn) % top, axis=1)


def shares(number_of, total, reach, lean, full):
    weights = [(1 << 20) // math.isqrt(rank ** lean) + 1 for rank in range(1, number_of + 1)]
    largest = reach if full else min(reach, max(-(-total // number_of), total * weights[0] // sum(weights)))
    least = 1 if total - largest >= number_of - 1 else 0
    holding, spare = [largest] + [least] * (number_of - 1), total - largest - least * (number_of - 1)
    while spare > 0:
        free = [i for i in range(1, number_of) if holding[i] < largest] or [i for i in range(1, number_of) if holding[i] < reach]
        whole, remaining = sum([weights[i] for i in free]), spare
        for i in free:
            more = min(reach - holding[i], max(1, remaining * weights[i] // whole), spare)
            holding[i] = holding[i] + more
            spare = spare - more
    return np.array(holding)


def scatter_about(key, shape, scale, bound, cuts=(), held_as=jnp.bfloat16):
    drawn = jax.random.normal(key, shape, jnp.float32) * scale
    if len(cuts) > 0:
        drawn = block_scale(key, shape, cuts, -0.22, 0.18) * drawn
    return jnp.clip(drawn, min=-bound, max=bound).astype(held_as)


def setup_inputs(seed: int = 0) -> dict:
    arg_keys = jax.random.split(jax.random.key(seed), 11)
    tokens = draw_tokens(jax.random.fold_in(arg_keys[10], 71), 0)
    norm_gain = jnp.clip(1.0 + 0.15 * jax.random.normal(arg_keys[1], (D,), jnp.float32), 0.25, 1.75).astype(jnp.bfloat16)
    wq = draw_wq(jax.random.fold_in(arg_keys[10], 71), 0)
    wk = draw_wk(jax.random.fold_in(arg_keys[10], 71), 0)
    wv = scatter_about(arg_keys[4], (D, KVH * HD), D ** -0.5, 0.0625, ((0, 2), (1, 16)))
    wo = scatter_about(arg_keys[5], (HEADS * HD, D), (HEADS * HD) ** -0.5, 0.0625, ((0, 16), (1, 2)))
    span_offsets = with_ends(jax.random.randint(arg_keys[6], (PROMPTS,), 0, 32768), jax.random.fold_in(arg_keys[6], 1), 0, 32767).astype(jnp.int32)
    shared_pages = with_ends((jax.random.randint(arg_keys[7], (PROMPTS, PAGES_DEV), 0, 4) < 1).astype(jnp.int32), jax.random.fold_in(arg_keys[7], 1), 0, 1)
    page_owner_keys = jax.random.split(jax.random.fold_in(arg_keys[8], 1), PROMPTS * PAGES_DEV // PAGES_DEV)
    page_owner_turns = jax.random.permutation(jax.random.fold_in(arg_keys[8], 3), PROMPTS * PAGES_DEV // PAGES_DEV)
    page_owner = jax.vmap(lambda own, number: deal_out(jax.random.fold_in(arg_keys[8], 2), own, number, PAGES_DEV, N_GRP, 1, CAP, 2))(page_owner_keys, page_owner_turns).reshape((PROMPTS, PAGES_DEV, 1))
    page_ids = with_ends(jax.random.randint(arg_keys[9], (PROMPTS, PAGES_DEV), 0, 65536), jax.random.fold_in(arg_keys[9], 1), 0, 65535).astype(jnp.int32)
    return dict(tokens=tokens, norm_gain=norm_gain, wq=wq, wk=wk, wv=wv, wo=wo, span_offsets=span_offsets, shared_pages=shared_pages, page_owner=page_owner, page_ids=page_ids)


EPS = 1e-05

def rotary(values, positions):
    half = values.shape[-1] // 2
    freq = jnp.exp(-jnp.log(500000.0) * (2.0 * jnp.arange(half, dtype=jnp.float32)) / values.shape[-1])
    angle = positions.astype(jnp.float32)[:, None] * freq[None, :]
    cosine = jnp.cos(angle)[:, None, :]
    sine = jnp.sin(angle)[:, None, :]
    first = values[..., :half]
    second = values[..., half:]
    return jnp.concatenate([first * cosine - second * sine, second * cosine + first * sine], axis=-1)

def reference(tokens, norm_gain, wq, wk, wv, wo, span_offsets, shared_pages, page_owner, page_ids):
    xf = tokens.astype(jnp.float32)
    normed = (xf * lax.rsqrt(lax.optimization_barrier(jnp.mean(xf * xf, axis=-1, keepdims=True)) + EPS) * norm_gain.astype(jnp.float32)).astype(jnp.bfloat16)
    positions = (span_offsets[:, None] + jnp.arange(TOK_DEV, dtype=jnp.int32)[None, :]).reshape(-1)
    q_raw = jnp.dot(normed, wq, preferred_element_type=jnp.float32).reshape(TOKENS, HEADS, HD)
    k_raw = jnp.dot(normed, wk, preferred_element_type=jnp.float32).reshape(TOKENS, KVH, HD)
    v_raw = jnp.dot(normed, wv, preferred_element_type=jnp.float32)
    query = rotary(q_raw, positions).astype(jnp.bfloat16)
    keys = rotary(k_raw, positions).astype(jnp.bfloat16)
    values = v_raw.astype(jnp.bfloat16).reshape(TOKENS, KVH, HD)
    group = HEADS // KVH
    causal = jnp.arange(TOK_DEV)[:, None] >= jnp.arange(TOK_DEV)[None, :]

    def attend(block):
        qb, kb, vb = block
        kx = jnp.repeat(kb, group, axis=1).astype(jnp.float32)
        vx = jnp.repeat(vb, group, axis=1).astype(jnp.float32)
        scores = jnp.einsum('qhd,khd->hqk', qb.astype(jnp.float32), kx) / jnp.sqrt(jnp.float32(HD))
        scores = jnp.where(causal[None], scores, -1e+30)
        top = lax.optimization_barrier(jnp.max(scores, axis=-1, keepdims=True))
        weights = jnp.exp(scores - top)
        probs = (weights / lax.optimization_barrier(jnp.sum(weights, axis=-1, keepdims=True))).astype(jnp.bfloat16)
        return jnp.einsum('hqk,khd->qhd', probs.astype(jnp.float32), vx).astype(jnp.bfloat16)
    context = lax.map(attend, (query.reshape(PROMPTS, TOK_DEV, HEADS, HD), keys.reshape(PROMPTS, TOK_DEV, KVH, HD), values.reshape(PROMPTS, TOK_DEV, KVH, HD)))
    context = context.reshape(TOKENS, N_TP, HEADS * HD // N_TP).transpose(1, 0, 2)
    out_rows = wo.reshape(N_TP, HEADS * HD // N_TP, D)

    def add_group(total, pair):
        part = jnp.dot(pair[0], pair[1], preferred_element_type=jnp.float32).astype(jnp.bfloat16)
        part = lax.optimization_barrier(part)
        return (total + part.astype(jnp.float32), None)
    attended, _ = lax.scan(add_group, jnp.zeros((TOKENS, D), jnp.float32), (context, out_rows))
    mixed = (xf + attended).astype(jnp.bfloat16)
    width = KVH * HD // N_TP
    kp = keys.reshape(PROMPTS, PAGES_DEV, PAGE, N_TP, width)
    vp = values.reshape(PROMPTS, PAGES_DEV, PAGE, N_TP, width)
    rows = jnp.stack([kp, vp], axis=4).transpose(0, 1, 3, 2, 4, 5).reshape(PROMPTS * PAGES_DEV, N_TP * PAGE * 2 * width)
    live = (1 - shared_pages).astype(jnp.int32)
    owner = page_owner[:, :, 0]
    onehot = (owner[:, :, None] == jnp.arange(N_GRP, dtype=jnp.int32)[None, None, :]).astype(jnp.int32) * live[:, :, None]
    rank = lax.optimization_barrier(jnp.sum(jnp.cumsum(onehot, axis=1) * onehot, axis=-1)) - 1
    prompt = jnp.arange(PROMPTS, dtype=jnp.int32)
    src_side = prompt // N_GRP
    src_grp = prompt % N_GRP
    slot = ((1 - src_side)[:, None] * N_GRP + owner) * (N_GRP * CAP) + src_grp[:, None] * CAP + rank
    slot = jnp.where(live == 1, slot, SLOTS).reshape(-1).astype(jnp.int32)
    kv_pool = jnp.zeros((SLOTS, rows.shape[1]), jnp.bfloat16).at[slot].set(rows, mode='drop')
    pool_ids = jnp.full((SLOTS,), -1, jnp.int32).at[slot].set(page_ids.reshape(-1), mode='drop')
    return (mixed, kv_pool, pool_ids)
```

```python
import jax
import jax.numpy as jnp
from jax import lax
from jax.experimental import pallas as pl
from jax.experimental.pallas import tpu as pltpu
from jax.sharding import PartitionSpec as P

KVH = 8
HD = 128
PAGE = 16
EPS = 1e-05
F32 = jnp.float32
BF16 = jnp.bfloat16
MESH = pl.DeviceIdType.MESH
VMEM = pltpu.VMEM

TOK = 512
COLS = 512
KCOLS = 64
NH = 2
RH = TOK // NH
NU = 2 * NH
NK = 2 * NU


def place():
    core = lax.axis_index("side")
    tp = lax.axis_index("tp")
    z = tp // 4
    y = lax.rem(tp, 4)
    m = jnp.where(core == 0, z, 3 - z)
    return core, z, y, m


def at_m(core, m, y):
    z = jnp.where(core == 0, m, 3 - m)
    return z * 4 + y


def greet(core, z, y, extra=()):
    barrier = pltpu.get_barrier_semaphore()
    near = [
        {"tp": lax.rem(z + 1, 4) * 4 + y},
        {"tp": lax.rem(z + 3, 4) * 4 + y},
        {"tp": z * 4 + lax.rem(y + 1, 4)},
        {"tp": z * 4 + lax.rem(y + 3, 4)},
        {"side": 1 - core},
    ]
    for one in near:
        pl.semaphore_signal(barrier, inc=1, device_id=one, device_id_type=MESH)
    count = len(near)
    return barrier, count


def gather_kernel(
    tok_ref, gain_ref, wq_hbm, wk_ref, wv_ref, q_ref, kv_ref,
    blocks, own, wq_v, wkv_v, acc_q, acc_kv, got_q, got_kv,
    w_sem, d_send, d_recv, up_send, up_recv, dn_send, dn_recv,
    yp_send, yp_recv, ym_send, ym_recv, fw_send, fw_recv, x_send, x_recv,
):
    core, z, y, m = place()
    root = z // 2
    weights = pltpu.make_async_copy(wq_hbm, wq_v, w_sem)
    weights.start()
    barrier, count = greet(core, z, y)
    own_zz = lax.rem(z, 2)

    for h in range(NH):
        scaled = (
            tok_ref[h * RH:(h + 1) * RH, :].astype(F32) * gain_ref[...].astype(F32)
        ).astype(BF16)
        own[h] = scaled

    def to_root(h):
        return pltpu.make_async_remote_copy(
            src_ref=own.at[h], dst_ref=blocks.at[own_zz, y, core, h],
            send_sem=d_send.at[h], recv_sem=d_recv.at[h],
            device_id={"side": 1 - core}, device_id_type=MESH,
        )

    pl.semaphore_wait(barrier, count)

    @pl.when(root != core)
    def _():
        for h in range(NH):
            to_root(h).start()

    @pl.when(root == core)
    def _():
        for h in range(NH):
            blocks[own_zz, y, core, h] = own[h]

    acc_q[...] = jnp.zeros_like(acc_q)
    acc_kv[...] = jnp.zeros_like(acc_kv)
    wkv_v[:, :, :, :KCOLS] = wk_ref[...]
    wkv_v[:, :, :, KCOLS:] = wv_ref[...]

    up = {"tp": at_m(core, lax.rem(m + 1, 4), y)}
    down = {"tp": at_m(core, lax.rem(m + 3, 4), y)}
    yp = {"tp": z * 4 + lax.rem(y + 1, 4)}
    ym = {"tp": z * 4 + lax.rem(y + 3, 4)}
    y1, y2, y3 = lax.rem(y + 1, 4), lax.rem(y + 2, 4), lax.rem(y + 3, 4)

    def unit(k):
        u = k // 2
        b = 1 - lax.rem(k, 2)
        zz = jnp.where(core == 0, b, 1 - b)
        first = u == 0
        mid = u <= NH
        side = jnp.where(first, core, jnp.where(mid, 1 - core, core))
        h = jnp.where(first, 0, jnp.where(mid, u - 1, u - NH))
        return b, zz, side, h

    def copy(ref, send, recv, to):
        return pltpu.make_async_remote_copy(
            src_ref=ref, dst_ref=ref, send_sem=send, recv_sem=recv,
            device_id=to, device_id_type=MESH,
        )

    def line(k):
        b, zz, side, h = unit(k)
        ref = blocks.at[zz, y, side, h]
        is_root = m == b

        @pl.when(is_root & (side != core))
        def _():
            copy(ref, d_send.at[h], d_recv.at[h], {"side": 1 - core}).wait_recv()

        @pl.when(m > b)
        def _():
            copy(ref, up_send.at[k], up_recv.at[k], up).wait_recv()

        @pl.when(m < b)
        def _():
            copy(ref, dn_send.at[k], dn_recv.at[k], down).wait_recv()

        @pl.when((m >= b) & (m < 3))
        def _():
            copy(ref, up_send.at[k], up_recv.at[k], up).start()

        @pl.when((m == 1) & (b == 1))
        def _():
            copy(ref, dn_send.at[k], dn_recv.at[k], down).start()

        copy(ref, yp_send.at[k], yp_recv.at[k], yp).start()
        copy(ref, ym_send.at[k], ym_recv.at[k], ym).start()

    def ring(k):
        b, zz, side, h = unit(k)
        low = blocks.at[zz, y3, side, h]
        high = blocks.at[zz, y1, side, h]
        copy(low, yp_send.at[k], yp_recv.at[k], yp).wait_recv()

        @pl.when(lax.rem(h, 2) == 0)
        def _():
            copy(low, fw_send.at[k], fw_recv.at[k], yp).start()

        copy(high, ym_send.at[k], ym_recv.at[k], ym).wait_recv()

        @pl.when(lax.rem(h, 2) == 1)
        def _():
            copy(high, fw_send.at[k], fw_recv.at[k], ym).start()

    def swap(which):
        if which == 0:
            return pltpu.make_async_remote_copy(
                src_ref=acc_q.at[1 - core], dst_ref=got_q, send_sem=x_send.at[0],
                recv_sem=x_recv.at[0], device_id={"side": 1 - core}, device_id_type=MESH)
        return pltpu.make_async_remote_copy(
            src_ref=acc_kv.at[1 - core], dst_ref=got_kv, send_sem=x_send.at[1],
            recv_sem=x_recv.at[1], device_id={"side": 1 - core}, device_id_type=MESH)

    def multiply(k):
        b, zz, side, h = unit(k)
        far = blocks.at[zz, y2, side, h]
        copy(far, fw_send.at[k], fw_recv.at[k], yp).wait_recv()
        rows = pl.ds(pl.multiple_of(h * RH, RH), RH)
        total_q = acc_q[side, rows, :]
        total_kv = acc_kv[side, rows, :]
        for yy in range(4):
            x = blocks[zz, yy, side, h]
            total_q += jnp.dot(x, wq_v[zz, yy], preferred_element_type=F32)
            total_kv += jnp.dot(x, wkv_v[zz, yy], preferred_element_type=F32)
        acc_q[side, rows, :] = total_q
        acc_kv[side, rows, :] = total_kv

        @pl.when(k == 2 * NH + 1)
        def _():
            swap(0).start()
            swap(1).start()

    LAG = 2
    weights.wait()

    def step(k, carry):
        @pl.when(k < NK)
        def _():
            line(k)

        @pl.when((k >= LAG) & (k < NK + LAG))
        def _():
            ring(k - LAG)

        @pl.when(k >= LAG + 1)
        def _():
            multiply(k - LAG - 1)
        return carry

    lax.fori_loop(0, NK + LAG + 1, step, 0)

    swap(0).wait()
    swap(1).wait()
    q_ref[...] = acc_q[core] + got_q[...]
    kv_ref[...] = acc_kv[core] + got_kv[...]

    @pl.when(root != core)
    def _():
        for h in range(NH):
            to_root(h).wait_send()

    def drain(k, carry):
        b, zz, side, h = unit(k)
        ref = blocks.at[zz, y, side, h]

        @pl.when((m >= b) & (m < 3))
        def _():
            copy(ref, up_send.at[k], up_recv.at[k], up).wait_send()

        @pl.when((m == 1) & (b == 1))
        def _():
            copy(ref, dn_send.at[k], dn_recv.at[k], down).wait_send()

        copy(ref, yp_send.at[k], yp_recv.at[k], yp).wait_send()
        copy(ref, ym_send.at[k], ym_recv.at[k], ym).wait_send()
        copy(ref, fw_send.at[k], fw_recv.at[k], yp).wait_send()
        return carry

    lax.fori_loop(0, NK, drain, 0)


def gather_project(tokens, gain, wq, wk, wv):
    sem = pltpu.SemaphoreType.DMA
    vm = pl.BlockSpec(memory_space=VMEM)
    return pl.pallas_call(
        gather_kernel,
        out_shape=(
            jax.ShapeDtypeStruct((TOK, COLS), F32),
            jax.ShapeDtypeStruct((TOK, 2 * KCOLS), F32),
        ),
        in_specs=[vm, vm, pl.BlockSpec(memory_space=pl.ANY), vm, vm],
        out_specs=(vm, vm),
        scratch_shapes=[
            VMEM((2, 4, 2, NH, RH, COLS), BF16),
            VMEM((NH, RH, COLS), BF16),
            VMEM((2, 4, COLS, COLS), BF16),
            VMEM((2, 4, COLS, 2 * KCOLS), BF16),
            VMEM((2, TOK, COLS), F32),
            VMEM((2, TOK, 2 * KCOLS), F32),
            VMEM((TOK, COLS), F32),
            VMEM((TOK, 2 * KCOLS), F32),
            sem, sem((NH,)), sem((NH,)),
        ] + [sem((NK,))] * 10 + [sem((2,)), sem((2,))],
        compiler_params=pltpu.CompilerParams(
            collective_id=0, has_side_effects=True, vmem_limit_bytes=48 * 2**20
        ),
        cost_estimate=pl.CostEstimate(
            flops=2 * 1024 * 4096 * 640, bytes_accessed=8 * 2**20, transcendentals=0
        ),
    )(
        tokens, gain.reshape(1, COLS), wq.reshape(2, 4, COLS, COLS),
        wk.reshape(2, 4, COLS, KCOLS), wv.reshape(2, 4, COLS, KCOLS),
    )


def partner(block, axis, apart):
    count = lax.axis_size(axis)
    route = []
    for low in range(count):
        high = low | 1 << apart
        if high != low and high < count:
            route += [(low, high), (high, low)]
    return lax.ppermute(block, axis, route)


def from_behind(value, axis, steps):
    count = lax.axis_size(axis)
    pairs = [(source, (source + steps) % count) for source in range(count)]
    return lax.ppermute(value, axis, pairs)


def rotary(values, positions):
    half = values.shape[-1] // 2
    freq = jnp.exp(
        -jnp.log(500000.0) * (2.0 * jnp.arange(half, dtype=jnp.float32)) / values.shape[-1]
    )
    angle = positions.astype(jnp.float32)[:, None] * freq[None, :]
    cosine = jnp.cos(angle)[:, None, :]
    sine = jnp.sin(angle)[:, None, :]
    first = values[..., :half]
    second = values[..., half:]
    return jnp.concatenate(
        [first * cosine - second * sine, second * cosine + first * sine], axis=-1
    )


def shards(tokens, norm_gain, wq, wk, wv, wo, span_offsets, shared_pages, page_owner, page_ids):
    count = tokens.shape[0]
    xf = tokens.astype(F32)
    squares = lax.psum(jnp.sum(xf * xf, axis=1, keepdims=True), "tp")
    q_raw, kv_raw = gather_project(tokens, norm_gain, wq, wk, wv)
    scale = lax.rsqrt(squares / 8192.0 + EPS)
    qcols = wq.shape[1]
    kcols = wk.shape[1]
    q_raw = q_raw * scale
    kv_raw = kv_raw * scale
    k_raw = kv_raw[:, :kcols]
    v_raw = kv_raw[:, kcols:]
    positions = span_offsets[0] + jnp.arange(count, dtype=jnp.int32)
    tp_index = lax.axis_index("tp")
    sharing = lax.axis_size("tp") // KVH
    k_block = k_raw
    v_block = v_raw
    other_k = partner(k_block.astype(jnp.bfloat16), "tp", 0).astype(k_block.dtype)
    other_v = partner(v_block.astype(jnp.bfloat16), "tp", 0).astype(v_block.dtype)
    upper_half = tp_index // (1 << 0) % 2 == 1
    k_block = jnp.where(
        upper_half,
        jnp.concatenate([other_k, k_block], axis=1),
        jnp.concatenate([k_block, other_k], axis=1),
    )
    v_block = jnp.where(
        upper_half,
        jnp.concatenate([other_v, v_block], axis=1),
        jnp.concatenate([v_block, other_v], axis=1),
    )
    query = rotary(q_raw.reshape(count, qcols // HD, HD), positions).astype(jnp.bfloat16)
    keys = rotary(k_block.reshape(count, 1, HD), positions).astype(jnp.bfloat16).reshape(count, HD)
    values = v_block.astype(jnp.bfloat16)
    scores = jnp.einsum("qhd,kd->hqk", query, keys, preferred_element_type=jnp.float32) / jnp.sqrt(
        jnp.float32(HD)
    )
    causal = jnp.arange(count)[:, None] >= jnp.arange(count)[None, :]
    scores = jnp.where(causal[None], scores, -1e30)
    top = jnp.max(scores, axis=-1, keepdims=True)
    weights = jnp.exp(scores - top)
    probs = (weights / jnp.sum(weights, axis=-1, keepdims=True)).astype(jnp.bfloat16)
    context = (
        jnp.einsum("hqk,kd->qhd", probs, values, preferred_element_type=jnp.float32)
        .astype(jnp.bfloat16)
        .reshape(count, qcols)
    )
    terms = jnp.dot(
        context, lax.all_gather(wo, "side", axis=1, tiled=True), preferred_element_type=jnp.float32
    )
    attended = lax.psum_scatter(
        terms.astype(jnp.bfloat16), "tp", scatter_dimension=1, tiled=True
    ).astype(jnp.float32)
    mixed = (tokens.astype(jnp.float32) + attended).astype(jnp.bfloat16)
    pages_dev = count // PAGE
    groups = lax.axis_size("grp")
    cap = max(2, 3 * pages_dev // (2 * groups))
    within_head = tp_index % sharing * kcols
    k_own = lax.dynamic_slice_in_dim(keys, within_head, kcols, 1)
    v_own = lax.dynamic_slice_in_dim(values, within_head, kcols, 1)
    rows = jnp.stack(
        [k_own.reshape(pages_dev, PAGE, kcols), v_own.reshape(pages_dev, PAGE, kcols)], axis=2
    ).reshape(pages_dev, PAGE * 2 * kcols)
    live = 1 - shared_pages[0]
    owner = page_owner[0, :, 0]
    onehot = (owner[:, None] == jnp.arange(groups, dtype=jnp.int32)[None, :]).astype(
        jnp.int32
    ) * live[:, None]
    rank = jnp.sum(jnp.cumsum(onehot, axis=0) * onehot, axis=1) - 1
    slots_count = groups * cap
    select = (
        (owner * cap + rank)[None, :] == jnp.arange(slots_count, dtype=jnp.int32)[:, None]
    ) & (live[None, :] == 1)
    buffer = jnp.dot(select.astype(jnp.bfloat16), rows, preferred_element_type=jnp.float32).astype(
        jnp.bfloat16
    )
    id_buffer = jnp.sum(select.astype(jnp.int32) * (page_ids[0] + 1)[None, :], axis=1) - 1
    buffer, id_buffer = (
        buffer.reshape(slots_count // cap, cap, rows.shape[1]),
        id_buffer.reshape(slots_count // cap, cap),
    )
    moved = (
        lax.all_to_all(buffer, "grp", split_axis=0, concat_axis=0, tiled=True),
        lax.all_to_all(id_buffer, "grp", split_axis=0, concat_axis=0, tiled=True),
    )
    got_pages, got_ids = from_behind((moved[0], moved[1]), "side", 1)
    kv_pool = got_pages.reshape(groups * cap, rows.shape[1])
    pool_ids = got_ids.reshape(groups * cap)
    return (mixed, kv_pool, pool_ids)


def solution(mesh):
    in_specs = (
        P(("side", "grp"), "tp"),
        P("tp"),
        P("side", "tp"),
        P("side", "tp"),
        P("side", "tp"),
        P("tp", "side"),
        P(("side", "grp")),
        P(("side", "grp"), None),
        P(("side", "grp"), None, None),
        P(("side", "grp"), None),
    )
    out_specs = (P(("side", "grp"), "tp"), P(("side", "grp"), "tp"), P(("side", "grp")))
    return jax.shard_map(shards, mesh=mesh, in_specs=in_specs, out_specs=out_specs, check_vma=False)
```

```python
import jax
import jax.numpy as jnp
from jax import lax
from jax.experimental import pallas as pl
from jax.experimental.pallas import tpu as pltpu
from jax.sharding import PartitionSpec as P

KVH = 8
HD = 128
PAGE = 16
EPS = 1e-05
F32 = jnp.float32
BF16 = jnp.bfloat16
MESH = pl.DeviceIdType.MESH
VMEM = pltpu.VMEM

TOK = 512
COLS = 512
KCOLS = 64
NH = 2
RH = TOK // NH
NU = 2 * NH
NK = 2 * NU
WO_Z = 1
WO_X = 3
WO_D = 8


def place():
    core = lax.axis_index("side")
    tp = lax.axis_index("tp")
    z = tp // 4
    y = lax.rem(tp, 4)
    m = jnp.where(core == 0, z, 3 - z)
    return core, z, y, m


def at_m(core, m, y):
    z = jnp.where(core == 0, m, 3 - m)
    return z * 4 + y


def greet(near):
    barrier = pltpu.get_barrier_semaphore()
    for one in near:
        pl.semaphore_signal(barrier, inc=1, device_id=one, device_id_type=MESH)
    count = len(near)
    return barrier, count


def gather_kernel(
    tok_ref, gain_ref, wq_hbm, wk_ref, wv_ref, wo_hbm, q_ref, kv_ref, wo_all,
    sq, blocks, own, wq_v, wkv_v, acc_q, acc_kv, got_q, got_kv,
    w_sem, d_send, d_recv, up_send, up_recv, dn_send, dn_recv,
    yp_send, yp_recv, ym_send, ym_recv, fw_send, fw_recv, x_send, x_recv,
    sy_send, sy_recv, sz_send, sz_recv,
    wz_send, wz_recv, wx_send, wx_recv, wd_send, wd_recv, wl_sem,
):
    core, z, y, m = place()
    root = z // 2
    weights = pltpu.make_async_copy(wq_hbm, wq_v, w_sem)
    weights.start()
    grp = lax.axis_index("grp")
    x = grp // 2
    z_hi = lax.rem(grp, 2)
    home = z // 2 == core
    z_near = [{"tp": lax.rem(z + d, 4) * 4 + y} for d in (1, 2, 3)]
    y_near = [{"tp": z * 4 + lax.rem(y + d, 4)} for d in (1, 2, 3)]
    x_near = [{"grp": lax.rem(x + d, 4) * 2 + z_hi} for d in (1, 2, 3)]
    sibling = {"side": 1 - core}
    barrier, count = greet(z_near + y_near + x_near + [sibling])
    own_zz = lax.rem(z, 2)

    for h in range(NH):
        scaled = (
            tok_ref[h * RH:(h + 1) * RH, :].astype(F32) * gain_ref[...].astype(F32)
        ).astype(BF16)
        own[h] = scaled
    xf = tok_ref[...].astype(F32)
    sq[0] = lax.dot_general(
        jnp.ones((8, COLS), F32), xf * xf, (((1,), (1,)), ((), ())),
        precision=lax.Precision.HIGHEST, preferred_element_type=F32,
    )

    def to_root(h):
        return pltpu.make_async_remote_copy(
            src_ref=own.at[h], dst_ref=blocks.at[own_zz, y, core, h],
            send_sem=d_send.at[h], recv_sem=d_recv.at[h],
            device_id={"side": 1 - core}, device_id_type=MESH,
        )

    pl.semaphore_wait(barrier, count)

    @pl.when(root != core)
    def _():
        for h in range(NH):
            to_root(h).start()

    @pl.when(root == core)
    def _():
        for h in range(NH):
            blocks[own_zz, y, core, h] = own[h]

    def sum_y(d):
        return pltpu.make_async_remote_copy(
            src_ref=sq.at[0], dst_ref=sq.at[d], send_sem=sy_send.at[d - 1],
            recv_sem=sy_recv.at[d - 1], device_id=y_near[d - 1], device_id_type=MESH)

    def sum_z(d):
        return pltpu.make_async_remote_copy(
            src_ref=sq.at[4], dst_ref=sq.at[4 + d], send_sem=sz_send.at[d - 1],
            recv_sem=sz_recv.at[d - 1], device_id=z_near[d - 1], device_id_type=MESH)

    def wo_line(zz):
        z_to = 2 * core + zz
        return pltpu.make_async_remote_copy(
            src_ref=wo_hbm.at[x, :, zz * 2048:(zz + 1) * 2048],
            dst_ref=wo_all.at[z, x], send_sem=wz_send.at[zz], recv_sem=wz_recv.at[z],
            device_id={"tp": z_to * 4 + y}, device_id_type=MESH)

    def wo_row(d, e):
        ref = wo_all.at[lax.rem(z + d, 4), x]
        return pltpu.make_async_remote_copy(
            src_ref=ref, dst_ref=ref, send_sem=wx_send.at[d - 1, e - 1],
            recv_sem=wx_recv.at[d - 1, e - 1], device_id=x_near[e - 1], device_id_type=MESH)

    own_cols = pl.ds(pl.multiple_of(own_zz * 2048, 2048), 2048)

    def wo_local():
        return pltpu.make_async_copy(wo_hbm.at[:, :, own_cols], wo_all.at[z], wl_sem)

    def wo_cross(d):
        here = wo_all.at[lax.rem(z + d, 4)]
        return pltpu.make_async_remote_copy(
            src_ref=wo_hbm.at[:, :, own_cols] if d == 0 else here, dst_ref=here,
            send_sem=wd_send.at[d], recv_sem=wd_recv.at[d],
            device_id=sibling, device_id_type=MESH)

    def redistribute(k):
        @pl.when(k == WO_Z)
        def _():
            for zz in range(2):
                @pl.when(2 * core + zz != z)
                def _():
                    wo_line(zz).start()

            @pl.when(home)
            def _():
                wo_local().start()
                wo_cross(0).start()

        for d in (1, 2, 3):
            z_from = lax.rem(z + d, 4)

            @pl.when(home & (k == WO_X + jnp.abs(z_from - z) - 1))
            def _():
                ref = wo_all.at[z_from, x]
                pltpu.make_async_remote_copy(
                    src_ref=ref, dst_ref=ref, send_sem=wz_send.at[0],
                    recv_sem=wz_recv.at[z_from], device_id=z_near[d - 1],
                    device_id_type=MESH).wait_recv()
                for e in (1, 2, 3):
                    wo_row(d, e).start()

            @pl.when(home & (k == WO_D + jnp.abs(z_from - z) - 1))
            def _():
                for e in (1, 2, 3):
                    wo_row(d, e).wait_recv()
                wo_cross(d).start()

    for d in (1, 2, 3):
        sum_y(d).start()
    acc_q[...] = jnp.zeros_like(acc_q)
    acc_kv[...] = jnp.zeros_like(acc_kv)
    wkv_v[:, :, :, :KCOLS] = wk_ref[...]
    wkv_v[:, :, :, KCOLS:] = wv_ref[...]

    up = {"tp": at_m(core, lax.rem(m + 1, 4), y)}
    down = {"tp": at_m(core, lax.rem(m + 3, 4), y)}
    yp = {"tp": z * 4 + lax.rem(y + 1, 4)}
    ym = {"tp": z * 4 + lax.rem(y + 3, 4)}
    y1, y2, y3 = lax.rem(y + 1, 4), lax.rem(y + 2, 4), lax.rem(y + 3, 4)

    def unit(k):
        u = k // 2
        b = 1 - lax.rem(k, 2)
        zz = jnp.where(core == 0, b, 1 - b)
        first = u == 0
        mid = u <= NH
        side = jnp.where(first, core, jnp.where(mid, 1 - core, core))
        h = jnp.where(first, 0, jnp.where(mid, u - 1, u - NH))
        return b, zz, side, h

    def copy(ref, send, recv, to):
        return pltpu.make_async_remote_copy(
            src_ref=ref, dst_ref=ref, send_sem=send, recv_sem=recv,
            device_id=to, device_id_type=MESH,
        )

    def line(k):
        b, zz, side, h = unit(k)
        ref = blocks.at[zz, y, side, h]
        is_root = m == b

        @pl.when(is_root & (side != core))
        def _():
            copy(ref, d_send.at[h], d_recv.at[h], {"side": 1 - core}).wait_recv()

        @pl.when(m > b)
        def _():
            copy(ref, up_send.at[k], up_recv.at[k], up).wait_recv()

        @pl.when(m < b)
        def _():
            copy(ref, dn_send.at[k], dn_recv.at[k], down).wait_recv()

        @pl.when((m >= b) & (m < 3))
        def _():
            copy(ref, up_send.at[k], up_recv.at[k], up).start()

        @pl.when((m == 1) & (b == 1))
        def _():
            copy(ref, dn_send.at[k], dn_recv.at[k], down).start()

        copy(ref, yp_send.at[k], yp_recv.at[k], yp).start()
        copy(ref, ym_send.at[k], ym_recv.at[k], ym).start()

    def ring(k):
        b, zz, side, h = unit(k)
        low = blocks.at[zz, y3, side, h]
        high = blocks.at[zz, y1, side, h]
        copy(low, yp_send.at[k], yp_recv.at[k], yp).wait_recv()

        @pl.when(lax.rem(h, 2) == 0)
        def _():
            copy(low, fw_send.at[k], fw_recv.at[k], yp).start()

        copy(high, ym_send.at[k], ym_recv.at[k], ym).wait_recv()

        @pl.when(lax.rem(h, 2) == 1)
        def _():
            copy(high, fw_send.at[k], fw_recv.at[k], ym).start()

    def swap(which):
        if which == 0:
            return pltpu.make_async_remote_copy(
                src_ref=acc_q.at[1 - core], dst_ref=got_q, send_sem=x_send.at[0],
                recv_sem=x_recv.at[0], device_id={"side": 1 - core}, device_id_type=MESH)
        return pltpu.make_async_remote_copy(
            src_ref=acc_kv.at[1 - core], dst_ref=got_kv, send_sem=x_send.at[1],
            recv_sem=x_recv.at[1], device_id={"side": 1 - core}, device_id_type=MESH)

    def multiply(k):
        b, zz, side, h = unit(k)
        far = blocks.at[zz, y2, side, h]
        copy(far, fw_send.at[k], fw_recv.at[k], yp).wait_recv()
        rows = pl.ds(pl.multiple_of(h * RH, RH), RH)
        total_q = acc_q[side, rows, :]
        total_kv = acc_kv[side, rows, :]
        for yy in range(4):
            x = blocks[zz, yy, side, h]
            total_q += jnp.dot(x, wq_v[zz, yy], preferred_element_type=F32)
            total_kv += jnp.dot(x, wkv_v[zz, yy], preferred_element_type=F32)
        acc_q[side, rows, :] = total_q
        acc_kv[side, rows, :] = total_kv

        @pl.when(k == 2 * NH + 1)
        def _():
            swap(0).start()
            swap(1).start()

    LAG = 2
    weights.wait()

    def step(k, carry):
        @pl.when(k < NK)
        def _():
            line(k)

        @pl.when((k >= LAG) & (k < NK + LAG))
        def _():
            ring(k - LAG)

        @pl.when(k >= LAG + 1)
        def _():
            multiply(k - LAG - 1)

        redistribute(k)

        @pl.when(k == 3)
        def _():
            for d in (1, 2, 3):
                sum_y(d).wait_recv()
            sq[4] = sq[0] + sq[1] + sq[2] + sq[3]
            for d in (1, 2, 3):
                sum_z(d).start()
        return carry

    lax.fori_loop(0, NK + LAG + 1, step, 0)

    swap(0).wait()
    swap(1).wait()
    for d in (1, 2, 3):
        sum_z(d).wait_recv()
    total = (sq[4] + sq[5] + sq[6] + sq[7]).T[:, :1]
    scale = lax.rsqrt(total * (1.0 / 8192.0) + EPS)
    q_ref[...] = (acc_q[core] + got_q[...]) * scale
    kv_ref[...] = (acc_kv[core] + got_kv[...]) * scale

    for d in (1, 2, 3):
        sum_y(d).wait_send()
        sum_z(d).wait_send()
    for zz in range(2):
        @pl.when(2 * core + zz != z)
        def _():
            wo_line(zz).wait_send()

    @pl.when(home)
    def _():
        wo_local().wait()
        for d in range(4):
            wo_cross(d).wait_send()
        for d in (1, 2, 3):
            for e in (1, 2, 3):
                wo_row(d, e).wait_send()

    @pl.when(jnp.logical_not(home))
    def _():
        for d in range(4):
            wo_cross(d).wait_recv()

    @pl.when(root != core)
    def _():
        for h in range(NH):
            to_root(h).wait_send()

    def drain(k, carry):
        b, zz, side, h = unit(k)
        ref = blocks.at[zz, y, side, h]

        @pl.when((m >= b) & (m < 3))
        def _():
            copy(ref, up_send.at[k], up_recv.at[k], up).wait_send()

        @pl.when((m == 1) & (b == 1))
        def _():
            copy(ref, dn_send.at[k], dn_recv.at[k], down).wait_send()

        copy(ref, yp_send.at[k], yp_recv.at[k], yp).wait_send()
        copy(ref, ym_send.at[k], ym_recv.at[k], ym).wait_send()
        copy(ref, fw_send.at[k], fw_recv.at[k], yp).wait_send()
        return carry

    lax.fori_loop(0, NK, drain, 0)


def gather_project(tokens, gain, wq, wk, wv, wo):
    sem = pltpu.SemaphoreType.DMA
    vm = pl.BlockSpec(memory_space=VMEM)
    return pl.pallas_call(
        gather_kernel,
        out_shape=(
            jax.ShapeDtypeStruct((TOK, COLS), F32),
            jax.ShapeDtypeStruct((TOK, 2 * KCOLS), F32),
            jax.ShapeDtypeStruct((4, 4, 128, 2048), BF16),
        ),
        in_specs=[vm, vm, pl.BlockSpec(memory_space=pl.ANY), vm, vm,
                  pl.BlockSpec(memory_space=pl.ANY)],
        out_specs=(vm, vm, pl.BlockSpec(memory_space=pl.ANY)),
        scratch_shapes=[
            VMEM((8, 8, TOK), F32),
            VMEM((2, 4, 2, NH, RH, COLS), BF16),
            VMEM((NH, RH, COLS), BF16),
            VMEM((2, 4, COLS, COLS), BF16),
            VMEM((2, 4, COLS, 2 * KCOLS), BF16),
            VMEM((2, TOK, COLS), F32),
            VMEM((2, TOK, 2 * KCOLS), F32),
            VMEM((TOK, COLS), F32),
            VMEM((TOK, 2 * KCOLS), F32),
            sem, sem((NH,)), sem((NH,)),
        ] + [sem((NK,))] * 10 + [
            sem((2,)), sem((2,)), sem((3,)), sem((3,)), sem((3,)), sem((3,)),
            sem((2,)), sem((4,)), sem((3, 3)), sem((3, 3)), sem((4,)), sem((4,)), sem,
        ],
        compiler_params=pltpu.CompilerParams(
            collective_id=0, has_side_effects=True, vmem_limit_bytes=48 * 2**20
        ),
        cost_estimate=pl.CostEstimate(
            flops=2 * 1024 * 4096 * 640, bytes_accessed=8 * 2**20, transcendentals=0
        ),
    )(
        tokens, gain.reshape(1, COLS), wq.reshape(2, 4, COLS, COLS),
        wk.reshape(2, 4, COLS, KCOLS), wv.reshape(2, 4, COLS, KCOLS),
        wo.reshape(4, 128, 4096),
    )


NT = 4
RT = TOK // NT
HT = RT // 2


def output_kernel(
    ctx_ref, tok_ref, wo_hbm, pages_ref, ids_ref, mixed_ref, pool_ref, pool_ids_ref,
    ctx, wo, opp_out, opp_in, near_out, near_in, near_part, own_part,
    w_sem, up_send, up_recv, dn_send, dn_recv, a_send, a_recv, b_send, b_recv,
    p_send, p_recv, i_send, i_recv,
):
    core, z, y, m = place()
    grp = lax.axis_index("grp")

    def weights(zs, yy):
        return pltpu.make_async_copy(
            wo_hbm.at[zs, :, yy * COLS:(yy + 1) * COLS], wo.at[zs, yy], w_sem.at[zs, yy])

    for zs in range(4):
        for yy in range(4):
            weights(zs, yy).start()
    owners = [{"side": 1 - core, "grp": jnp.int32(o)} for o in range(8)]
    up = {"tp": lax.rem(z + 1, 4) * 4 + y}
    down = {"tp": lax.rem(z + 3, 4) * 4 + y}
    yp = {"tp": z * 4 + lax.rem(y + 1, 4)}
    ym = {"tp": z * 4 + lax.rem(y + 3, 4)}
    barrier, count = greet([up, down, yp, ym] + owners)
    ctx[z] = ctx_ref[...]
    pl.semaphore_wait(barrier, count)

    def copy(src, dst, send, recv, to):
        return pltpu.make_async_remote_copy(
            src_ref=src, dst_ref=dst, send_sem=send, recv_sem=recv,
            device_id=to, device_id_type=MESH)

    def climb(zs, t):
        ref = ctx.at[zs, t]
        return copy(ref, ref, up_send.at[zs, t], up_recv.at[zs, t], up)

    def descend(zs, t):
        ref = ctx.at[zs, t]
        return copy(ref, ref, dn_send.at[zs, t], dn_recv.at[zs, t], down)

    def opposite(t, way):
        return copy(opp_out.at[t, way], opp_in.at[t, way], a_send.at[t, way],
                    a_recv.at[t, way], (yp, ym)[way])

    def neighbour(t, way):
        return copy(near_out.at[t, way], near_in.at[t, way], b_send.at[t, way],
                    b_recv.at[t, way], (yp, ym)[way])

    def page(o):
        return copy(pages_ref.at[o], pool_ref.at[grp], p_send.at[o], p_recv.at[grp], owners[o])

    def page_id(o):
        return copy(ids_ref.at[o], pool_ids_ref.at[grp], i_send.at[o], i_recv.at[grp], owners[o])

    def launch(t):
        @pl.when(z < 3)
        def _():
            climb(z, t).start()

        @pl.when(z > 0)
        def _():
            descend(z, t).start()

    def fetch(t):
        @pl.when(t < NT - 1)
        def _():
            launch(t + 1)

        for d in (1, 2, 3):
            @pl.when(z - d >= 0)
            def _():
                climb(z - d, t).wait_recv()

                @pl.when(z < 3)
                def _():
                    climb(z - d, t).start()

            @pl.when(z + d <= 3)
            def _():
                descend(z + d, t).wait_recv()

                @pl.when(z > 0)
                def _():
                    descend(z + d, t).start()

    def product(t, r):
        yy = lax.rem(y + r, 4)
        total = jnp.dot(ctx[0, t], wo[0, yy], preferred_element_type=F32)
        for zs in (1, 2, 3):
            total += jnp.dot(ctx[zs, t], wo[zs, yy], preferred_element_type=F32)
        return total

    def compute(t):
        far = product(t, 2).astype(BF16)
        for way in (0, 1):
            opp_out[t, way] = far[way * HT:(way + 1) * HT]
            opposite(t, way).start()
        near_part[t, 0] = product(t, 1)
        near_part[t, 1] = product(t, 3)
        own_part[t] = product(t, 0)

    def pass_on(t):
        for way in (0, 1):
            opposite(t, way).wait_recv()
            with_sum = slice(way * HT, (way + 1) * HT)
            without = slice((1 - way) * HT, (2 - way) * HT)
            near_out[t, way, with_sum, :] = (
                near_part[t, way, with_sum, :] + opp_in[t, way].astype(F32)
            ).astype(BF16)
            near_out[t, way, without, :] = near_part[t, way, without, :].astype(BF16)
            neighbour(t, way).start()

    def finish(t):
        neighbour(t, 0).wait_recv()
        neighbour(t, 1).wait_recv()
        total = own_part[t] + near_in[t, 0].astype(F32) + near_in[t, 1].astype(F32)
        mixed_ref[t] = (tok_ref[t].astype(F32) + total).astype(BF16)

    launch(0)
    for o in range(8):
        page(o).start()
        page_id(o).start()
    for zs in range(4):
        for yy in range(4):
            weights(zs, yy).wait()

    def step(t, carry):
        @pl.when(t < NT)
        def _():
            fetch(t)
            compute(t)

        @pl.when((t >= 1) & (t <= NT))
        def _():
            pass_on(t - 1)

        @pl.when(t >= 2)
        def _():
            finish(t - 2)
        return carry

    lax.fori_loop(0, NT + 2, step, 0)

    def drain(t, carry):
        for zs in range(4):
            @pl.when((z < 3) & (zs <= z))
            def _():
                climb(zs, t).wait_send()

            @pl.when((z > 0) & (zs >= z))
            def _():
                descend(zs, t).wait_send()

        for way in (0, 1):
            opposite(t, way).wait_send()
            neighbour(t, way).wait_send()
        return carry

    lax.fori_loop(0, NT, drain, 0)
    for o in range(8):
        page(o).wait_send()
        page_id(o).wait_send()
        copy(pages_ref.at[o], pool_ref.at[o], p_send.at[o], p_recv.at[o], owners[o]).wait_recv()
        copy(ids_ref.at[o], pool_ids_ref.at[o], i_send.at[o], i_recv.at[o], owners[o]).wait_recv()


def output_project(context, tokens, wo_all, pages, ids):
    sem = pltpu.SemaphoreType.DMA
    vm = pl.BlockSpec(memory_space=VMEM)
    return pl.pallas_call(
        output_kernel,
        out_shape=(
            jax.ShapeDtypeStruct((NT, RT, COLS), BF16),
            jax.ShapeDtypeStruct(pages.shape, BF16),
            jax.ShapeDtypeStruct(ids.shape, jnp.int32),
        ),
        in_specs=[vm, vm, pl.BlockSpec(memory_space=pl.ANY), vm, vm],
        out_specs=(vm, vm, vm),
        scratch_shapes=[
            VMEM((4, NT, RT, COLS), BF16),
            VMEM((4, 4, COLS, COLS), BF16),
            VMEM((NT, 2, HT, COLS), BF16),
            VMEM((NT, 2, HT, COLS), BF16),
            VMEM((NT, 2, RT, COLS), BF16),
            VMEM((NT, 2, RT, COLS), BF16),
            VMEM((NT, 2, RT, COLS), F32),
            VMEM((NT, RT, COLS), F32),
            sem((4, 4)), sem((4, NT)), sem((4, NT)), sem((4, NT)), sem((4, NT)),
            sem((NT, 2)), sem((NT, 2)), sem((NT, 2)), sem((NT, 2)),
            sem((8,)), sem((8,)), sem((8,)), sem((8,)),
        ],
        compiler_params=pltpu.CompilerParams(
            collective_id=1, has_side_effects=True, vmem_limit_bytes=48 * 2**20
        ),
        cost_estimate=pl.CostEstimate(
            flops=2 * 512 * 2048 * 2048, bytes_accessed=10 * 2**20, transcendentals=0
        ),
    )(
        context.reshape(NT, RT, COLS), tokens.reshape(NT, RT, COLS),
        wo_all.reshape(4, COLS, 2048), pages, ids,
    )


def rotary(values, positions):
    half = values.shape[-1] // 2
    freq = jnp.exp(
        -jnp.log(500000.0) * (2.0 * jnp.arange(half, dtype=jnp.float32)) / values.shape[-1]
    )
    angle = positions.astype(jnp.float32)[:, None] * freq[None, :]
    cosine = jnp.cos(angle)[:, None, :]
    sine = jnp.sin(angle)[:, None, :]
    first = values[..., :half]
    second = values[..., half:]
    return jnp.concatenate(
        [first * cosine - second * sine, second * cosine + first * sine], axis=-1
    )


def shards(tokens, norm_gain, wq, wk, wv, wo, span_offsets, shared_pages, page_owner, page_ids):
    q_raw, kv_raw, wo_all = gather_project(tokens, norm_gain, wq, wk, wv, wo)
    upper = lax.rem(lax.axis_index("tp"), 2) == 1
    other = lax.ppermute(
        kv_raw.astype(BF16), "tp", [(i, i ^ 1) for i in range(16)]
    ).astype(F32)
    low = jnp.where(upper, other, kv_raw)
    high = jnp.where(upper, kv_raw, other)
    k_raw = jnp.concatenate([low[:, :KCOLS], high[:, :KCOLS]], axis=1)
    values = jnp.concatenate([low[:, KCOLS:], high[:, KCOLS:]], axis=1).astype(BF16)
    positions = span_offsets[0] + jnp.arange(TOK, dtype=jnp.int32)
    query = rotary(q_raw.reshape(TOK, COLS // HD, HD), positions).astype(BF16)
    keys = rotary(k_raw.reshape(TOK, 1, HD), positions).astype(BF16).reshape(TOK, HD)

    live = 1 - shared_pages[0]
    owner = page_owner[0, :, 0]
    onehot = (owner[:, None] == jnp.arange(8, dtype=jnp.int32)[None, :]).astype(
        jnp.int32
    ) * live[:, None]
    rank = jnp.sum(jnp.cumsum(onehot, axis=0) * onehot, axis=1) - 1
    slot = jnp.where(live == 1, owner * 6 + rank, -1)
    select = slot[None, :] == jnp.arange(48, dtype=jnp.int32)[:, None]
    ids = jnp.sum(select.astype(jnp.int32) * (page_ids[0] + 1)[None, :], axis=1) - 1
    ids = jnp.pad(ids.reshape(8, 1, 6), ((0, 0), (0, 0), (0, 122)))
    ids = jnp.broadcast_to(ids, (8, 8, 128))
    row = (slot[:, None] * PAGE + jnp.arange(PAGE, dtype=jnp.int32)[None, :]).reshape(TOK)
    picks = (row[None, :] == jnp.arange(768, dtype=jnp.int32)[:, None]).astype(BF16)
    kv_own = jnp.concatenate(
        [
            jnp.where(upper, keys[:, KCOLS:], keys[:, :KCOLS]),
            jnp.where(upper, values[:, KCOLS:], values[:, :KCOLS]),
        ],
        axis=1,
    )
    pages = jnp.dot(picks, kv_own, preferred_element_type=F32).astype(BF16).reshape(8, 96, 128)

    scores = jnp.einsum("qhd,kd->hqk", query, keys, preferred_element_type=F32) / jnp.sqrt(
        F32(HD)
    )
    causal = jnp.arange(TOK)[:, None] >= jnp.arange(TOK)[None, :]
    scores = jnp.where(causal[None], scores, -1e30)
    top = jnp.max(scores, axis=-1, keepdims=True)
    weights = jnp.exp(scores - top)
    probs = (weights / jnp.sum(weights, axis=-1, keepdims=True)).astype(BF16)
    context = (
        jnp.einsum("hqk,kd->qhd", probs, values, preferred_element_type=F32)
        .astype(BF16)
        .reshape(TOK, COLS)
    )
    mixed, pool, pool_ids = output_project(context, tokens, wo_all, pages, ids)
    return (
        mixed.reshape(TOK, COLS),
        pool.reshape(48, 2048),
        pool_ids[:, 0, :6].reshape(48),
    )


def solution(mesh):
    in_specs = (
        P(("side", "grp"), "tp"),
        P("tp"),
        P("side", "tp"),
        P("side", "tp"),
        P("side", "tp"),
        P("tp", "side"),
        P(("side", "grp")),
        P(("side", "grp"), None),
        P(("side", "grp"), None, None),
        P(("side", "grp"), None),
    )
    out_specs = (P(("side", "grp"), "tp"), P(("side", "grp"), "tp"), P(("side", "grp")))
    return jax.shard_map(shards, mesh=mesh, in_specs=in_specs, out_specs=out_specs, check_vma=False)
```

```python
import jax
import jax.numpy as jnp
from jax import lax
from jax.experimental import pallas as pl
from jax.experimental.pallas import tpu as pltpu
from jax.sharding import PartitionSpec as P

HD = 128
PAGE = 16
EPS = 1e-05
F32 = jnp.float32
BF16 = jnp.bfloat16
MESH = pl.DeviceIdType.MESH
VMEM = pltpu.VMEM

TOK = 512
COLS = 512
KCOLS = 64
HEADS = COLS // HD
NH = 2
RH = TOK // NH
NU = 2 * NH
NK = 2 * NU
LAG = 2
PIECES = 4
PR = 128 // PIECES
WO_Z = 1
WO_X = 3
NT = 4
RT = TOK // NT
HT = RT // 2


def layer_kernel(
    tok_ref, gain_ref, wq_hbm, wk_ref, wv_ref, wo_hbm, cos_ref, sin_ref,
    shared_ref, owner_ref, page_id_ref,
    mixed_ref, pool_ref, pool_ids_ref,
    sq, blocks, own, wq_v, wkv_v, acc_q, acc_kv, got_q, got_kv,
    heads, keys, values, kv_own, kv_other, pages, ids,
    ctx, wo, opp_out, opp_in, near_out, near_in, near_part, own_part,
    w_sem, d_send, d_recv, up_send, up_recv, dn_send, dn_recv,
    yp_send, yp_recv, ym_send, ym_recv, fw_send, fw_recv, x_send, x_recv,
    sy_send, sy_recv, sz_send, sz_recv,
    wz_send, wz_recv, wx_send, wx_recv, wd_send, wd_recv, wl_sem,
    kv_send, kv_recv, cu_send, cu_recv, cd_send, cd_recv,
    a_send, a_recv, b_send, b_recv, p_send, p_recv, i_send, i_recv,
):
    core = lax.axis_index("side")
    grp = lax.axis_index("grp")
    tp = lax.axis_index("tp")
    x = grp // 2
    z_hi = lax.rem(grp, 2)
    z = tp // 4
    y = lax.rem(tp, 4)
    m = jnp.where(core == 0, z, 3 - z)
    home = z // 2 == core
    own_zz = lax.rem(z, 2)

    weights = pltpu.make_async_copy(wq_hbm, wq_v, w_sem)
    weights.start()

    z_near = [{"tp": lax.rem(z + d, 4) * 4 + y} for d in (1, 2, 3)]
    y_near = [{"tp": z * 4 + lax.rem(y + d, 4)} for d in (1, 2, 3)]
    x_near = [{"grp": lax.rem(x + d, 4) * 2 + z_hi} for d in (1, 2, 3)]
    owners = [{"side": 1 - core, "grp": jnp.int32(o)} for o in range(8)]
    sibling = {"side": 1 - core}
    barrier = pltpu.get_barrier_semaphore()
    near = z_near + y_near + x_near + owners
    for one in near:
        pl.semaphore_signal(barrier, inc=1, device_id=one, device_id_type=MESH)

    for h in range(NH):
        own[h] = (
            tok_ref[h * RH:(h + 1) * RH, :].astype(F32) * gain_ref[...].astype(F32)
        ).astype(BF16)

    def remote(src, dst, send, recv, to):
        return pltpu.make_async_remote_copy(
            src_ref=src, dst_ref=dst, send_sem=send, recv_sem=recv,
            device_id=to, device_id_type=MESH)

    def same(ref, send, recv, to):
        return remote(ref, ref, send, recv, to)

    def to_root(h):
        return remote(own.at[h], blocks.at[own_zz, y, core, h], d_send.at[h], d_recv.at[h], sibling)

    pl.semaphore_wait(barrier, len(near))

    @pl.when(jnp.logical_not(home))
    def _():
        for h in range(NH):
            to_root(h).start()

    @pl.when(home)
    def _():
        for h in range(NH):
            blocks[own_zz, y, core, h] = own[h]

    up = {"tp": jnp.where(core == 0, lax.rem(z + 1, 4), lax.rem(z + 3, 4)) * 4 + y}
    down = {"tp": jnp.where(core == 0, lax.rem(z + 3, 4), lax.rem(z + 1, 4)) * 4 + y}
    yp = y_near[0]
    ym = y_near[2]
    y1, y2, y3 = lax.rem(y + 1, 4), lax.rem(y + 2, 4), lax.rem(y + 3, 4)

    def unit(k):
        u = k // 2
        b = 1 - lax.rem(k, 2)
        zz = jnp.where(core == 0, b, 1 - b)
        first = u == 0
        mid = u <= NH
        side = jnp.where(first, core, jnp.where(mid, 1 - core, core))
        h = jnp.where(first, 0, jnp.where(mid, u - 1, u - NH))
        return b, zz, side, h

    def line(k):
        b, zz, side, h = unit(k)
        ref = blocks.at[zz, y, side, h]

        @pl.when((m == b) & (side != core))
        def _():
            same(ref, d_send.at[h], d_recv.at[h], sibling).wait_recv()

        @pl.when(m > b)
        def _():
            same(ref, up_send.at[k], up_recv.at[k], up).wait_recv()

        @pl.when(m < b)
        def _():
            same(ref, dn_send.at[k], dn_recv.at[k], down).wait_recv()

        @pl.when((m >= b) & (m < 3))
        def _():
            same(ref, up_send.at[k], up_recv.at[k], up).start()

        @pl.when((m == 1) & (b == 1))
        def _():
            same(ref, dn_send.at[k], dn_recv.at[k], down).start()

        same(ref, yp_send.at[k], yp_recv.at[k], yp).start()
        same(ref, ym_send.at[k], ym_recv.at[k], ym).start()

    def ring(k):
        b, zz, side, h = unit(k)
        low = blocks.at[zz, y3, side, h]
        high = blocks.at[zz, y1, side, h]
        same(low, yp_send.at[k], yp_recv.at[k], yp).wait_recv()

        @pl.when(lax.rem(h, 2) == 0)
        def _():
            same(low, fw_send.at[k], fw_recv.at[k], yp).start()

        same(high, ym_send.at[k], ym_recv.at[k], ym).wait_recv()

        @pl.when(lax.rem(h, 2) == 1)
        def _():
            same(high, fw_send.at[k], fw_recv.at[k], ym).start()

    def swap_q():
        return remote(acc_q.at[1 - core], got_q, x_send.at[0], x_recv.at[0], sibling)

    def swap_kv():
        return remote(acc_kv.at[1 - core], got_kv, x_send.at[1], x_recv.at[1], sibling)

    def multiply(k):
        b, zz, side, h = unit(k)
        far = blocks.at[zz, y2, side, h]
        same(far, fw_send.at[k], fw_recv.at[k], yp).wait_recv()
        rows = pl.ds(pl.multiple_of(h * RH, RH), RH)
        total_q = acc_q[side, rows, :]
        total_kv = acc_kv[side, rows, :]
        for yy in range(4):
            block = blocks[zz, yy, side, h]
            total_q += jnp.dot(block, wq_v[zz, yy], preferred_element_type=F32)
            total_kv += lax.dot_general(
                block, wkv_v[zz, yy], (((1,), (1,)), ((), ())), preferred_element_type=F32)
        acc_q[side, rows, :] = total_q
        acc_kv[side, rows, :] = total_kv

        @pl.when(k == 2 * NH + 1)
        def _():
            swap_kv().start()
            swap_q().start()

    def sum_y(d):
        return remote(sq.at[0], sq.at[d], sy_send.at[d - 1], sy_recv.at[d - 1], y_near[d - 1])

    def sum_z(d):
        return remote(sq.at[4], sq.at[4 + d], sz_send.at[d - 1], sz_recv.at[d - 1], z_near[d - 1])

    def piece(zs, xx, j):
        return wo.at[zs, xx, pl.ds(pl.multiple_of(j * PR, PR), PR), :]

    def wo_line(zz, j):
        return remote(
            wo_hbm.at[x, pl.ds(pl.multiple_of(j * PR, PR), PR), zz * 2048:(zz + 1) * 2048],
            piece(z, x, j), wz_send.at[zz, j], wz_recv.at[z, j],
            {"tp": (2 * core + zz) * 4 + y})

    def wo_landed(d, j):
        zs = lax.rem(z + d, 4)
        return same(piece(zs, x, j), wz_send.at[0, j], wz_recv.at[zs, j], z_near[d - 1])

    def wo_row(d, e, j):
        return same(piece(lax.rem(z + d, 4), x, j), wx_send.at[d - 1, e - 1, j],
                    wx_recv.at[d - 1, e - 1, j], x_near[e - 1])

    own_cols = pl.ds(pl.multiple_of(own_zz * 2048, 2048), 2048)

    def wo_local():
        return pltpu.make_async_copy(wo_hbm.at[:, :, own_cols], wo.at[z], wl_sem)

    def wo_cross(d):
        here = wo.at[lax.rem(z + d, 4)]
        return remote(wo_hbm.at[:, :, own_cols] if d == 0 else here, here,
                      wd_send.at[d], wd_recv.at[d], sibling)

    def redistribute(k):
        @pl.when((k >= WO_Z) & (k < WO_Z + PIECES))
        def _():
            for zz in range(2):
                @pl.when(2 * core + zz != z)
                def _():
                    wo_line(zz, k - WO_Z).start()

        @pl.when(home & (k == WO_Z))
        def _():
            wo_local().start()
            wo_cross(0).start()

        @pl.when(home & (k >= WO_X) & (k < WO_X + PIECES))
        def _():
            for d in (1, 2, 3):
                wo_landed(d, k - WO_X).wait_recv()
                for e in (1, 2, 3):
                    wo_row(d, e, k - WO_X).start()

    xf = tok_ref[...].astype(F32)
    sq[0] = lax.dot_general(
        jnp.ones((8, COLS), F32), xf * xf, (((1,), (1,)), ((), ())),
        precision=lax.Precision.HIGHEST, preferred_element_type=F32,
    )
    for d in (1, 2, 3):
        sum_y(d).start()
    acc_q[...] = jnp.zeros_like(acc_q)
    acc_kv[...] = jnp.zeros_like(acc_kv)
    for zz in range(2):
        for yy in range(4):
            cols = slice((zz * 4 + yy) * COLS, (zz * 4 + yy + 1) * COLS)
            wkv_v[zz, yy, :KCOLS, :] = wk_ref[:, cols]
            wkv_v[zz, yy, KCOLS:, :] = wv_ref[:, cols]
    weights.wait()

    def step(k, carry):
        @pl.when(k < NK)
        def _():
            line(k)

        @pl.when((k >= LAG) & (k < NK + LAG))
        def _():
            ring(k - LAG)

        @pl.when(k >= LAG + 1)
        def _():
            multiply(k - LAG - 1)

        redistribute(k)

        @pl.when(k == 3)
        def _():
            for d in (1, 2, 3):
                sum_y(d).wait_recv()
            sq[4] = sq[0] + sq[1] + sq[2] + sq[3]
            for d in (1, 2, 3):
                sum_z(d).start()
        return carry

    lax.fori_loop(0, NK + LAG + 1, step, 0)

    for d in (1, 2, 3):
        sum_z(d).wait_recv()
    total = (sq[4] + sq[5] + sq[6] + sq[7]).T[:, :1]
    scale = lax.rsqrt(total * (1.0 / 8192.0) + EPS)
    upper = lax.rem(y, 2) == 1
    swap_kv().wait()
    mine = (acc_kv[core] + got_kv[...]) * scale
    kv_own[...] = mine.astype(BF16)
    trade = remote(kv_own, kv_other, kv_send, kv_recv, {"tp": z * 4 + y + 1 - 2 * lax.rem(y, 2)})
    trade.start()

    @pl.when(home)
    def _():
        for d in (1, 2, 3):
            for j in range(PIECES):
                for e in (1, 2, 3):
                    wo_row(d, e, j).wait_recv()
            wo_cross(d).start()

    cosine = cos_ref[...]
    sine = sin_ref[...]
    swap_q().wait()
    q_all = (acc_q[core] + got_q[...]) * scale
    for h in range(HEADS):
        head = q_all[:, h * HD:(h + 1) * HD]
        heads[h] = (head * cosine + pltpu.roll(head, HD // 2, 1) * sine).astype(BF16)
    trade.wait()
    theirs = kv_other[...].astype(F32)
    low = jnp.where(upper, theirs, mine)
    high = jnp.where(upper, mine, theirs)
    left = lax.broadcasted_iota(jnp.int32, (TOK, HD), 1) < KCOLS
    k_full = jnp.where(left, low, pltpu.roll(high, KCOLS, 1))
    v_full = jnp.where(left, pltpu.roll(low, KCOLS, 1), high)
    k_full = k_full * cosine + pltpu.roll(k_full, HD // 2, 1) * sine
    keys[...] = k_full.astype(BF16)
    values[...] = v_full.astype(BF16)
    kv_own[...] = jnp.where(
        left,
        jnp.where(upper, pltpu.roll(k_full, KCOLS, 1), k_full),
        jnp.where(upper, v_full, pltpu.roll(v_full, KCOLS, 1)),
    ).astype(BF16)

    climb_to = z_near[0]
    descend_to = z_near[2]

    def climb(zs, t):
        return same(ctx.at[zs, t], cu_send.at[zs, t], cu_recv.at[zs, t], climb_to)

    def descend(zs, t):
        return same(ctx.at[zs, t], cd_send.at[zs, t], cd_recv.at[zs, t], descend_to)

    def attend(t):
        query = heads[:, pl.ds(pl.multiple_of(t * RT, RT), RT), :].reshape(HEADS * RT, HD)
        scores = lax.dot_general(
            query, keys[...], (((1,), (1,)), ((), ())), preferred_element_type=F32
        ) / jnp.sqrt(F32(HD))
        shape = (HEADS * RT, TOK)
        place = t * RT + lax.rem(lax.broadcasted_iota(jnp.int32, shape, 0), RT)
        scores = jnp.where(lax.broadcasted_iota(jnp.int32, shape, 1) <= place, scores, -1e30)
        weight = jnp.exp(scores - jnp.max(scores, axis=-1, keepdims=True))
        share = weight / jnp.sum(weight, axis=-1, keepdims=True)
        out = jnp.dot(share.astype(BF16), values[...], preferred_element_type=F32).astype(BF16)
        for h in range(HEADS):
            ctx[z, t, :, h * HD:(h + 1) * HD] = out[h * RT:(h + 1) * RT]

        @pl.when(z < 3)
        def _():
            climb(z, t).start()

        @pl.when(z > 0)
        def _():
            descend(z, t).start()

    def page(o):
        return remote(pages.at[o], pool_ref.at[grp], p_send.at[o], p_recv.at[grp], owners[o])

    def page_id(o):
        return remote(ids.at[o], pool_ids_ref.at[grp], i_send.at[o], i_recv.at[grp], owners[o])

    def hand_over():
        live = 1.0 - shared_ref[...].astype(F32)
        owner = owner_ref[...]
        named = lax.broadcasted_iota(jnp.int32, (8, 32), 0) == owner
        onehot = jnp.where(named, live, 0.0)
        upto = (
            lax.broadcasted_iota(jnp.int32, (32, 32), 0)
            <= lax.broadcasted_iota(jnp.int32, (32, 32), 1)
        ).astype(F32)
        count = jnp.dot(onehot, upto, preferred_element_type=F32)
        rank = jnp.sum(count * onehot, axis=0, keepdims=True) - 1.0
        slot = jnp.where(live > 0.5, owner.astype(F32) * 6.0 + rank, -1.0)
        spread = (
            lax.broadcasted_iota(jnp.int32, (32, TOK), 0)
            == lax.broadcasted_iota(jnp.int32, (32, TOK), 1) // PAGE
        ).astype(F32)
        slots = jnp.dot(jnp.broadcast_to(slot, (8, 32)), spread, preferred_element_type=F32)
        inside = lax.rem(lax.broadcasted_iota(jnp.int32, (1, TOK), 1), PAGE)
        row = slots[:1] * float(PAGE) + inside.astype(F32)
        for o in range(8):
            at = (lax.broadcasted_iota(jnp.int32, (96, TOK), 0) + o * 96).astype(F32)
            picks = jnp.where(at == row, 1.0, 0.0).astype(BF16)
            pages[o] = jnp.dot(picks, kv_own[...], preferred_element_type=F32).astype(BF16)
            rank_of = lax.broadcasted_iota(jnp.int32, (8, 32), 0)
            chosen = (slot == (rank_of + o * 6).astype(F32)) & (rank_of < 6)
            found = jnp.sum(jnp.where(chosen, page_id_ref[...] + 1, 0), axis=1, keepdims=True) - 1
            ids[o] = jnp.broadcast_to(found, (8, 128))
            page(o).start()
            page_id(o).start()

    def opposite(t, way):
        return remote(opp_out.at[t, way], opp_in.at[t, way], a_send.at[t, way],
                      a_recv.at[t, way], (yp, ym)[way])

    def neighbour(t, way):
        return remote(near_out.at[t, way], near_in.at[t, way], b_send.at[t, way],
                      b_recv.at[t, way], (yp, ym)[way])

    def fetch(t):
        for d in (1, 2, 3):
            @pl.when(z - d >= 0)
            def _():
                climb(z - d, t).wait_recv()

                @pl.when(z < 3)
                def _():
                    climb(z - d, t).start()

            @pl.when(z + d <= 3)
            def _():
                descend(z + d, t).wait_recv()

                @pl.when(z > 0)
                def _():
                    descend(z + d, t).start()

    def product(t, r):
        cols = pl.ds(pl.multiple_of(lax.rem(y + r, 4) * COLS, COLS), COLS)
        total = None
        for zs in range(4):
            part = jnp.dot(
                ctx[zs, t], wo[zs, :, :, cols].reshape(COLS, COLS), preferred_element_type=F32)
            total = part if total is None else total + part
        return total

    def compute(t):
        far = product(t, 2).astype(BF16)
        for way in (0, 1):
            opp_out[t, way] = far[way * HT:(way + 1) * HT]
            opposite(t, way).start()
        near_part[t, 0] = product(t, 1)
        near_part[t, 1] = product(t, 3)
        own_part[t] = product(t, 0)

    def pass_on(t):
        for way in (0, 1):
            opposite(t, way).wait_recv()
            with_sum = slice(way * HT, (way + 1) * HT)
            without = slice((1 - way) * HT, (2 - way) * HT)
            near_out[t, way, with_sum, :] = (
                near_part[t, way, with_sum, :] + opp_in[t, way].astype(F32)
            ).astype(BF16)
            near_out[t, way, without, :] = near_part[t, way, without, :].astype(BF16)
            neighbour(t, way).start()

    def finish(t):
        neighbour(t, 0).wait_recv()
        neighbour(t, 1).wait_recv()
        total = own_part[t] + near_in[t, 0].astype(F32) + near_in[t, 1].astype(F32)
        rows = pl.ds(pl.multiple_of(t * RT, RT), RT)
        mixed_ref[rows, :] = (tok_ref[rows, :].astype(F32) + total).astype(BF16)

    attend(0)
    attend(1)
    hand_over()

    @pl.when(home)
    def _():
        wo_local().wait()

    @pl.when(jnp.logical_not(home))
    def _():
        for d in range(4):
            wo_cross(d).wait_recv()

    def out_step(t, carry):
        @pl.when(t < NT)
        def _():
            @pl.when((t >= 1) & (t < NT - 1))
            def _():
                attend(t + 1)
            fetch(t)
            compute(t)

        @pl.when((t >= 1) & (t <= NT))
        def _():
            pass_on(t - 1)

        @pl.when(t >= 2)
        def _():
            finish(t - 2)
        return carry

    lax.fori_loop(0, NT + 2, out_step, 0)

    def drain(k, carry):
        b, zz, side, h = unit(k)
        ref = blocks.at[zz, y, side, h]

        @pl.when((m >= b) & (m < 3))
        def _():
            same(ref, up_send.at[k], up_recv.at[k], up).wait_send()

        @pl.when((m == 1) & (b == 1))
        def _():
            same(ref, dn_send.at[k], dn_recv.at[k], down).wait_send()

        same(ref, yp_send.at[k], yp_recv.at[k], yp).wait_send()
        same(ref, ym_send.at[k], ym_recv.at[k], ym).wait_send()
        same(ref, fw_send.at[k], fw_recv.at[k], yp).wait_send()
        return carry

    lax.fori_loop(0, NK, drain, 0)

    def drain_out(t, carry):
        for zs in range(4):
            @pl.when((z < 3) & (zs <= z))
            def _():
                climb(zs, t).wait_send()

            @pl.when((z > 0) & (zs >= z))
            def _():
                descend(zs, t).wait_send()

        for way in (0, 1):
            opposite(t, way).wait_send()
            neighbour(t, way).wait_send()
        return carry

    lax.fori_loop(0, NT, drain_out, 0)

    @pl.when(jnp.logical_not(home))
    def _():
        for h in range(NH):
            to_root(h).wait_send()

    for d in (1, 2, 3):
        sum_y(d).wait_send()
        sum_z(d).wait_send()

    def drain_wo(j, carry):
        for zz in range(2):
            @pl.when(2 * core + zz != z)
            def _():
                wo_line(zz, j).wait_send()

        @pl.when(home)
        def _():
            for d in (1, 2, 3):
                for e in (1, 2, 3):
                    wo_row(d, e, j).wait_send()
        return carry

    lax.fori_loop(0, PIECES, drain_wo, 0)

    @pl.when(home)
    def _():
        for d in range(4):
            wo_cross(d).wait_send()

    for o in range(8):
        page(o).wait_send()
        page_id(o).wait_send()
        remote(pages.at[o], pool_ref.at[o], p_send.at[o], p_recv.at[o], owners[o]).wait_recv()
        remote(ids.at[o], pool_ids_ref.at[o], i_send.at[o], i_recv.at[o], owners[o]).wait_recv()


def layer(tokens, gain, wq, wk, wv, wo, cosine, sine, shared, owner, page_ids):
    sem = pltpu.SemaphoreType.DMA
    vm = pl.BlockSpec(memory_space=VMEM)
    hbm = pl.BlockSpec(memory_space=pl.ANY)
    return pl.pallas_call(
        layer_kernel,
        out_shape=(
            jax.ShapeDtypeStruct((TOK, COLS), BF16),
            jax.ShapeDtypeStruct((8, 96, 128), BF16),
            jax.ShapeDtypeStruct((8, 8, 128), jnp.int32),
        ),
        in_specs=[vm, vm, hbm, vm, vm, hbm, vm, vm, vm, vm, vm],
        out_specs=(vm, vm, vm),
        scratch_shapes=[
            VMEM((8, 8, TOK), F32),
            VMEM((2, 4, 2, NH, RH, COLS), BF16),
            VMEM((NH, RH, COLS), BF16),
            VMEM((2, 4, COLS, COLS), BF16),
            VMEM((2, 4, 2 * KCOLS, COLS), BF16),
            VMEM((2, TOK, COLS), F32),
            VMEM((2, TOK, 2 * KCOLS), F32),
            VMEM((TOK, COLS), F32),
            VMEM((TOK, 2 * KCOLS), F32),
            VMEM((HEADS, TOK, HD), BF16),
            VMEM((TOK, HD), BF16),
            VMEM((TOK, HD), BF16),
            VMEM((TOK, HD), BF16),
            VMEM((TOK, HD), BF16),
            VMEM((8, 96, 128), BF16),
            VMEM((8, 8, 128), jnp.int32),
            VMEM((4, NT, RT, COLS), BF16),
            VMEM((4, 4, 128, 2048), BF16),
            VMEM((NT, 2, HT, COLS), BF16),
            VMEM((NT, 2, HT, COLS), BF16),
            VMEM((NT, 2, RT, COLS), BF16),
            VMEM((NT, 2, RT, COLS), BF16),
            VMEM((NT, 2, RT, COLS), F32),
            VMEM((NT, RT, COLS), F32),
            sem, sem((NH,)), sem((NH,)),
        ] + [sem((NK,))] * 10 + [
            sem((2,)), sem((2,)), sem((3,)), sem((3,)), sem((3,)), sem((3,)),
            sem((2, PIECES)), sem((4, PIECES)), sem((3, 3, PIECES)), sem((3, 3, PIECES)),
            sem((4,)), sem((4,)), sem, sem, sem,
            sem((4, NT)), sem((4, NT)), sem((4, NT)), sem((4, NT)),
            sem((NT, 2)), sem((NT, 2)), sem((NT, 2)), sem((NT, 2)),
            sem((8,)), sem((8,)), sem((8,)), sem((8,)),
        ],
        compiler_params=pltpu.CompilerParams(
            collective_id=0, has_side_effects=True, vmem_limit_bytes=56 * 2**20
        ),
    )(
        tokens, gain.reshape(1, COLS), wq.reshape(2, 4, COLS, COLS), wk.T, wv.T,
        wo.reshape(4, 128, 4096), cosine, sine, shared, owner, page_ids,
    )


def shards(tokens, norm_gain, wq, wk, wv, wo, span_offsets, shared_pages, page_owner, page_ids):
    half = HD // 2
    freq = jnp.exp(-jnp.log(500000.0) * (2.0 * jnp.arange(half, dtype=F32)) / HD)
    positions = span_offsets[0] + jnp.arange(TOK, dtype=jnp.int32)
    angle = positions.astype(F32)[:, None] * jnp.concatenate([freq, freq])[None, :]
    sign = jnp.where(jnp.arange(HD) < half, -1.0, 1.0).astype(F32)
    cosine = jnp.cos(angle)
    sine = jnp.sin(angle) * sign[None, :]
    mixed, pool, pool_ids = layer(
        tokens, norm_gain, wq, wk, wv, wo, cosine, sine,
        shared_pages, page_owner.reshape(1, 32), page_ids,
    )
    return mixed, pool.reshape(48, 2048), pool_ids[:, :6, 0].reshape(48)


def solution(mesh):
    in_specs = (
        P(("side", "grp"), "tp"),
        P("tp"),
        P("side", "tp"),
        P("side", "tp"),
        P("side", "tp"),
        P("tp", "side"),
        P(("side", "grp")),
        P(("side", "grp"), None),
        P(("side", "grp"), None, None),
        P(("side", "grp"), None),
    )
    out_specs = (P(("side", "grp"), "tp"), P(("side", "grp"), "tp"), P(("side", "grp")))
    return jax.shard_map(shards, mesh=mesh, in_specs=in_specs, out_specs=out_specs, check_vma=False)
```

```python
import jax
import jax.numpy as jnp
from jax import lax
from jax.experimental import pallas as pl
from jax.experimental.pallas import tpu as pltpu
from jax.sharding import PartitionSpec as P

HD = 128
PAGE = 16
EPS = 1e-05
F32 = jnp.float32
BF16 = jnp.bfloat16
MESH = pl.DeviceIdType.MESH
VMEM = pltpu.VMEM

TOK = 512
COLS = 512
KCOLS = 64
HEADS = COLS // HD
NH = 4
RH = TOK // NH
NU = 2 * NH
NK = 2 * NU
LAG = 2
AHEAD = 3
PIECES = 4
PR = 128 // PIECES
WO_Z = 3
WO_X = 7
WO_D = 12
NT = 4
RT = TOK // NT
HT = RT // 2
TRADE = 4
ATTEND = 7
FETCH = (9, 10, 11)
COMPUTE = 12
PASS_ON = 14
FINISH = 16
STEPS = LAG + 1 + 4 * (NT - 1) + FINISH + 1


def layer_kernel(
    tok_ref, gain_ref, wq_hbm, wk_ref, wv_ref, wo_hbm, cos_ref, sin_ref,
    shared_ref, owner_ref, page_id_ref,
    mixed_ref, pool_ref, pool_ids_ref,
    sq, blocks, own, wq_v, wkv_v, acc_q, acc_kv, got_q, got_kv,
    heads, keys, values, kv_own, kv_other, kv_page, scale, pages, ids,
    ctx, wo, opp_out, opp_in, near_out, near_in, near_part, own_part,
    w_sem, d_send, d_recv, up_send, up_recv, dn_send, dn_recv,
    yp_send, yp_recv, ym_send, ym_recv, fw_send, fw_recv, x_send, x_recv,
    sy_send, sy_recv, sz_send, sz_recv,
    wz_send, wz_recv, wx_send, wx_recv, wd_send, wd_recv, wl_sem,
    kv_send, kv_recv, cu_send, cu_recv, cd_send, cd_recv,
    a_send, a_recv, b_send, b_recv, p_send, p_recv, i_send, i_recv,
):
    core = lax.axis_index("side")
    grp = lax.axis_index("grp")
    tp = lax.axis_index("tp")
    x = grp // 2
    z_hi = lax.rem(grp, 2)
    z = tp // 4
    y = lax.rem(tp, 4)
    m = jnp.where(core == 0, z, 3 - z)
    home = z // 2 == core
    own_zz = lax.rem(z, 2)

    weights = pltpu.make_async_copy(wq_hbm, wq_v, w_sem)
    weights.start()

    z_near = [{"tp": lax.rem(z + d, 4) * 4 + y} for d in (1, 2, 3)]
    z_all = z_hi * 4 + z
    z_ring = []
    for far in (1, 2, 6, 7):
        ahead = lax.rem(z_all + far, 8)
        z_ring.append({"grp": x * 2 + ahead // 4, "tp": lax.rem(ahead, 4) * 4 + y})
    y_near = [{"tp": z * 4 + lax.rem(y + d, 4)} for d in (1, 2, 3)]
    x_near = [{"grp": lax.rem(x + d, 4) * 2 + z_hi} for d in (1, 2, 3)]
    owners = [{"side": 1 - core, "grp": jnp.int32(o)} for o in range(8)]
    sibling = {"side": 1 - core}
    barrier = pltpu.get_barrier_semaphore()
    near = z_near + z_ring + y_near + x_near + owners
    for one in near:
        pl.semaphore_signal(barrier, inc=1, device_id=one, device_id_type=MESH)

    for h in range(NH):
        own[h] = (
            tok_ref[h * RH:(h + 1) * RH, :].astype(F32) * gain_ref[...].astype(F32)
        ).astype(BF16)

    def remote(src, dst, send, recv, to):
        return pltpu.make_async_remote_copy(
            src_ref=src, dst_ref=dst, send_sem=send, recv_sem=recv,
            device_id=to, device_id_type=MESH)

    def same(ref, send, recv, to):
        return remote(ref, ref, send, recv, to)

    def to_root(h):
        return remote(own.at[h], blocks.at[own_zz, y, core, h], d_send.at[h], d_recv.at[h], sibling)

    pl.semaphore_wait(barrier, len(near))

    @pl.when(jnp.logical_not(home))
    def _():
        for h in range(NH):
            to_root(h).start()

    @pl.when(home)
    def _():
        for h in range(NH):
            blocks[own_zz, y, core, h] = own[h]

    up = {"tp": jnp.where(core == 0, lax.rem(z + 1, 4), lax.rem(z + 3, 4)) * 4 + y}
    down = {"tp": jnp.where(core == 0, lax.rem(z + 3, 4), lax.rem(z + 1, 4)) * 4 + y}
    yp = y_near[0]
    ym = y_near[2]
    y1, y2, y3 = lax.rem(y + 1, 4), lax.rem(y + 2, 4), lax.rem(y + 3, 4)

    def unit(k):
        b = 1 - lax.rem(k, 4) // 2
        zz = jnp.where(core == 0, b, 1 - b)
        side = jnp.where(lax.rem(k, 2) == 0, core, 1 - core)
        h = k // 4
        return b, zz, side, h

    def from_root(k, carry):
        b, zz, side, h = unit(k)
        ref = blocks.at[zz, y, side, h]

        @pl.when(m == b)
        def _():
            @pl.when(side != core)
            def _():
                same(ref, d_send.at[h], d_recv.at[h], sibling).wait_recv()

            same(ref, up_send.at[k], up_recv.at[k], up).start()

            @pl.when(m == 1)
            def _():
                same(ref, dn_send.at[k], dn_recv.at[k], down).start()
        return carry

    def line(k):
        b, zz, side, h = unit(k)
        ref = blocks.at[zz, y, side, h]

        @pl.when(m > b)
        def _():
            same(ref, up_send.at[k], up_recv.at[k], up).wait_recv()

            @pl.when(m < 3)
            def _():
                same(ref, up_send.at[k], up_recv.at[k], up).start()

        @pl.when(m < b)
        def _():
            same(ref, dn_send.at[k], dn_recv.at[k], down).wait_recv()

    def spread(k):
        b, zz, side, h = unit(k)
        ref = blocks.at[zz, y, side, h]
        same(ref, yp_send.at[k], yp_recv.at[k], yp).start()
        same(ref, ym_send.at[k], ym_recv.at[k], ym).start()

    def ring(k):
        b, zz, side, h = unit(k)
        low = blocks.at[zz, y3, side, h]
        high = blocks.at[zz, y1, side, h]
        same(low, yp_send.at[k], yp_recv.at[k], yp).wait_recv()

        @pl.when(lax.rem(k, 2) == 0)
        def _():
            same(low, fw_send.at[k], fw_recv.at[k], yp).start()

        same(high, ym_send.at[k], ym_recv.at[k], ym).wait_recv()

        @pl.when(lax.rem(k, 2) == 1)
        def _():
            same(high, fw_send.at[k], fw_recv.at[k], ym).start()

    def chunk(t):
        return pl.ds(pl.multiple_of(t * RT, RT), RT)

    def swap_q(t):
        return remote(acc_q.at[1 - core, chunk(t), :], got_q.at[chunk(t), :],
                      x_send.at[0, t], x_recv.at[0, t], sibling)

    def swap_kv(t):
        return remote(acc_kv.at[1 - core, chunk(t), :], got_kv.at[chunk(t), :],
                      x_send.at[1, t], x_recv.at[1, t], sibling)

    def multiply(k):
        b, zz, side, h = unit(k)
        far = blocks.at[zz, y2, side, h]
        same(far, fw_send.at[k], fw_recv.at[k], yp).wait_recv()
        rows = pl.ds(pl.multiple_of(h * RH, RH), RH)
        total_q = acc_q[side, rows, :]
        total_kv = acc_kv[side, rows, :]
        for yy in range(4):
            block = blocks[zz, yy, side, h]
            total_q += jnp.dot(block, wq_v[zz, yy], preferred_element_type=F32)
            total_kv += lax.dot_general(
                block, wkv_v[zz, yy], (((1,), (1,)), ((), ())), preferred_element_type=F32)
        acc_q[side, rows, :] = total_q
        acc_kv[side, rows, :] = total_kv

        @pl.when(lax.rem(k, 4) == 3)
        def _():
            swap_kv(h).start()
            swap_q(h).start()

    def sum_y(d):
        return remote(sq.at[0], sq.at[d], sy_send.at[d - 1], sy_recv.at[d - 1], y_near[d - 1])

    def sum_z(d):
        return remote(sq.at[4], sq.at[4 + d], sz_send.at[d - 1], sz_recv.at[d - 1], z_near[d - 1])

    def piece(zs, xx, j):
        return wo.at[zs, xx, pl.ds(pl.multiple_of(j * PR, PR), PR), :]

    def wo_line(d, j):
        ahead = lax.rem(z_all + (1, jnp.where(lax.rem(j, 2) == 0, 2, 6), 7)[d - 1], 8)
        z_to = lax.rem(z + d, 4)
        col = pl.ds(pl.multiple_of(lax.rem(z_to, 2) * 2048, 2048), 2048)
        return remote(
            wo_hbm.at[x, pl.ds(pl.multiple_of(j * PR, PR), PR), col],
            piece(z, x, j), wz_send.at[d - 1, j], wz_recv.at[d - 1, j],
            {"grp": x * 2 + ahead // 4, "tp": lax.rem(ahead, 4) * 4 + y})

    def wo_sends(d):
        return lax.rem(z + d, 4) // 2 == core

    def wo_landed(d, j):
        zs = lax.rem(z + d, 4)
        return same(piece(zs, x, j), wz_send.at[3 - d, j], wz_recv.at[3 - d, j], z_near[d - 1])

    def wo_row(d, e, j):
        return same(piece(lax.rem(z + d, 4), x, j), wx_send.at[d - 1, e - 1, j],
                    wx_recv.at[d - 1, e - 1, j], x_near[e - 1])

    own_cols = pl.ds(pl.multiple_of(own_zz * 2048, 2048), 2048)

    def wo_local():
        return pltpu.make_async_copy(wo_hbm.at[:, :, own_cols], wo.at[z], wl_sem)

    def wo_cross(d):
        here = wo.at[lax.rem(z + d, 4)]
        return remote(wo_hbm.at[:, :, own_cols] if d == 0 else here, here,
                      wd_send.at[d], wd_recv.at[d], sibling)

    def redistribute(k):
        @pl.when((k >= WO_Z) & (k < WO_Z + PIECES))
        def _():
            for d in (1, 2, 3):
                @pl.when(wo_sends(d))
                def _():
                    wo_line(d, k - WO_Z).start()

        @pl.when(home & (k == WO_Z))
        def _():
            wo_local().start()
            wo_cross(0).start()

        @pl.when(home & (k >= WO_X) & (k < WO_X + PIECES))
        def _():
            for d in (1, 2, 3):
                wo_landed(d, k - WO_X).wait_recv()
                for e in (1, 2, 3):
                    wo_row(d, e, k - WO_X).start()

        for d in (1, 2, 3):
            @pl.when(home & (k == WO_D + d - 1))
            def _():
                for j in range(PIECES):
                    for e in (1, 2, 3):
                        wo_row(d, e, j).wait_recv()
                wo_cross(d).start()

    xf = tok_ref[...].astype(F32)
    sq[0] = lax.dot_general(
        jnp.ones((8, COLS), F32), xf * xf, (((1,), (1,)), ((), ())),
        precision=lax.Precision.HIGHEST, preferred_element_type=F32,
    )
    for d in (1, 2, 3):
        sum_y(d).start()
    lax.fori_loop(0, NK, from_root, 0)
    line(0)
    acc_q[...] = jnp.zeros_like(acc_q)
    acc_kv[...] = jnp.zeros_like(acc_kv)
    for zz in range(2):
        for yy in range(4):
            cols = slice((zz * 4 + yy) * COLS, (zz * 4 + yy + 1) * COLS)
            wkv_v[zz, yy, :KCOLS, :] = wk_ref[:, cols]
            wkv_v[zz, yy, KCOLS:, :] = wv_ref[:, cols]
    weights.wait()

    keys[...] = jnp.zeros_like(keys)
    values[...] = jnp.zeros_like(values)
    upper = lax.rem(y, 2) == 1
    left = lax.broadcasted_iota(jnp.int32, (RT, HD), 1) < KCOLS

    def trade(t):
        return remote(kv_own.at[chunk(t), :], kv_other.at[chunk(t), :], kv_send.at[t],
                      kv_recv.at[t], {"tp": z * 4 + y + 1 - 2 * lax.rem(y, 2)})

    def start_trade(t):
        @pl.when(t == 0)
        def _():
            for d in (1, 2, 3):
                sum_z(d).wait_recv()
            total = (sq[4] + sq[5] + sq[6] + sq[7]).T[:, :1]
            scale[...] = jnp.broadcast_to(lax.rsqrt(total * (1.0 / 8192.0) + EPS), (TOK, HD))
        swap_kv(t).wait()
        swap_q(t).wait()
        rows = chunk(t)
        mine = (acc_kv[core, rows, :] + got_kv[rows, :]) * scale[rows, :]
        got_kv[rows, :] = mine
        kv_own[rows, :] = mine.astype(BF16)
        trade(t).start()
        cosine = cos_ref[rows, :]
        sine = sin_ref[rows, :]
        for h in range(HEADS):
            cols = slice(h * HD, (h + 1) * HD)
            head = (acc_q[core, rows, cols] + got_q[rows, cols]) * scale[rows, :]
            heads[h, rows, :] = (head * cosine + pltpu.roll(head, HD // 2, 1) * sine).astype(BF16)

    def end_trade(t):
        trade(t).wait()
        rows = chunk(t)
        mine = got_kv[rows, :]
        theirs = kv_other[rows, :].astype(F32)
        low = jnp.where(upper, theirs, mine)
        high = jnp.where(upper, mine, theirs)
        k_full = jnp.where(left, low, pltpu.roll(high, KCOLS, 1))
        v_full = jnp.where(left, pltpu.roll(low, KCOLS, 1), high)
        k_full = k_full * cos_ref[rows, :] + pltpu.roll(k_full, HD // 2, 1) * sin_ref[rows, :]
        keys[rows, :] = k_full.astype(BF16)
        values[rows, :] = v_full.astype(BF16)
        kv_page[rows, :] = jnp.where(
            left,
            jnp.where(upper, pltpu.roll(k_full, KCOLS, 1), k_full),
            jnp.where(upper, v_full, pltpu.roll(v_full, KCOLS, 1)),
        ).astype(BF16)

    climb_to = z_near[0]
    descend_to = z_near[2]

    def climb(zs, t):
        return same(ctx.at[zs, t], cu_send.at[zs, t], cu_recv.at[zs, t], climb_to)

    def descend(zs, t):
        return same(ctx.at[zs, t], cd_send.at[zs, t], cd_recv.at[zs, t], descend_to)

    def attend(t):
        query = heads[:, pl.ds(pl.multiple_of(t * RT, RT), RT), :].reshape(HEADS * RT, HD)
        scores = lax.dot_general(
            query, keys[...], (((1,), (1,)), ((), ())), preferred_element_type=F32
        ) / jnp.sqrt(F32(HD))
        shape = (HEADS * RT, TOK)
        place = t * RT + lax.rem(lax.broadcasted_iota(jnp.int32, shape, 0), RT)
        scores = jnp.where(lax.broadcasted_iota(jnp.int32, shape, 1) <= place, scores, -1e30)
        weight = jnp.exp(scores - jnp.max(scores, axis=-1, keepdims=True))
        share = weight / jnp.sum(weight, axis=-1, keepdims=True)
        out = jnp.dot(share.astype(BF16), values[...], preferred_element_type=F32).astype(BF16)
        for h in range(HEADS):
            ctx[z, t, :, h * HD:(h + 1) * HD] = out[h * RT:(h + 1) * RT]

        @pl.when(z < 3)
        def _():
            climb(z, t).start()

        @pl.when(z > 0)
        def _():
            descend(z, t).start()

    def page(o):
        return remote(pages.at[o], pool_ref.at[grp], p_send.at[o], p_recv.at[grp], owners[o])

    def page_id(o):
        return remote(ids.at[o], pool_ids_ref.at[grp], i_send.at[o], i_recv.at[grp], owners[o])

    def hand_over():
        live = 1.0 - shared_ref[...].astype(F32)
        owner = owner_ref[...]
        named = lax.broadcasted_iota(jnp.int32, (8, 32), 0) == owner
        onehot = jnp.where(named, live, 0.0)
        upto = (
            lax.broadcasted_iota(jnp.int32, (32, 32), 0)
            <= lax.broadcasted_iota(jnp.int32, (32, 32), 1)
        ).astype(F32)
        count = jnp.dot(onehot, upto, preferred_element_type=F32)
        rank = jnp.sum(count * onehot, axis=0, keepdims=True) - 1.0
        slot = jnp.where(live > 0.5, owner.astype(F32) * 6.0 + rank, -1.0)
        spread = (
            lax.broadcasted_iota(jnp.int32, (32, TOK), 0)
            == lax.broadcasted_iota(jnp.int32, (32, TOK), 1) // PAGE
        ).astype(F32)
        slots = jnp.dot(jnp.broadcast_to(slot, (8, 32)), spread, preferred_element_type=F32)
        inside = lax.rem(lax.broadcasted_iota(jnp.int32, (1, TOK), 1), PAGE)
        row = slots[:1] * float(PAGE) + inside.astype(F32)
        for o in range(8):
            at = (lax.broadcasted_iota(jnp.int32, (96, TOK), 0) + o * 96).astype(F32)
            picks = jnp.where(at == row, 1.0, 0.0).astype(BF16)
            pages[o] = jnp.dot(picks, kv_page[...], preferred_element_type=F32).astype(BF16)
            rank_of = lax.broadcasted_iota(jnp.int32, (8, 32), 0)
            chosen = (slot == (rank_of + o * 6).astype(F32)) & (rank_of < 6)
            found = jnp.sum(jnp.where(chosen, page_id_ref[...] + 1, 0), axis=1, keepdims=True) - 1
            ids[o] = jnp.broadcast_to(found, (8, 128))
            page(o).start()
            page_id(o).start()

    def opposite(t, way):
        return remote(opp_out.at[t, way], opp_in.at[t, way], a_send.at[t, way],
                      a_recv.at[t, way], (yp, ym)[way])

    def neighbour(t, way):
        return remote(near_out.at[t, way], near_in.at[t, way], b_send.at[t, way],
                      b_recv.at[t, way], (yp, ym)[way])

    def fetch(t, d):
        if True:
            @pl.when(z - d >= 0)
            def _():
                climb(z - d, t).wait_recv()

                @pl.when(z < 3)
                def _():
                    climb(z - d, t).start()

            @pl.when(z + d <= 3)
            def _():
                descend(z + d, t).wait_recv()

                @pl.when(z > 0)
                def _():
                    descend(z + d, t).start()

    def product(t, r):
        cols = pl.ds(pl.multiple_of(lax.rem(y + r, 4) * COLS, COLS), COLS)
        total = None
        for zs in range(4):
            part = jnp.dot(
                ctx[zs, t], wo[zs, :, :, cols].reshape(COLS, COLS), preferred_element_type=F32)
            total = part if total is None else total + part
        return total

    def compute(t):
        far = product(t, 2).astype(BF16)
        for way in (0, 1):
            opp_out[t, way] = far[way * HT:(way + 1) * HT]
            opposite(t, way).start()
        near_part[t, 0] = product(t, 1)
        near_part[t, 1] = product(t, 3)
        own_part[t] = product(t, 0)

    def pass_on(t):
        for way in (0, 1):
            opposite(t, way).wait_recv()
            with_sum = slice(way * HT, (way + 1) * HT)
            without = slice((1 - way) * HT, (2 - way) * HT)
            near_out[t, way, with_sum, :] = (
                near_part[t, way, with_sum, :] + opp_in[t, way].astype(F32)
            ).astype(BF16)
            near_out[t, way, without, :] = near_part[t, way, without, :].astype(BF16)
            neighbour(t, way).start()

    def finish(t):
        neighbour(t, 0).wait_recv()
        neighbour(t, 1).wait_recv()
        total = own_part[t] + near_in[t, 0].astype(F32) + near_in[t, 1].astype(F32)
        rows = pl.ds(pl.multiple_of(t * RT, RT), RT)
        mixed_ref[rows, :] = (tok_ref[rows, :].astype(F32) + total).astype(BF16)

    def wo_ready():
        @pl.when(home)
        def _():
            wo_local().wait()

        @pl.when(jnp.logical_not(home))
        def _():
            for d in range(4):
                wo_cross(d).wait_recv()

    def step(k, carry):
        @pl.when(k < NK)
        def _():
            spread(k)

        @pl.when(k < NK - AHEAD)
        def _():
            line(k + AHEAD)

        @pl.when((k >= LAG) & (k < NK + LAG))
        def _():
            ring(k - LAG)

        @pl.when((k >= LAG + 1) & (k < NK + LAG + 1))
        def _():
            multiply(k - LAG - 1)

        redistribute(k)

        @pl.when(k == 3)
        def _():
            for d in (1, 2, 3):
                sum_y(d).wait_recv()
            sq[4] = sq[0] + sq[1] + sq[2] + sq[3]
            for d in (1, 2, 3):
                sum_z(d).start()

        def at(offset):
            since = k - (LAG + 1) - offset
            return (since >= 0) & (since <= 4 * (NT - 1)) & (lax.rem(since, 4) == 0), since // 4

        turn, t1 = at(TRADE)

        @pl.when(turn)
        def _():
            start_trade(t1)

        turn, t2 = at(ATTEND)

        @pl.when(turn)
        def _():
            end_trade(t2)
            attend(t2)

        for d in (1, 2, 3):
            turn, t3 = at(FETCH[d - 1])

            @pl.when(turn)
            def _():
                fetch(t3, d)

        @pl.when(k == LAG + 1 + COMPUTE)
        def _():
            wo_ready()

        turn, t4 = at(COMPUTE)

        @pl.when(turn)
        def _():
            compute(t4)

        @pl.when(k == LAG + 2 + 4 * (NT - 1) + ATTEND)
        def _():
            hand_over()

        turn, t5 = at(PASS_ON)

        @pl.when(turn)
        def _():
            pass_on(t5)

        turn, t6 = at(FINISH)

        @pl.when(turn)
        def _():
            finish(t6)
        return carry

    for k in range(1, AHEAD):
        line(k)
    lax.fori_loop(0, STEPS, step, 0)

    def drain(k, carry):
        b, zz, side, h = unit(k)
        ref = blocks.at[zz, y, side, h]

        @pl.when((m >= b) & (m < 3))
        def _():
            same(ref, up_send.at[k], up_recv.at[k], up).wait_send()

        @pl.when((m == 1) & (b == 1))
        def _():
            same(ref, dn_send.at[k], dn_recv.at[k], down).wait_send()

        same(ref, yp_send.at[k], yp_recv.at[k], yp).wait_send()
        same(ref, ym_send.at[k], ym_recv.at[k], ym).wait_send()
        same(ref, fw_send.at[k], fw_recv.at[k], yp).wait_send()
        return carry

    lax.fori_loop(0, NK, drain, 0)

    def drain_out(t, carry):
        for zs in range(4):
            @pl.when((z < 3) & (zs <= z))
            def _():
                climb(zs, t).wait_send()

            @pl.when((z > 0) & (zs >= z))
            def _():
                descend(zs, t).wait_send()

        for way in (0, 1):
            opposite(t, way).wait_send()
            neighbour(t, way).wait_send()
        return carry

    lax.fori_loop(0, NT, drain_out, 0)

    @pl.when(jnp.logical_not(home))
    def _():
        for h in range(NH):
            to_root(h).wait_send()

    for d in (1, 2, 3):
        sum_y(d).wait_send()
        sum_z(d).wait_send()

    def drain_wo(j, carry):
        for d in (1, 2, 3):
            @pl.when(wo_sends(d))
            def _():
                wo_line(d, j).wait_send()

        @pl.when(home)
        def _():
            for d in (1, 2, 3):
                for e in (1, 2, 3):
                    wo_row(d, e, j).wait_send()
        return carry

    lax.fori_loop(0, PIECES, drain_wo, 0)

    @pl.when(home)
    def _():
        for d in range(4):
            wo_cross(d).wait_send()

    for o in range(8):
        page(o).wait_send()
        page_id(o).wait_send()
        remote(pages.at[o], pool_ref.at[o], p_send.at[o], p_recv.at[o], owners[o]).wait_recv()
        remote(ids.at[o], pool_ids_ref.at[o], i_send.at[o], i_recv.at[o], owners[o]).wait_recv()


def layer(tokens, gain, wq, wk, wv, wo, cosine, sine, shared, owner, page_ids):
    sem = pltpu.SemaphoreType.DMA
    vm = pl.BlockSpec(memory_space=VMEM)
    hbm = pl.BlockSpec(memory_space=pl.ANY)
    return pl.pallas_call(
        layer_kernel,
        out_shape=(
            jax.ShapeDtypeStruct((TOK, COLS), BF16),
            jax.ShapeDtypeStruct((8, 96, 128), BF16),
            jax.ShapeDtypeStruct((8, 8, 128), jnp.int32),
        ),
        in_specs=[vm, vm, hbm, vm, vm, hbm, vm, vm, vm, vm, vm],
        out_specs=(vm, vm, vm),
        scratch_shapes=[
            VMEM((8, 8, TOK), F32),
            VMEM((2, 4, 2, NH, RH, COLS), BF16),
            VMEM((NH, RH, COLS), BF16),
            VMEM((2, 4, COLS, COLS), BF16),
            VMEM((2, 4, 2 * KCOLS, COLS), BF16),
            VMEM((2, TOK, COLS), F32),
            VMEM((2, TOK, 2 * KCOLS), F32),
            VMEM((TOK, COLS), F32),
            VMEM((TOK, 2 * KCOLS), F32),
            VMEM((HEADS, TOK, HD), BF16),
            VMEM((TOK, HD), BF16),
            VMEM((TOK, HD), BF16),
            VMEM((TOK, HD), BF16),
            VMEM((TOK, HD), BF16),
            VMEM((TOK, HD), BF16),
            VMEM((TOK, HD), F32),
            VMEM((8, 96, 128), BF16),
            VMEM((8, 8, 128), jnp.int32),
            VMEM((4, NT, RT, COLS), BF16),
            VMEM((4, 4, 128, 2048), BF16),
            VMEM((NT, 2, HT, COLS), BF16),
            VMEM((NT, 2, HT, COLS), BF16),
            VMEM((NT, 2, RT, COLS), BF16),
            VMEM((NT, 2, RT, COLS), BF16),
            VMEM((NT, 2, RT, COLS), F32),
            VMEM((NT, RT, COLS), F32),
            sem, sem((NH,)), sem((NH,)),
        ] + [sem((NK,))] * 10 + [
            sem((2, NT)), sem((2, NT)), sem((3,)), sem((3,)), sem((3,)), sem((3,)),
            sem((3, PIECES)), sem((3, PIECES)), sem((3, 3, PIECES)), sem((3, 3, PIECES)),
            sem((4,)), sem((4,)), sem, sem((NT,)), sem((NT,)),
            sem((4, NT)), sem((4, NT)), sem((4, NT)), sem((4, NT)),
            sem((NT, 2)), sem((NT, 2)), sem((NT, 2)), sem((NT, 2)),
            sem((8,)), sem((8,)), sem((8,)), sem((8,)),
        ],
        compiler_params=pltpu.CompilerParams(
            collective_id=0, has_side_effects=True, vmem_limit_bytes=56 * 2**20
        ),
    )(
        tokens, gain.reshape(1, COLS), wq.reshape(2, 4, COLS, COLS), wk.T, wv.T,
        wo.reshape(4, 128, 4096), cosine, sine, shared, owner, page_ids,
    )


def shards(tokens, norm_gain, wq, wk, wv, wo, span_offsets, shared_pages, page_owner, page_ids):
    half = HD // 2
    freq = jnp.exp(-jnp.log(500000.0) * (2.0 * jnp.arange(half, dtype=F32)) / HD)
    positions = span_offsets[0] + jnp.arange(TOK, dtype=jnp.int32)
    angle = positions.astype(F32)[:, None] * jnp.concatenate([freq, freq])[None, :]
    sign = jnp.where(jnp.arange(HD) < half, -1.0, 1.0).astype(F32)
    cosine = jnp.cos(angle)
    sine = jnp.sin(angle) * sign[None, :]
    mixed, pool, pool_ids = layer(
        tokens, norm_gain, wq, wk, wv, wo, cosine, sine,
        shared_pages, page_owner.reshape(1, 32), page_ids,
    )
    return mixed, pool.reshape(48, 2048), pool_ids[:, :6, 0].reshape(48)


def solution(mesh):
    in_specs = (
        P(("side", "grp"), "tp"),
        P("tp"),
        P("side", "tp"),
        P("side", "tp"),
        P("side", "tp"),
        P("tp", "side"),
        P(("side", "grp")),
        P(("side", "grp"), None),
        P(("side", "grp"), None, None),
        P(("side", "grp"), None),
    )
    out_specs = (P(("side", "grp"), "tp"), P(("side", "grp"), "tp"), P(("side", "grp")))
    return jax.shard_map(shards, mesh=mesh, in_specs=in_specs, out_specs=out_specs, check_vma=False)
```

```python
import jax
import jax.numpy as jnp
from jax import lax
from jax.experimental import pallas as pl
from jax.experimental.pallas import tpu as pltpu
from jax.sharding import PartitionSpec as P

HD = 128
PAGE = 16
EPS = 1e-05
F32 = jnp.float32
BF16 = jnp.bfloat16
MESH = pl.DeviceIdType.MESH
VMEM = pltpu.VMEM

TOK = 512
COLS = 512
KCOLS = 64
HEADS = COLS // HD
NH = 4
RH = TOK // NH
NU = 2 * NH
NK = 2 * NU
LAG = 2
AHEAD = 3
PIECES = 4
PR = 128 // PIECES
WO_Z = 3
WO_X = 7
WO_D = 12
NT = 4
RT = TOK // NT
HT = RT // 2
TRADE = 4
ATTEND = 7
FETCH = (10, 12, 14)
COMPUTE = 15
PASS_ON = 17
FINISH = 19
STEPS = LAG + 1 + 4 * (NT - 1) + FINISH + 1


def layer_kernel(
    tok_ref, gain_ref, wq_hbm, wk_ref, wv_ref, wo_hbm, cos_ref, sin_ref,
    shared_ref, owner_ref, page_id_ref,
    mixed_ref, pool_ref, pool_ids_ref,
    sq, blocks, own, wq_v, wkv_v, acc_q, acc_kv, got_q, got_kv,
    heads, keys, values, kv_own, kv_other, kv_page, scale, pages, ids, pool_in, ids_in,
    ctx, wo, opp_out, opp_in, near_out, near_in, near_part, own_part,
    w_sem, d_send, d_recv, up_send, up_recv, dn_send, dn_recv,
    yp_send, yp_recv, ym_send, ym_recv, fw_send, fw_recv, x_send, x_recv,
    sy_send, sy_recv, sz_send, sz_recv,
    wz_send, wz_recv, wx_send, wx_recv, wd_send, wd_recv, wl_sem,
    kv_send, kv_recv, cu_send, cu_recv, cd_send, cd_recv,
    a_send, a_recv, b_send, b_recv, p_send, p_recv, i_send, i_recv,
):
    core = lax.axis_index("side")
    grp = lax.axis_index("grp")
    tp = lax.axis_index("tp")
    x = grp // 2
    z_hi = lax.rem(grp, 2)
    z = tp // 4
    y = lax.rem(tp, 4)
    m = jnp.where(core == 0, z, 3 - z)
    home = z // 2 == core
    own_zz = lax.rem(z, 2)

    weights = pltpu.make_async_copy(wq_hbm, wq_v, w_sem)
    weights.start()

    z_near = [{"tp": lax.rem(z + d, 4) * 4 + y} for d in (1, 2, 3)]
    z_all = z_hi * 4 + z
    z_ring = []
    for far in (1, 2, 6, 7):
        ahead = lax.rem(z_all + far, 8)
        z_ring.append({"grp": x * 2 + ahead // 4, "tp": lax.rem(ahead, 4) * 4 + y})
    y_near = [{"tp": z * 4 + lax.rem(y + d, 4)} for d in (1, 2, 3)]
    x_near = [{"grp": lax.rem(x + d, 4) * 2 + z_hi} for d in (1, 2, 3)]
    owners = [{"side": 1 - core, "grp": jnp.int32(o)} for o in range(8)]
    sibling = {"side": 1 - core}
    barrier = pltpu.get_barrier_semaphore()
    near = z_near + z_ring + y_near + x_near + owners
    for one in near:
        pl.semaphore_signal(barrier, inc=1, device_id=one, device_id_type=MESH)

    for h in range(NH):
        own[h] = (
            tok_ref[h * RH:(h + 1) * RH, :].astype(F32) * gain_ref[...].astype(F32).reshape(1, COLS)
        ).astype(BF16)

    def remote(src, dst, send, recv, to):
        return pltpu.make_async_remote_copy(
            src_ref=src, dst_ref=dst, send_sem=send, recv_sem=recv,
            device_id=to, device_id_type=MESH)

    def same(ref, send, recv, to):
        return remote(ref, ref, send, recv, to)

    def to_root(h):
        return remote(own.at[h], blocks.at[own_zz, y, core, h], d_send.at[h], d_recv.at[h], sibling)

    pl.semaphore_wait(barrier, len(near))

    @pl.when(jnp.logical_not(home))
    def _():
        for h in range(NH):
            to_root(h).start()

    @pl.when(home)
    def _():
        for h in range(NH):
            blocks[own_zz, y, core, h] = own[h]

    up = {"tp": jnp.where(core == 0, lax.rem(z + 1, 4), lax.rem(z + 3, 4)) * 4 + y}
    down = {"tp": jnp.where(core == 0, lax.rem(z + 3, 4), lax.rem(z + 1, 4)) * 4 + y}
    yp = y_near[0]
    ym = y_near[2]
    y1, y2, y3 = lax.rem(y + 1, 4), lax.rem(y + 2, 4), lax.rem(y + 3, 4)

    def unit(k):
        b = 1 - lax.rem(k, 4) // 2
        zz = jnp.where(core == 0, b, 1 - b)
        side = jnp.where(lax.rem(k, 2) == 0, core, 1 - core)
        h = k // 4
        return b, zz, side, h

    def from_root(k, carry):
        b, zz, side, h = unit(k)
        ref = blocks.at[zz, y, side, h]

        @pl.when(m == b)
        def _():
            @pl.when(side != core)
            def _():
                same(ref, d_send.at[h], d_recv.at[h], sibling).wait_recv()

            same(ref, up_send.at[k], up_recv.at[k], up).start()

            @pl.when(m == 1)
            def _():
                same(ref, dn_send.at[k], dn_recv.at[k], down).start()
        return carry

    def line(k):
        b, zz, side, h = unit(k)
        ref = blocks.at[zz, y, side, h]

        @pl.when(m > b)
        def _():
            same(ref, up_send.at[k], up_recv.at[k], up).wait_recv()

            @pl.when(m < 3)
            def _():
                same(ref, up_send.at[k], up_recv.at[k], up).start()

        @pl.when(m < b)
        def _():
            same(ref, dn_send.at[k], dn_recv.at[k], down).wait_recv()

    def spread(k):
        b, zz, side, h = unit(k)
        ref = blocks.at[zz, y, side, h]
        same(ref, yp_send.at[k], yp_recv.at[k], yp).start()
        same(ref, ym_send.at[k], ym_recv.at[k], ym).start()

    def ring(k):
        b, zz, side, h = unit(k)
        low = blocks.at[zz, y3, side, h]
        high = blocks.at[zz, y1, side, h]
        same(low, yp_send.at[k], yp_recv.at[k], yp).wait_recv()

        @pl.when(lax.rem(k, 2) == 0)
        def _():
            same(low, fw_send.at[k], fw_recv.at[k], yp).start()

        same(high, ym_send.at[k], ym_recv.at[k], ym).wait_recv()

        @pl.when(lax.rem(k, 2) == 1)
        def _():
            same(high, fw_send.at[k], fw_recv.at[k], ym).start()

    def chunk(t):
        return pl.ds(pl.multiple_of(t * RT, RT), RT)

    def swap_q(t):
        return remote(acc_q.at[1 - core, chunk(t), :], got_q.at[chunk(t), :],
                      x_send.at[0, t], x_recv.at[0, t], sibling)

    def swap_kv(t):
        return remote(acc_kv.at[1 - core, chunk(t), :], got_kv.at[chunk(t), :],
                      x_send.at[1, t], x_recv.at[1, t], sibling)

    def multiply(k):
        b, zz, side, h = unit(k)
        far = blocks.at[zz, y2, side, h]
        same(far, fw_send.at[k], fw_recv.at[k], yp).wait_recv()
        rows = pl.ds(pl.multiple_of(h * RH, RH), RH)
        total_q = acc_q[side, rows, :]
        total_kv = acc_kv[side, rows, :]
        for yy in range(4):
            block = blocks[zz, yy, side, h]
            total_q += jnp.dot(block, wq_v[zz, yy], preferred_element_type=F32)
            total_kv += lax.dot_general(
                block, wkv_v[zz, yy], (((1,), (1,)), ((), ())), preferred_element_type=F32)
        acc_q[side, rows, :] = total_q
        acc_kv[side, rows, :] = total_kv

        @pl.when(lax.rem(k, 4) == 3)
        def _():
            swap_kv(h).start()
            swap_q(h).start()

    def sum_y(d):
        return remote(sq.at[0], sq.at[d], sy_send.at[d - 1], sy_recv.at[d - 1], y_near[d - 1])

    def sum_z(d):
        return remote(sq.at[4], sq.at[4 + d], sz_send.at[d - 1], sz_recv.at[d - 1], z_near[d - 1])

    def piece(zs, xx, j):
        return wo.at[zs, xx, pl.ds(pl.multiple_of(j * PR, PR), PR), :]

    def wo_line(d, j):
        ahead = lax.rem(z_all + (1, jnp.where(lax.rem(j, 2) == 0, 2, 6), 7)[d - 1], 8)
        z_to = lax.rem(z + d, 4)
        col = pl.ds(pl.multiple_of(lax.rem(z_to, 2) * 2048, 2048), 2048)
        return remote(
            wo_hbm.at[x, pl.ds(pl.multiple_of(j * PR, PR), PR), col],
            piece(z, x, j), wz_send.at[d - 1, j], wz_recv.at[d - 1, j],
            {"grp": x * 2 + ahead // 4, "tp": lax.rem(ahead, 4) * 4 + y})

    def wo_sends(d):
        return lax.rem(z + d, 4) // 2 == core

    def wo_landed(d, j):
        zs = lax.rem(z + d, 4)
        return same(piece(zs, x, j), wz_send.at[3 - d, j], wz_recv.at[3 - d, j], z_near[d - 1])

    def wo_row(d, e, j):
        return same(piece(lax.rem(z + d, 4), x, j), wx_send.at[d - 1, e - 1, j],
                    wx_recv.at[d - 1, e - 1, j], x_near[e - 1])

    own_cols = pl.ds(pl.multiple_of(own_zz * 2048, 2048), 2048)

    def wo_local():
        return pltpu.make_async_copy(wo_hbm.at[:, :, own_cols], wo.at[z], wl_sem)

    def wo_cross(d):
        here = wo.at[lax.rem(z + d, 4)]
        return remote(wo_hbm.at[:, :, own_cols] if d == 0 else here, here,
                      wd_send.at[d], wd_recv.at[d], sibling)

    def redistribute(k):
        @pl.when((k >= WO_Z) & (k < WO_Z + PIECES))
        def _():
            for d in (1, 2, 3):
                @pl.when(wo_sends(d))
                def _():
                    wo_line(d, k - WO_Z).start()

        @pl.when(home & (k == WO_Z))
        def _():
            wo_local().start()
            wo_cross(0).start()

        @pl.when(home & (k >= WO_X) & (k < WO_X + PIECES))
        def _():
            for d in (1, 2, 3):
                wo_landed(d, k - WO_X).wait_recv()
                for e in (1, 2, 3):
                    wo_row(d, e, k - WO_X).start()

        for d in (1, 2, 3):
            @pl.when(home & (k == WO_D + d - 1))
            def _():
                for j in range(PIECES):
                    for e in (1, 2, 3):
                        wo_row(d, e, j).wait_recv()
                wo_cross(d).start()

    xf = tok_ref[...].astype(F32)
    sq[0] = lax.dot_general(
        jnp.ones((8, COLS), F32), xf * xf, (((1,), (1,)), ((), ())),
        precision=lax.Precision.HIGHEST, preferred_element_type=F32,
    )
    for d in (1, 2, 3):
        sum_y(d).start()
    lax.fori_loop(0, NK, from_root, 0)
    line(0)
    acc_q[...] = jnp.zeros_like(acc_q)
    acc_kv[...] = jnp.zeros_like(acc_kv)
    for zz in range(2):
        for yy in range(4):
            cols = slice((zz * 4 + yy) * COLS, (zz * 4 + yy + 1) * COLS)
            wkv_v[zz, yy, :KCOLS, :] = wk_ref[:, cols]
            wkv_v[zz, yy, KCOLS:, :] = wv_ref[:, cols]
    weights.wait()

    keys[...] = jnp.zeros_like(keys)
    values[...] = jnp.zeros_like(values)
    upper = lax.rem(y, 2) == 1
    left = lax.broadcasted_iota(jnp.int32, (RT, HD), 1) < KCOLS

    def trade(t):
        return remote(kv_own.at[chunk(t), :], kv_other.at[chunk(t), :], kv_send.at[t],
                      kv_recv.at[t], {"tp": z * 4 + y + 1 - 2 * lax.rem(y, 2)})

    def start_trade(t):
        @pl.when(t == 0)
        def _():
            for d in (1, 2, 3):
                sum_z(d).wait_recv()
            total = (sq[4] + sq[5] + sq[6] + sq[7]).T[:, :1]
            scale[...] = jnp.broadcast_to(lax.rsqrt(total * (1.0 / 8192.0) + EPS), (TOK, HD))
        swap_kv(t).wait()
        swap_q(t).wait()
        rows = chunk(t)
        mine = (acc_kv[core, rows, :] + got_kv[rows, :]) * scale[rows, :]
        got_kv[rows, :] = mine
        kv_own[rows, :] = mine.astype(BF16)
        trade(t).start()
        cosine = cos_ref[rows, :]
        sine = sin_ref[rows, :]
        for h in range(HEADS):
            cols = slice(h * HD, (h + 1) * HD)
            head = (acc_q[core, rows, cols] + got_q[rows, cols]) * scale[rows, :]
            heads[h, rows, :] = (head * cosine + pltpu.roll(head, HD // 2, 1) * sine).astype(BF16)

    def end_trade(t):
        trade(t).wait()
        rows = chunk(t)
        mine = got_kv[rows, :]
        theirs = kv_other[rows, :].astype(F32)
        low = jnp.where(upper, theirs, mine)
        high = jnp.where(upper, mine, theirs)
        k_full = jnp.where(left, low, pltpu.roll(high, KCOLS, 1))
        v_full = jnp.where(left, pltpu.roll(low, KCOLS, 1), high)
        k_full = k_full * cos_ref[rows, :] + pltpu.roll(k_full, HD // 2, 1) * sin_ref[rows, :]
        keys[rows, :] = k_full.astype(BF16)
        values[rows, :] = v_full.astype(BF16)
        kv_page[rows, :] = jnp.where(
            left,
            jnp.where(upper, pltpu.roll(k_full, KCOLS, 1), k_full),
            jnp.where(upper, v_full, pltpu.roll(v_full, KCOLS, 1)),
        ).astype(BF16)

    climb_to = z_near[0]
    descend_to = z_near[2]

    def climb(zs, t):
        return same(ctx.at[zs, t], cu_send.at[zs, t], cu_recv.at[zs, t], climb_to)

    def descend(zs, t):
        return same(ctx.at[zs, t], cd_send.at[zs, t], cd_recv.at[zs, t], descend_to)

    def attend(t):
        query = heads[:, pl.ds(pl.multiple_of(t * RT, RT), RT), :].reshape(HEADS * RT, HD)
        scores = lax.dot_general(
            query, keys[...], (((1,), (1,)), ((), ())), preferred_element_type=F32
        ) / jnp.sqrt(F32(HD))
        shape = (HEADS * RT, TOK)
        place = t * RT + lax.rem(lax.broadcasted_iota(jnp.int32, shape, 0), RT)
        scores = jnp.where(lax.broadcasted_iota(jnp.int32, shape, 1) <= place, scores, -1e30)
        weight = jnp.exp(scores - jnp.max(scores, axis=-1, keepdims=True))
        share = weight / jnp.sum(weight, axis=-1, keepdims=True)
        out = jnp.dot(share.astype(BF16), values[...], preferred_element_type=F32).astype(BF16)
        for h in range(HEADS):
            ctx[z, t, :, h * HD:(h + 1) * HD] = out[h * RT:(h + 1) * RT]

        @pl.when(z < 3)
        def _():
            climb(z, t).start()

        @pl.when(z > 0)
        def _():
            descend(z, t).start()

    def page(o):
        return remote(pages.at[o], pool_in.at[grp], p_send.at[o], p_recv.at[grp], owners[o])

    def page_id(o):
        return remote(ids.at[o], ids_in.at[grp], i_send.at[o], i_recv.at[grp], owners[o])

    def hand_over():
        live = 1.0 - shared_ref[...].astype(F32)
        owner = owner_ref[...]
        named = lax.broadcasted_iota(jnp.int32, (8, 32), 0) == owner
        onehot = jnp.where(named, live, 0.0)
        upto = (
            lax.broadcasted_iota(jnp.int32, (32, 32), 0)
            <= lax.broadcasted_iota(jnp.int32, (32, 32), 1)
        ).astype(F32)
        count = jnp.dot(onehot, upto, preferred_element_type=F32)
        rank = jnp.sum(count * onehot, axis=0, keepdims=True) - 1.0
        slot = jnp.where(live > 0.5, owner.astype(F32) * 6.0 + rank, -1.0)
        spread = (
            lax.broadcasted_iota(jnp.int32, (32, TOK), 0)
            == lax.broadcasted_iota(jnp.int32, (32, TOK), 1) // PAGE
        ).astype(F32)
        slots = jnp.dot(jnp.broadcast_to(slot, (8, 32)), spread, preferred_element_type=F32)
        inside = lax.rem(lax.broadcasted_iota(jnp.int32, (1, TOK), 1), PAGE)
        row = slots[:1] * float(PAGE) + inside.astype(F32)
        for o in range(8):
            at = (lax.broadcasted_iota(jnp.int32, (96, TOK), 0) + o * 96).astype(F32)
            picks = jnp.where(at == row, 1.0, 0.0).astype(BF16)
            pages[o] = jnp.dot(picks, kv_page[...], preferred_element_type=F32).astype(BF16)
            rank_of = lax.broadcasted_iota(jnp.int32, (8, 32), 0)
            chosen = (slot == (rank_of + o * 6).astype(F32)) & (rank_of < 6)
            found = jnp.sum(jnp.where(chosen, page_id_ref[...] + 1, 0), axis=1, keepdims=True) - 1
            ids[o] = jnp.broadcast_to(found, (8, 128))
            page(o).start()
            page_id(o).start()

    def take_over():
        for o in range(8):
            remote(pages.at[o], pool_in.at[o], p_send.at[o], p_recv.at[o], owners[o]).wait_recv()
            remote(ids.at[o], ids_in.at[o], i_send.at[o], i_recv.at[o], owners[o]).wait_recv()
        token = lax.broadcasted_iota(jnp.int32, (PAGE, 48, 768), 0)
        slot = lax.broadcasted_iota(jnp.int32, (PAGE, 48, 768), 1)
        source = lax.broadcasted_iota(jnp.int32, (PAGE, 48, 768), 2)
        picks = jnp.where(source == slot * PAGE + token, 1.0, 0.0).astype(BF16)
        moved = jnp.dot(
            picks.reshape(768, 768), pool_in[...].reshape(768, 128),
            preferred_element_type=F32).astype(BF16)
        for i in range(PAGE):
            pool_ref[:, i * 128:(i + 1) * 128] = moved[i * 48:(i + 1) * 48]
        line_ids = jnp.zeros((1, 128), jnp.int32)
        lane = lax.broadcasted_iota(jnp.int32, (1, 128), 1)
        for o in range(8):
            for r in range(6):
                line_ids = jnp.where(lane == o * 6 + r, ids_in[o, r:r + 1, :], line_ids)
        pool_ids_ref[...] = line_ids

    def opposite(t, way):
        return remote(opp_out.at[t, way], opp_in.at[t, way], a_send.at[t, way],
                      a_recv.at[t, way], (yp, ym)[way])

    def neighbour(t, way):
        return remote(near_out.at[t, way], near_in.at[t, way], b_send.at[t, way],
                      b_recv.at[t, way], (yp, ym)[way])

    def fetch(t, d):
        if True:
            @pl.when(z - d >= 0)
            def _():
                climb(z - d, t).wait_recv()

                @pl.when(z < 3)
                def _():
                    climb(z - d, t).start()

            @pl.when(z + d <= 3)
            def _():
                descend(z + d, t).wait_recv()

                @pl.when(z > 0)
                def _():
                    descend(z + d, t).start()

    def product(t, r):
        cols = pl.ds(pl.multiple_of(lax.rem(y + r, 4) * COLS, COLS), COLS)
        total = None
        for zs in range(4):
            part = jnp.dot(
                ctx[zs, t], wo[zs, :, :, cols].reshape(COLS, COLS), preferred_element_type=F32)
            total = part if total is None else total + part
        return total

    def compute(t):
        far = product(t, 2).astype(BF16)
        for way in (0, 1):
            opp_out[t, way] = far[way * HT:(way + 1) * HT]
            opposite(t, way).start()
        near_part[t, 0] = product(t, 1)
        near_part[t, 1] = product(t, 3)
        own_part[t] = product(t, 0)

    def pass_on(t):
        for way in (0, 1):
            opposite(t, way).wait_recv()
            with_sum = slice(way * HT, (way + 1) * HT)
            without = slice((1 - way) * HT, (2 - way) * HT)
            near_out[t, way, with_sum, :] = (
                near_part[t, way, with_sum, :] + opp_in[t, way].astype(F32)
            ).astype(BF16)
            near_out[t, way, without, :] = near_part[t, way, without, :].astype(BF16)
            neighbour(t, way).start()

    def finish(t):
        neighbour(t, 0).wait_recv()
        neighbour(t, 1).wait_recv()
        total = own_part[t] + near_in[t, 0].astype(F32) + near_in[t, 1].astype(F32)
        rows = pl.ds(pl.multiple_of(t * RT, RT), RT)
        mixed_ref[rows, :] = (tok_ref[rows, :].astype(F32) + total).astype(BF16)

    def wo_ready():
        @pl.when(home)
        def _():
            wo_local().wait()

        @pl.when(jnp.logical_not(home))
        def _():
            for d in range(4):
                wo_cross(d).wait_recv()

    def step(k, carry):
        @pl.when(k < NK)
        def _():
            spread(k)

        @pl.when(k < NK - AHEAD)
        def _():
            line(k + AHEAD)

        @pl.when((k >= LAG) & (k < NK + LAG))
        def _():
            ring(k - LAG)

        @pl.when((k >= LAG + 1) & (k < NK + LAG + 1))
        def _():
            multiply(k - LAG - 1)

        redistribute(k)

        @pl.when(k == 3)
        def _():
            for d in (1, 2, 3):
                sum_y(d).wait_recv()
            sq[4] = sq[0] + sq[1] + sq[2] + sq[3]
            for d in (1, 2, 3):
                sum_z(d).start()

        def at(offset):
            since = k - (LAG + 1) - offset
            return (since >= 0) & (since <= 4 * (NT - 1)) & (lax.rem(since, 4) == 0), since // 4

        turn, t1 = at(TRADE)

        @pl.when(turn)
        def _():
            start_trade(t1)

        turn, t2 = at(ATTEND)

        @pl.when(turn)
        def _():
            end_trade(t2)
            attend(t2)

        for d in (1, 2, 3):
            turn, t3 = at(FETCH[d - 1])

            @pl.when(turn)
            def _():
                fetch(t3, d)

        @pl.when(k == LAG + 1 + COMPUTE)
        def _():
            wo_ready()

        turn, t4 = at(COMPUTE)

        @pl.when(turn)
        def _():
            compute(t4)

        @pl.when(k == LAG + 2 + 4 * (NT - 1) + ATTEND)
        def _():
            hand_over()

        turn, t5 = at(PASS_ON)

        @pl.when(turn)
        def _():
            pass_on(t5)

        @pl.when(k == LAG + 2 + 4 * (NT - 1) + PASS_ON)
        def _():
            take_over()

        turn, t6 = at(FINISH)

        @pl.when(turn)
        def _():
            finish(t6)
        return carry

    for k in range(1, AHEAD):
        line(k)
    lax.fori_loop(0, STEPS, step, 0)

    def drain(k, carry):
        b, zz, side, h = unit(k)
        ref = blocks.at[zz, y, side, h]

        @pl.when((m >= b) & (m < 3))
        def _():
            same(ref, up_send.at[k], up_recv.at[k], up).wait_send()

        @pl.when((m == 1) & (b == 1))
        def _():
            same(ref, dn_send.at[k], dn_recv.at[k], down).wait_send()

        same(ref, yp_send.at[k], yp_recv.at[k], yp).wait_send()
        same(ref, ym_send.at[k], ym_recv.at[k], ym).wait_send()
        same(ref, fw_send.at[k], fw_recv.at[k], yp).wait_send()
        return carry

    lax.fori_loop(0, NK, drain, 0)

    def drain_out(t, carry):
        for zs in range(4):
            @pl.when((z < 3) & (zs <= z))
            def _():
                climb(zs, t).wait_send()

            @pl.when((z > 0) & (zs >= z))
            def _():
                descend(zs, t).wait_send()

        for way in (0, 1):
            opposite(t, way).wait_send()
            neighbour(t, way).wait_send()
        return carry

    lax.fori_loop(0, NT, drain_out, 0)

    @pl.when(jnp.logical_not(home))
    def _():
        for h in range(NH):
            to_root(h).wait_send()

    for d in (1, 2, 3):
        sum_y(d).wait_send()
        sum_z(d).wait_send()

    def drain_wo(j, carry):
        for d in (1, 2, 3):
            @pl.when(wo_sends(d))
            def _():
                wo_line(d, j).wait_send()

        @pl.when(home)
        def _():
            for d in (1, 2, 3):
                for e in (1, 2, 3):
                    wo_row(d, e, j).wait_send()
        return carry

    lax.fori_loop(0, PIECES, drain_wo, 0)

    @pl.when(home)
    def _():
        for d in range(4):
            wo_cross(d).wait_send()

    for o in range(8):
        page(o).wait_send()
        page_id(o).wait_send()


def layer(tokens, gain, wq, wk, wv, wo, cosine, sine, shared, owner, page_ids):
    sem = pltpu.SemaphoreType.DMA
    vm = pl.BlockSpec(memory_space=VMEM)
    hbm = pl.BlockSpec(memory_space=pl.ANY)
    return pl.pallas_call(
        layer_kernel,
        out_shape=(
            jax.ShapeDtypeStruct((TOK, COLS), BF16),
            jax.ShapeDtypeStruct((48, 2048), BF16),
            jax.ShapeDtypeStruct((1, 128), jnp.int32),
        ),
        in_specs=[vm, vm, hbm, vm, vm, hbm, vm, vm, vm, vm, vm],
        out_specs=(vm, vm, vm),
        scratch_shapes=[
            VMEM((8, 8, TOK), F32),
            VMEM((2, 4, 2, NH, RH, COLS), BF16),
            VMEM((NH, RH, COLS), BF16),
            VMEM((2, 4, COLS, COLS), BF16),
            VMEM((2, 4, 2 * KCOLS, COLS), BF16),
            VMEM((2, TOK, COLS), F32),
            VMEM((2, TOK, 2 * KCOLS), F32),
            VMEM((TOK, COLS), F32),
            VMEM((TOK, 2 * KCOLS), F32),
            VMEM((HEADS, TOK, HD), BF16),
            VMEM((TOK, HD), BF16),
            VMEM((TOK, HD), BF16),
            VMEM((TOK, HD), BF16),
            VMEM((TOK, HD), BF16),
            VMEM((TOK, HD), BF16),
            VMEM((TOK, HD), F32),
            VMEM((8, 96, 128), BF16),
            VMEM((8, 8, 128), jnp.int32),
            VMEM((8, 96, 128), BF16),
            VMEM((8, 8, 128), jnp.int32),
            VMEM((4, NT, RT, COLS), BF16),
            VMEM((4, 4, 128, 2048), BF16),
            VMEM((NT, 2, HT, COLS), BF16),
            VMEM((NT, 2, HT, COLS), BF16),
            VMEM((NT, 2, RT, COLS), BF16),
            VMEM((NT, 2, RT, COLS), BF16),
            VMEM((NT, 2, RT, COLS), F32),
            VMEM((NT, RT, COLS), F32),
            sem, sem((NH,)), sem((NH,)),
        ] + [sem((NK,))] * 10 + [
            sem((2, NT)), sem((2, NT)), sem((3,)), sem((3,)), sem((3,)), sem((3,)),
            sem((3, PIECES)), sem((3, PIECES)), sem((3, 3, PIECES)), sem((3, 3, PIECES)),
            sem((4,)), sem((4,)), sem, sem((NT,)), sem((NT,)),
            sem((4, NT)), sem((4, NT)), sem((4, NT)), sem((4, NT)),
            sem((NT, 2)), sem((NT, 2)), sem((NT, 2)), sem((NT, 2)),
            sem((8,)), sem((8,)), sem((8,)), sem((8,)),
        ],
        compiler_params=pltpu.CompilerParams(
            collective_id=0, has_side_effects=True, vmem_limit_bytes=56 * 2**20
        ),
    )(
        tokens, gain, wq.reshape(2, 4, COLS, COLS), wk.T, wv.T,
        wo.reshape(4, 128, 4096), cosine, sine, shared, owner, page_ids,
    )


def shards(tokens, norm_gain, wq, wk, wv, wo, span_offsets, shared_pages, page_owner, page_ids):
    half = HD // 2
    freq = jnp.exp(-jnp.log(500000.0) * (2.0 * jnp.arange(half, dtype=F32)) / HD)
    positions = span_offsets[0] + jnp.arange(TOK, dtype=jnp.int32)
    angle = positions.astype(F32)[:, None] * jnp.concatenate([freq, freq])[None, :]
    sign = jnp.where(jnp.arange(HD) < half, -1.0, 1.0).astype(F32)
    cosine = jnp.cos(angle)
    sine = jnp.sin(angle) * sign[None, :]
    mixed, pool, pool_ids = layer(
        tokens, norm_gain, wq, wk, wv, wo, cosine, sine,
        shared_pages, page_owner.reshape(1, 32), page_ids,
    )
    return mixed, pool, pool_ids[0, :48]


def solution(mesh):
    in_specs = (
        P(("side", "grp"), "tp"),
        P("tp"),
        P("side", "tp"),
        P("side", "tp"),
        P("side", "tp"),
        P("tp", "side"),
        P(("side", "grp")),
        P(("side", "grp"), None),
        P(("side", "grp"), None, None),
        P(("side", "grp"), None),
    )
    out_specs = (P(("side", "grp"), "tp"), P(("side", "grp"), "tp"), P(("side", "grp")))
    return jax.shard_map(shards, mesh=mesh, in_specs=in_specs, out_specs=out_specs, check_vma=False)
```

```python
import jax
import jax.numpy as jnp
from jax import lax
from jax.experimental import pallas as pl
from jax.experimental.pallas import tpu as pltpu
from jax.sharding import PartitionSpec as P

HD = 128
PAGE = 16
EPS = 1e-05
F32 = jnp.float32
BF16 = jnp.bfloat16
MESH = pl.DeviceIdType.MESH
VMEM = pltpu.VMEM

TOK = 512
COLS = 512
KCOLS = 64
HEADS = COLS // HD
NH = 4
RH = TOK // NH
NU = 2 * NH
NK = 2 * NU
LAG = 2
AHEAD = 3
PIECES = 4
PR = 128 // PIECES
WO_Z = 3
WO_X = 7
WO_D = 12
NT = 4
RT = TOK // NT
HT = RT // 2
TRADE = 4
ATTEND = 7
FETCH = (10, 12, 14)
COMPUTE = 15
PASS_ON = 17
FINISH = 19
STEPS = LAG + 1 + 4 * (NT - 1) + FINISH + 1


def layer_kernel(
    tok_ref, gain_ref, wq_hbm, wk_ref, wv_ref, wo_hbm, cos_in, sin_in,
    shared_ref, owner_ref, page_id_ref,
    mixed_ref, pool_ref, pool_ids_ref,
    sq, blocks, own, wq_v, wkv_v, acc_q, acc_kv, got_q, got_kv,
    heads, keys, values, kv_own, kv_other, kv_page, scale, pages, ids, pool_in, ids_in, cos_ref, sin_ref,
    ctx, wo, opp_out, opp_in, near_out, near_in, near_part, own_part,
    w_sem, d_send, d_recv, up_send, up_recv, dn_send, dn_recv,
    yp_send, yp_recv, ym_send, ym_recv, fw_send, fw_recv, x_send, x_recv,
    sy_send, sy_recv, sz_send, sz_recv,
    wz_send, wz_recv, wx_send, wx_recv, wd_send, wd_recv, wl_sem,
    kv_send, kv_recv, cu_send, cu_recv, cd_send, cd_recv,
    a_send, a_recv, b_send, b_recv, p_send, p_recv, i_send, i_recv,
):
    core = lax.axis_index("side")
    grp = lax.axis_index("grp")
    tp = lax.axis_index("tp")
    x = grp // 2
    z_hi = lax.rem(grp, 2)
    z = tp // 4
    y = lax.rem(tp, 4)
    m = jnp.where(core == 0, z, 3 - z)
    home = z // 2 == core
    own_zz = lax.rem(z, 2)

    weights = pltpu.make_async_copy(wq_hbm, wq_v, w_sem)
    weights.start()

    z_near = [{"tp": lax.rem(z + d, 4) * 4 + y} for d in (1, 2, 3)]
    z_all = z_hi * 4 + z
    z_ring = []
    for far in (1, 2, 6, 7):
        ahead = lax.rem(z_all + far, 8)
        z_ring.append({"grp": x * 2 + ahead // 4, "tp": lax.rem(ahead, 4) * 4 + y})
    y_near = [{"tp": z * 4 + lax.rem(y + d, 4)} for d in (1, 2, 3)]
    x_near = [{"grp": lax.rem(x + d, 4) * 2 + z_hi} for d in (1, 2, 3)]
    owners = [{"side": 1 - core, "grp": jnp.int32(o)} for o in range(8)]
    sibling = {"side": 1 - core}
    barrier = pltpu.get_barrier_semaphore()
    near = z_near + z_ring + y_near + x_near + owners
    for one in near:
        pl.semaphore_signal(barrier, inc=1, device_id=one, device_id_type=MESH)

    for h in range(NH):
        own[h] = (
            tok_ref[h * RH:(h + 1) * RH, :].astype(F32) * gain_ref[...].astype(F32).reshape(1, COLS)
        ).astype(BF16)

    def remote(src, dst, send, recv, to):
        return pltpu.make_async_remote_copy(
            src_ref=src, dst_ref=dst, send_sem=send, recv_sem=recv,
            device_id=to, device_id_type=MESH)

    def same(ref, send, recv, to):
        return remote(ref, ref, send, recv, to)

    def to_root(h):
        return remote(own.at[h], blocks.at[own_zz, y, core, h], d_send.at[h], d_recv.at[h], sibling)

    xf = tok_ref[...].astype(F32)
    sq[0] = lax.dot_general(
        jnp.ones((8, COLS), F32), xf * xf, (((1,), (1,)), ((), ())),
        precision=lax.Precision.HIGHEST, preferred_element_type=F32,
    )
    acc_q[...] = jnp.zeros_like(acc_q)
    acc_kv[...] = jnp.zeros_like(acc_kv)
    for zz in range(2):
        for yy in range(4):
            cols = slice((zz * 4 + yy) * COLS, (zz * 4 + yy + 1) * COLS)
            wkv_v[zz, yy, :KCOLS, :] = wk_ref[:, cols]
            wkv_v[zz, yy, KCOLS:, :] = wv_ref[:, cols]
    keys[...] = jnp.zeros_like(keys)
    values[...] = jnp.zeros_like(values)
    cos_b, sin_b = cos_in[32:, :], sin_in[32:, :]
    sign = jnp.where(lax.broadcasted_iota(jnp.int32, (PAGE, HD), 1) < HD // 2, -1.0, 1.0)
    for a in range(TOK // PAGE):
        cos_a, sin_a = cos_in[a:a + 1, :], sin_in[a:a + 1, :]
        rows = slice(a * PAGE, (a + 1) * PAGE)
        cos_ref[rows, :] = cos_a * cos_b - sin_a * sin_b
        sin_ref[rows, :] = (sin_a * cos_b + cos_a * sin_b) * sign
    pl.semaphore_wait(barrier, len(near))

    @pl.when(jnp.logical_not(home))
    def _():
        for h in range(NH):
            to_root(h).start()

    @pl.when(home)
    def _():
        for h in range(NH):
            blocks[own_zz, y, core, h] = own[h]

    up = {"tp": jnp.where(core == 0, lax.rem(z + 1, 4), lax.rem(z + 3, 4)) * 4 + y}
    down = {"tp": jnp.where(core == 0, lax.rem(z + 3, 4), lax.rem(z + 1, 4)) * 4 + y}
    yp = y_near[0]
    ym = y_near[2]
    y1, y2, y3 = lax.rem(y + 1, 4), lax.rem(y + 2, 4), lax.rem(y + 3, 4)

    def unit(k):
        b = 1 - lax.rem(k, 4) // 2
        zz = jnp.where(core == 0, b, 1 - b)
        side = jnp.where(lax.rem(k, 2) == 0, core, 1 - core)
        h = k // 4
        return b, zz, side, h

    def from_root(k, carry):
        b, zz, side, h = unit(k)
        ref = blocks.at[zz, y, side, h]

        @pl.when(m == b)
        def _():
            @pl.when(side != core)
            def _():
                same(ref, d_send.at[h], d_recv.at[h], sibling).wait_recv()

            same(ref, up_send.at[k], up_recv.at[k], up).start()

            @pl.when(m == 1)
            def _():
                same(ref, dn_send.at[k], dn_recv.at[k], down).start()
        return carry

    def line(k):
        b, zz, side, h = unit(k)
        ref = blocks.at[zz, y, side, h]

        @pl.when(m > b)
        def _():
            same(ref, up_send.at[k], up_recv.at[k], up).wait_recv()

            @pl.when(m < 3)
            def _():
                same(ref, up_send.at[k], up_recv.at[k], up).start()

        @pl.when(m < b)
        def _():
            same(ref, dn_send.at[k], dn_recv.at[k], down).wait_recv()

    def spread(k):
        b, zz, side, h = unit(k)
        ref = blocks.at[zz, y, side, h]
        same(ref, yp_send.at[k], yp_recv.at[k], yp).start()
        same(ref, ym_send.at[k], ym_recv.at[k], ym).start()

    def ring(k):
        b, zz, side, h = unit(k)
        low = blocks.at[zz, y3, side, h]
        high = blocks.at[zz, y1, side, h]
        same(low, yp_send.at[k], yp_recv.at[k], yp).wait_recv()

        @pl.when(lax.rem(k, 2) == 0)
        def _():
            same(low, fw_send.at[k], fw_recv.at[k], yp).start()

        same(high, ym_send.at[k], ym_recv.at[k], ym).wait_recv()

        @pl.when(lax.rem(k, 2) == 1)
        def _():
            same(high, fw_send.at[k], fw_recv.at[k], ym).start()

    def chunk(t):
        return pl.ds(pl.multiple_of(t * RT, RT), RT)

    def swap_q(t):
        return remote(acc_q.at[1 - core, chunk(t), :], got_q.at[chunk(t), :],
                      x_send.at[0, t], x_recv.at[0, t], sibling)

    def swap_kv(t):
        return remote(acc_kv.at[1 - core, chunk(t), :], got_kv.at[chunk(t), :],
                      x_send.at[1, t], x_recv.at[1, t], sibling)

    def multiply(k):
        b, zz, side, h = unit(k)
        far = blocks.at[zz, y2, side, h]
        same(far, fw_send.at[k], fw_recv.at[k], yp).wait_recv()
        rows = pl.ds(pl.multiple_of(h * RH, RH), RH)
        total_q = acc_q[side, rows, :]
        total_kv = acc_kv[side, rows, :]
        for yy in range(4):
            block = blocks[zz, yy, side, h]
            total_q += jnp.dot(block, wq_v[zz, yy], preferred_element_type=F32)
            total_kv += lax.dot_general(
                block, wkv_v[zz, yy], (((1,), (1,)), ((), ())), preferred_element_type=F32)
        acc_q[side, rows, :] = total_q
        acc_kv[side, rows, :] = total_kv

        @pl.when(lax.rem(k, 4) == 3)
        def _():
            swap_kv(h).start()
            swap_q(h).start()

    def sum_y(d):
        return remote(sq.at[0], sq.at[d], sy_send.at[d - 1], sy_recv.at[d - 1], y_near[d - 1])

    def sum_z(d):
        return remote(sq.at[4], sq.at[4 + d], sz_send.at[d - 1], sz_recv.at[d - 1], z_near[d - 1])

    def piece(zs, xx, j):
        return wo.at[zs, xx, pl.ds(pl.multiple_of(j * PR, PR), PR), :]

    def wo_line(d, j):
        ahead = lax.rem(z_all + (1, jnp.where(lax.rem(j, 2) == 0, 2, 6), 7)[d - 1], 8)
        z_to = lax.rem(z + d, 4)
        col = pl.ds(pl.multiple_of(lax.rem(z_to, 2) * 2048, 2048), 2048)
        return remote(
            wo_hbm.at[x, pl.ds(pl.multiple_of(j * PR, PR), PR), col],
            piece(z, x, j), wz_send.at[d - 1, j], wz_recv.at[d - 1, j],
            {"grp": x * 2 + ahead // 4, "tp": lax.rem(ahead, 4) * 4 + y})

    def wo_sends(d):
        return lax.rem(z + d, 4) // 2 == core

    def wo_landed(d, j):
        zs = lax.rem(z + d, 4)
        return same(piece(zs, x, j), wz_send.at[3 - d, j], wz_recv.at[3 - d, j], z_near[d - 1])

    def wo_row(d, e, j):
        return same(piece(lax.rem(z + d, 4), x, j), wx_send.at[d - 1, e - 1, j],
                    wx_recv.at[d - 1, e - 1, j], x_near[e - 1])

    own_cols = pl.ds(pl.multiple_of(own_zz * 2048, 2048), 2048)

    def wo_local():
        return pltpu.make_async_copy(wo_hbm.at[:, :, own_cols], wo.at[z], wl_sem)

    def wo_cross(d):
        here = wo.at[lax.rem(z + d, 4)]
        return remote(wo_hbm.at[:, :, own_cols] if d == 0 else here, here,
                      wd_send.at[d], wd_recv.at[d], sibling)

    def redistribute(k):
        @pl.when((k >= WO_Z) & (k < WO_Z + PIECES))
        def _():
            for d in (1, 2, 3):
                @pl.when(wo_sends(d))
                def _():
                    wo_line(d, k - WO_Z).start()

        @pl.when(home & (k == WO_Z))
        def _():
            wo_local().start()
            wo_cross(0).start()

        @pl.when(home & (k >= WO_X) & (k < WO_X + PIECES))
        def _():
            for d in (1, 2, 3):
                wo_landed(d, k - WO_X).wait_recv()
                for e in (1, 2, 3):
                    wo_row(d, e, k - WO_X).start()

        for d in (1, 2, 3):
            @pl.when(home & (k == WO_D + d - 1))
            def _():
                for j in range(PIECES):
                    for e in (1, 2, 3):
                        wo_row(d, e, j).wait_recv()
                wo_cross(d).start()

    lax.fori_loop(0, NK, from_root, 0)
    line(0)
    for d in (1, 2, 3):
        sum_y(d).start()
    weights.wait()

    upper = lax.rem(y, 2) == 1
    left = lax.broadcasted_iota(jnp.int32, (RT, HD), 1) < KCOLS

    def trade(t):
        return remote(kv_own.at[chunk(t), :], kv_other.at[chunk(t), :], kv_send.at[t],
                      kv_recv.at[t], {"tp": z * 4 + y + 1 - 2 * lax.rem(y, 2)})

    def start_trade(t):
        @pl.when(t == 0)
        def _():
            for d in (1, 2, 3):
                sum_z(d).wait_recv()
            total = (sq[4] + sq[5] + sq[6] + sq[7]).T[:, :1]
            scale[...] = jnp.broadcast_to(lax.rsqrt(total * (1.0 / 8192.0) + EPS), (TOK, HD))
        swap_kv(t).wait()
        swap_q(t).wait()
        rows = chunk(t)
        mine = (acc_kv[core, rows, :] + got_kv[rows, :]) * scale[rows, :]
        got_kv[rows, :] = mine
        kv_own[rows, :] = mine.astype(BF16)
        trade(t).start()
        cosine = cos_ref[rows, :]
        sine = sin_ref[rows, :]
        for h in range(HEADS):
            cols = slice(h * HD, (h + 1) * HD)
            head = (acc_q[core, rows, cols] + got_q[rows, cols]) * scale[rows, :]
            heads[h, rows, :] = (head * cosine + pltpu.roll(head, HD // 2, 1) * sine).astype(BF16)

    def end_trade(t):
        trade(t).wait()
        rows = chunk(t)
        mine = got_kv[rows, :]
        theirs = kv_other[rows, :].astype(F32)
        low = jnp.where(upper, theirs, mine)
        high = jnp.where(upper, mine, theirs)
        k_full = jnp.where(left, low, pltpu.roll(high, KCOLS, 1))
        v_full = jnp.where(left, pltpu.roll(low, KCOLS, 1), high)
        k_full = k_full * cos_ref[rows, :] + pltpu.roll(k_full, HD // 2, 1) * sin_ref[rows, :]
        keys[rows, :] = k_full.astype(BF16)
        values[rows, :] = v_full.astype(BF16)
        kv_page[rows, :] = jnp.where(
            left,
            jnp.where(upper, pltpu.roll(k_full, KCOLS, 1), k_full),
            jnp.where(upper, v_full, pltpu.roll(v_full, KCOLS, 1)),
        ).astype(BF16)

    climb_to = z_near[0]
    descend_to = z_near[2]

    def climb(zs, t):
        return same(ctx.at[zs, t], cu_send.at[zs, t], cu_recv.at[zs, t], climb_to)

    def descend(zs, t):
        return same(ctx.at[zs, t], cd_send.at[zs, t], cd_recv.at[zs, t], descend_to)

    def attend(t):
        query = heads[:, pl.ds(pl.multiple_of(t * RT, RT), RT), :].reshape(HEADS * RT, HD)
        scores = lax.dot_general(
            query, keys[...], (((1,), (1,)), ((), ())), preferred_element_type=F32
        ) / jnp.sqrt(F32(HD))
        shape = (HEADS * RT, TOK)
        place = t * RT + lax.rem(lax.broadcasted_iota(jnp.int32, shape, 0), RT)
        scores = jnp.where(lax.broadcasted_iota(jnp.int32, shape, 1) <= place, scores, -1e30)
        weight = jnp.exp(scores - jnp.max(scores, axis=-1, keepdims=True))
        share = weight / jnp.sum(weight, axis=-1, keepdims=True)
        out = jnp.dot(share.astype(BF16), values[...], preferred_element_type=F32).astype(BF16)
        for h in range(HEADS):
            ctx[z, t, :, h * HD:(h + 1) * HD] = out[h * RT:(h + 1) * RT]

        @pl.when(z < 3)
        def _():
            climb(z, t).start()

        @pl.when(z > 0)
        def _():
            descend(z, t).start()

    def page(o):
        return remote(pages.at[o], pool_in.at[grp], p_send.at[o], p_recv.at[grp], owners[o])

    def page_id(o):
        return remote(ids.at[o], ids_in.at[grp], i_send.at[o], i_recv.at[grp], owners[o])

    def hand_over():
        live = 1.0 - shared_ref[...].astype(F32)
        owner = owner_ref[...]
        named = lax.broadcasted_iota(jnp.int32, (8, 32), 0) == owner
        onehot = jnp.where(named, live, 0.0)
        upto = (
            lax.broadcasted_iota(jnp.int32, (32, 32), 0)
            <= lax.broadcasted_iota(jnp.int32, (32, 32), 1)
        ).astype(F32)
        count = jnp.dot(onehot, upto, preferred_element_type=F32)
        rank = jnp.sum(count * onehot, axis=0, keepdims=True) - 1.0
        slot = jnp.where(live > 0.5, owner.astype(F32) * 6.0 + rank, -1.0)
        spread = (
            lax.broadcasted_iota(jnp.int32, (32, TOK), 0)
            == lax.broadcasted_iota(jnp.int32, (32, TOK), 1) // PAGE
        ).astype(F32)
        slots = jnp.dot(jnp.broadcast_to(slot, (8, 32)), spread, preferred_element_type=F32)
        inside = lax.rem(lax.broadcasted_iota(jnp.int32, (1, TOK), 1), PAGE)
        row = slots[:1] * float(PAGE) + inside.astype(F32)
        for o in range(8):
            at = (lax.broadcasted_iota(jnp.int32, (96, TOK), 0) + o * 96).astype(F32)
            picks = jnp.where(at == row, 1.0, 0.0).astype(BF16)
            pages[o] = jnp.dot(picks, kv_page[...], preferred_element_type=F32).astype(BF16)
            rank_of = lax.broadcasted_iota(jnp.int32, (8, 32), 0)
            chosen = (slot == (rank_of + o * 6).astype(F32)) & (rank_of < 6)
            found = jnp.sum(jnp.where(chosen, page_id_ref[...] + 1, 0), axis=1, keepdims=True) - 1
            ids[o] = jnp.broadcast_to(found, (8, 128))
            page(o).start()
            page_id(o).start()

    def take_over():
        for o in range(8):
            remote(pages.at[o], pool_in.at[o], p_send.at[o], p_recv.at[o], owners[o]).wait_recv()
            remote(ids.at[o], ids_in.at[o], i_send.at[o], i_recv.at[o], owners[o]).wait_recv()
        token = lax.broadcasted_iota(jnp.int32, (PAGE, 48, 768), 0)
        slot = lax.broadcasted_iota(jnp.int32, (PAGE, 48, 768), 1)
        source = lax.broadcasted_iota(jnp.int32, (PAGE, 48, 768), 2)
        picks = jnp.where(source == slot * PAGE + token, 1.0, 0.0).astype(BF16)
        moved = jnp.dot(
            picks.reshape(768, 768), pool_in[...].reshape(768, 128),
            preferred_element_type=F32).astype(BF16)
        for i in range(PAGE):
            pool_ref[:, i * 128:(i + 1) * 128] = moved[i * 48:(i + 1) * 48]
        line_ids = jnp.zeros((1, 128), jnp.int32)
        lane = lax.broadcasted_iota(jnp.int32, (1, 128), 1)
        for o in range(8):
            for r in range(6):
                line_ids = jnp.where(lane == o * 6 + r, ids_in[o, r:r + 1, :], line_ids)
        pool_ids_ref[...] = line_ids

    def opposite(t, way):
        return remote(opp_out.at[t, way], opp_in.at[t, way], a_send.at[t, way],
                      a_recv.at[t, way], (yp, ym)[way])

    def neighbour(t, way):
        return remote(near_out.at[t, way], near_in.at[t, way], b_send.at[t, way],
                      b_recv.at[t, way], (yp, ym)[way])

    def fetch(t, d):
        if True:
            @pl.when(z - d >= 0)
            def _():
                climb(z - d, t).wait_recv()

                @pl.when(z < 3)
                def _():
                    climb(z - d, t).start()

            @pl.when(z + d <= 3)
            def _():
                descend(z + d, t).wait_recv()

                @pl.when(z > 0)
                def _():
                    descend(z + d, t).start()

    def product(t, r):
        cols = pl.ds(pl.multiple_of(lax.rem(y + r, 4) * COLS, COLS), COLS)
        total = None
        for zs in range(4):
            part = jnp.dot(
                ctx[zs, t], wo[zs, :, :, cols].reshape(COLS, COLS), preferred_element_type=F32)
            total = part if total is None else total + part
        return total

    def compute(t):
        far = product(t, 2).astype(BF16)
        for way in (0, 1):
            opp_out[t, way] = far[way * HT:(way + 1) * HT]
            opposite(t, way).start()
        near_part[t, 0] = product(t, 1)
        near_part[t, 1] = product(t, 3)
        own_part[t] = product(t, 0)

    def pass_on(t):
        for way in (0, 1):
            opposite(t, way).wait_recv()
            with_sum = slice(way * HT, (way + 1) * HT)
            without = slice((1 - way) * HT, (2 - way) * HT)
            near_out[t, way, with_sum, :] = (
                near_part[t, way, with_sum, :] + opp_in[t, way].astype(F32)
            ).astype(BF16)
            near_out[t, way, without, :] = near_part[t, way, without, :].astype(BF16)
            neighbour(t, way).start()

    def finish(t):
        neighbour(t, 0).wait_recv()
        neighbour(t, 1).wait_recv()
        total = own_part[t] + near_in[t, 0].astype(F32) + near_in[t, 1].astype(F32)
        rows = pl.ds(pl.multiple_of(t * RT, RT), RT)
        mixed_ref[rows, :] = (tok_ref[rows, :].astype(F32) + total).astype(BF16)

    def wo_ready():
        @pl.when(home)
        def _():
            wo_local().wait()

        @pl.when(jnp.logical_not(home))
        def _():
            for d in range(4):
                wo_cross(d).wait_recv()

    def step(k, carry):
        @pl.when(k < NK)
        def _():
            spread(k)

        @pl.when(k < NK - AHEAD)
        def _():
            line(k + AHEAD)

        @pl.when((k >= LAG) & (k < NK + LAG))
        def _():
            ring(k - LAG)

        @pl.when((k >= LAG + 1) & (k < NK + LAG + 1))
        def _():
            multiply(k - LAG - 1)

        redistribute(k)

        @pl.when(k == 3)
        def _():
            for d in (1, 2, 3):
                sum_y(d).wait_recv()
            sq[4] = sq[0] + sq[1] + sq[2] + sq[3]
            for d in (1, 2, 3):
                sum_z(d).start()

        def at(offset):
            since = k - (LAG + 1) - offset
            return (since >= 0) & (since <= 4 * (NT - 1)) & (lax.rem(since, 4) == 0), since // 4

        turn, t1 = at(TRADE)

        @pl.when(turn)
        def _():
            start_trade(t1)

        turn, t2 = at(ATTEND)

        @pl.when(turn)
        def _():
            end_trade(t2)
            attend(t2)

        for d in (1, 2, 3):
            turn, t3 = at(FETCH[d - 1])

            @pl.when(turn)
            def _():
                fetch(t3, d)

        @pl.when(k == LAG + 1 + COMPUTE)
        def _():
            wo_ready()

        turn, t4 = at(COMPUTE)

        @pl.when(turn)
        def _():
            compute(t4)

        @pl.when(k == LAG + 2 + 4 * (NT - 1) + ATTEND)
        def _():
            hand_over()

        turn, t5 = at(PASS_ON)

        @pl.when(turn)
        def _():
            pass_on(t5)

        @pl.when(k == LAG + 2 + 4 * (NT - 1) + PASS_ON)
        def _():
            take_over()

        turn, t6 = at(FINISH)

        @pl.when(turn)
        def _():
            finish(t6)
        return carry

    for k in range(1, AHEAD):
        line(k)
    lax.fori_loop(0, STEPS, step, 0)

    def drain(k, carry):
        b, zz, side, h = unit(k)
        ref = blocks.at[zz, y, side, h]

        @pl.when((m >= b) & (m < 3))
        def _():
            same(ref, up_send.at[k], up_recv.at[k], up).wait_send()

        @pl.when((m == 1) & (b == 1))
        def _():
            same(ref, dn_send.at[k], dn_recv.at[k], down).wait_send()

        same(ref, yp_send.at[k], yp_recv.at[k], yp).wait_send()
        same(ref, ym_send.at[k], ym_recv.at[k], ym).wait_send()
        same(ref, fw_send.at[k], fw_recv.at[k], yp).wait_send()
        return carry

    lax.fori_loop(0, NK, drain, 0)

    def drain_out(t, carry):
        for zs in range(4):
            @pl.when((z < 3) & (zs <= z))
            def _():
                climb(zs, t).wait_send()

            @pl.when((z > 0) & (zs >= z))
            def _():
                descend(zs, t).wait_send()

        for way in (0, 1):
            opposite(t, way).wait_send()
            neighbour(t, way).wait_send()
        return carry

    lax.fori_loop(0, NT, drain_out, 0)

    @pl.when(jnp.logical_not(home))
    def _():
        for h in range(NH):
            to_root(h).wait_send()

    for d in (1, 2, 3):
        sum_y(d).wait_send()
        sum_z(d).wait_send()

    def drain_wo(j, carry):
        for d in (1, 2, 3):
            @pl.when(wo_sends(d))
            def _():
                wo_line(d, j).wait_send()

        @pl.when(home)
        def _():
            for d in (1, 2, 3):
                for e in (1, 2, 3):
                    wo_row(d, e, j).wait_send()
        return carry

    lax.fori_loop(0, PIECES, drain_wo, 0)

    @pl.when(home)
    def _():
        for d in range(4):
            wo_cross(d).wait_send()

    for o in range(8):
        page(o).wait_send()
        page_id(o).wait_send()


def layer(tokens, gain, wq, wk, wv, wo, cosine, sine, shared, owner, page_ids):
    sem = pltpu.SemaphoreType.DMA
    vm = pl.BlockSpec(memory_space=VMEM)
    hbm = pl.BlockSpec(memory_space=pl.ANY)
    return pl.pallas_call(
        layer_kernel,
        out_shape=(
            jax.ShapeDtypeStruct((TOK, COLS), BF16),
            jax.ShapeDtypeStruct((48, 2048), BF16),
            jax.ShapeDtypeStruct((1, 128), jnp.int32),
        ),
        in_specs=[vm, vm, hbm, vm, vm, hbm, vm, vm, vm, vm, vm],
        out_specs=(vm, vm, vm),
        scratch_shapes=[
            VMEM((8, 8, TOK), F32),
            VMEM((2, 4, 2, NH, RH, COLS), BF16),
            VMEM((NH, RH, COLS), BF16),
            VMEM((2, 4, COLS, COLS), BF16),
            VMEM((2, 4, 2 * KCOLS, COLS), BF16),
            VMEM((2, TOK, COLS), F32),
            VMEM((2, TOK, 2 * KCOLS), F32),
            VMEM((TOK, COLS), F32),
            VMEM((TOK, 2 * KCOLS), F32),
            VMEM((HEADS, TOK, HD), BF16),
            VMEM((TOK, HD), BF16),
            VMEM((TOK, HD), BF16),
            VMEM((TOK, HD), BF16),
            VMEM((TOK, HD), BF16),
            VMEM((TOK, HD), BF16),
            VMEM((TOK, HD), F32),
            VMEM((8, 96, 128), BF16),
            VMEM((8, 8, 128), jnp.int32),
            VMEM((8, 96, 128), BF16),
            VMEM((8, 8, 128), jnp.int32),
            VMEM((TOK, HD), F32),
            VMEM((TOK, HD), F32),
            VMEM((4, NT, RT, COLS), BF16),
            VMEM((4, 4, 128, 2048), BF16),
            VMEM((NT, 2, HT, COLS), BF16),
            VMEM((NT, 2, HT, COLS), BF16),
            VMEM((NT, 2, RT, COLS), BF16),
            VMEM((NT, 2, RT, COLS), BF16),
            VMEM((NT, 2, RT, COLS), F32),
            VMEM((NT, RT, COLS), F32),
            sem, sem((NH,)), sem((NH,)),
        ] + [sem((NK,))] * 10 + [
            sem((2, NT)), sem((2, NT)), sem((3,)), sem((3,)), sem((3,)), sem((3,)),
            sem((3, PIECES)), sem((3, PIECES)), sem((3, 3, PIECES)), sem((3, 3, PIECES)),
            sem((4,)), sem((4,)), sem, sem((NT,)), sem((NT,)),
            sem((4, NT)), sem((4, NT)), sem((4, NT)), sem((4, NT)),
            sem((NT, 2)), sem((NT, 2)), sem((NT, 2)), sem((NT, 2)),
            sem((8,)), sem((8,)), sem((8,)), sem((8,)),
        ],
        compiler_params=pltpu.CompilerParams(
            collective_id=0, has_side_effects=True, vmem_limit_bytes=56 * 2**20
        ),
    )(
        tokens, gain, wq.reshape(2, 4, COLS, COLS), wk.T, wv.T,
        wo.reshape(4, 128, 4096), cosine, sine, shared, owner, page_ids,
    )


def shards(tokens, norm_gain, wq, wk, wv, wo, span_offsets, shared_pages, page_owner, page_ids):
    half = HD // 2
    freq = jnp.exp(-jnp.log(500000.0) * (2.0 * jnp.arange(half, dtype=F32)) / HD)
    marks = jnp.concatenate(
        [span_offsets[0] + PAGE * jnp.arange(TOK // PAGE, dtype=jnp.int32),
         jnp.arange(PAGE, dtype=jnp.int32)])
    angle = marks.astype(F32)[:, None] * jnp.concatenate([freq, freq])[None, :]
    cosine = jnp.cos(angle)
    sine = jnp.sin(angle)
    mixed, pool, pool_ids = layer(
        tokens, norm_gain, wq, wk, wv, wo, cosine, sine,
        shared_pages, page_owner.reshape(1, 32), page_ids,
    )
    return mixed, pool, pool_ids[0, :48]


def solution(mesh):
    in_specs = (
        P(("side", "grp"), "tp"),
        P("tp"),
        P("side", "tp"),
        P("side", "tp"),
        P("side", "tp"),
        P("tp", "side"),
        P(("side", "grp")),
        P(("side", "grp"), None),
        P(("side", "grp"), None, None),
        P(("side", "grp"), None),
    )
    out_specs = (P(("side", "grp"), "tp"), P(("side", "grp"), "tp"), P(("side", "grp")))
    return jax.shard_map(shards, mesh=mesh, in_specs=in_specs, out_specs=out_specs, check_vma=False)
```

```python
import jax
import jax.numpy as jnp
from jax import lax
from jax.experimental import pallas as pl
from jax.experimental.pallas import tpu as pltpu
from jax.sharding import PartitionSpec as P

HD = 128
PAGE = 16
EPS = 1e-05
F32 = jnp.float32
BF16 = jnp.bfloat16
MESH = pl.DeviceIdType.MESH
VMEM = pltpu.VMEM

TOK = 512
COLS = 512
KCOLS = 64
HEADS = COLS // HD
NH = 4
RH = TOK // NH
NU = 2 * NH
NK = 2 * NU
LAG = 3
AHEAD = 3
PIECES = 4
PR = 128 // PIECES
WO_Z = 4
WO_X = 8
WO_D = 14
NT = 4
RT = TOK // NT
HT = RT // 2
TRADE = 4
ATTEND = 7
FETCH = (10, 12, 14)
COMPUTE = 15
PASS_ON = 17
FINISH = 19
STEPS = LAG + 1 + 4 * (NT - 1) + FINISH + 1


def layer_kernel(
    tok_ref, gain_ref, wq_hbm, wk_ref, wv_ref, wo_hbm, cos_in, sin_in,
    shared_ref, owner_ref, page_id_ref,
    mixed_ref, pool_ref, pool_ids_ref,
    sq, blocks, own, wq_v, wkv_v, acc_q, acc_kv, got_q, got_kv,
    heads, keys, values, kv_own, kv_other, kv_page, scale, pages, ids, pool_in, ids_in, cos_ref, sin_ref,
    ctx, wo, opp_out, opp_in, near_out, near_in, near_part, own_part,
    w_sem, d_send, d_recv, up_send, up_recv, dn_send, dn_recv,
    yp_send, yp_recv, ym_send, ym_recv, fw_send, fw_recv, x_send, x_recv,
    sy_send, sy_recv, sz_send, sz_recv,
    wz_send, wz_recv, wx_send, wx_recv, wd_send, wd_recv, wl_sem,
    kv_send, kv_recv, cu_send, cu_recv, cd_send, cd_recv,
    a_send, a_recv, b_send, b_recv, p_send, p_recv, i_send, i_recv,
):
    core = lax.axis_index("side")
    grp = lax.axis_index("grp")
    tp = lax.axis_index("tp")
    x = grp // 2
    z_hi = lax.rem(grp, 2)
    z = tp // 4
    y = lax.rem(tp, 4)
    m = jnp.where(core == 0, z, 3 - z)
    home = z // 2 == core
    own_zz = lax.rem(z, 2)

    weights = pltpu.make_async_copy(wq_hbm, wq_v, w_sem)
    weights.start()

    z_near = [{"tp": lax.rem(z + d, 4) * 4 + y} for d in (1, 2, 3)]
    z_all = z_hi * 4 + z
    z_ring = []
    for far in (1, 2, 6, 7):
        ahead = lax.rem(z_all + far, 8)
        z_ring.append({"grp": x * 2 + ahead // 4, "tp": lax.rem(ahead, 4) * 4 + y})
    y_near = [{"tp": z * 4 + lax.rem(y + d, 4)} for d in (1, 2, 3)]
    x_near = [{"grp": lax.rem(x + d, 4) * 2 + z_hi} for d in (1, 2, 3)]
    owners = [{"side": 1 - core, "grp": jnp.int32(o)} for o in range(8)]
    sibling = {"side": 1 - core}
    barrier = pltpu.get_barrier_semaphore()
    near = z_near + z_ring + y_near + x_near + owners
    for one in near:
        pl.semaphore_signal(barrier, inc=1, device_id=one, device_id_type=MESH)

    for h in range(NH):
        own[h] = (
            tok_ref[h * RH:(h + 1) * RH, :].astype(F32) * gain_ref[...].astype(F32).reshape(1, COLS)
        ).astype(BF16)

    def remote(src, dst, send, recv, to):
        return pltpu.make_async_remote_copy(
            src_ref=src, dst_ref=dst, send_sem=send, recv_sem=recv,
            device_id=to, device_id_type=MESH)

    def same(ref, send, recv, to):
        return remote(ref, ref, send, recv, to)

    def to_root(h):
        return remote(own.at[h], blocks.at[own_zz, y, core, h], d_send.at[h], d_recv.at[h], sibling)

    xf = tok_ref[...].astype(F32)
    sq[0] = lax.dot_general(
        jnp.ones((8, COLS), F32), xf * xf, (((1,), (1,)), ((), ())),
        precision=lax.Precision.HIGHEST, preferred_element_type=F32,
    )
    acc_q[...] = jnp.zeros_like(acc_q)
    acc_kv[...] = jnp.zeros_like(acc_kv)
    for zz in range(2):
        for yy in range(4):
            cols = slice((zz * 4 + yy) * COLS, (zz * 4 + yy + 1) * COLS)
            wkv_v[zz, yy, :KCOLS, :] = wk_ref[:, cols]
            wkv_v[zz, yy, KCOLS:, :] = wv_ref[:, cols]
    keys[...] = jnp.zeros_like(keys)
    values[...] = jnp.zeros_like(values)
    cos_b, sin_b = cos_in[32:, :], sin_in[32:, :]
    sign = jnp.where(lax.broadcasted_iota(jnp.int32, (PAGE, HD), 1) < HD // 2, -1.0, 1.0)
    for a in range(TOK // PAGE):
        cos_a, sin_a = cos_in[a:a + 1, :], sin_in[a:a + 1, :]
        rows = slice(a * PAGE, (a + 1) * PAGE)
        cos_ref[rows, :] = cos_a * cos_b - sin_a * sin_b
        sin_ref[rows, :] = (sin_a * cos_b + cos_a * sin_b) * sign
    pl.semaphore_wait(barrier, len(near))

    @pl.when(jnp.logical_not(home))
    def _():
        for h in range(NH):
            to_root(h).start()

    @pl.when(home)
    def _():
        for h in range(NH):
            blocks[own_zz, y, core, h] = own[h]

    up = {"tp": jnp.where(core == 0, lax.rem(z + 1, 4), lax.rem(z + 3, 4)) * 4 + y}
    down = {"tp": jnp.where(core == 0, lax.rem(z + 3, 4), lax.rem(z + 1, 4)) * 4 + y}
    yp = y_near[0]
    ym = y_near[2]
    y1, y2, y3 = lax.rem(y + 1, 4), lax.rem(y + 2, 4), lax.rem(y + 3, 4)

    def unit(k):
        b = 1 - lax.rem(k, 4) // 2
        zz = jnp.where(core == 0, b, 1 - b)
        side = jnp.where(lax.rem(k, 2) == 0, core, 1 - core)
        h = k // 4
        return b, zz, side, h

    def from_root(k, carry):
        b, zz, side, h = unit(k)
        ref = blocks.at[zz, y, side, h]

        @pl.when(m == b)
        def _():
            @pl.when(side != core)
            def _():
                same(ref, d_send.at[h], d_recv.at[h], sibling).wait_recv()

            same(ref, up_send.at[k], up_recv.at[k], up).start()

            @pl.when(m == 1)
            def _():
                same(ref, dn_send.at[k], dn_recv.at[k], down).start()
        return carry

    def line(k):
        b, zz, side, h = unit(k)
        ref = blocks.at[zz, y, side, h]

        @pl.when(m > b)
        def _():
            same(ref, up_send.at[k], up_recv.at[k], up).wait_recv()

            @pl.when(m < 3)
            def _():
                same(ref, up_send.at[k], up_recv.at[k], up).start()

        @pl.when(m < b)
        def _():
            same(ref, dn_send.at[k], dn_recv.at[k], down).wait_recv()

    def spread(k):
        b, zz, side, h = unit(k)
        ref = blocks.at[zz, y, side, h]
        same(ref, yp_send.at[k], yp_recv.at[k], yp).start()
        same(ref, ym_send.at[k], ym_recv.at[k], ym).start()

    def ring(k):
        b, zz, side, h = unit(k)
        low = blocks.at[zz, y3, side, h]
        high = blocks.at[zz, y1, side, h]
        same(low, yp_send.at[k], yp_recv.at[k], yp).wait_recv()

        @pl.when(lax.rem(k, 2) == 0)
        def _():
            same(low, fw_send.at[k], fw_recv.at[k], yp).start()

        same(high, ym_send.at[k], ym_recv.at[k], ym).wait_recv()

        @pl.when(lax.rem(k, 2) == 1)
        def _():
            same(high, fw_send.at[k], fw_recv.at[k], ym).start()

    def chunk(t):
        return pl.ds(pl.multiple_of(t * RT, RT), RT)

    def swap_q(t):
        return remote(acc_q.at[1 - core, chunk(t), :], got_q.at[chunk(t), :],
                      x_send.at[0, t], x_recv.at[0, t], sibling)

    def swap_kv(t):
        return remote(acc_kv.at[1 - core, chunk(t), :], got_kv.at[chunk(t), :],
                      x_send.at[1, t], x_recv.at[1, t], sibling)

    def multiply(k):
        b, zz, side, h = unit(k)
        far = blocks.at[zz, y2, side, h]
        same(far, fw_send.at[k], fw_recv.at[k], yp).wait_recv()
        rows = pl.ds(pl.multiple_of(h * RH, RH), RH)
        total_q = acc_q[side, rows, :]
        total_kv = acc_kv[side, rows, :]
        for yy in range(4):
            block = blocks[zz, yy, side, h]
            total_q += jnp.dot(block, wq_v[zz, yy], preferred_element_type=F32)
            total_kv += lax.dot_general(
                block, wkv_v[zz, yy], (((1,), (1,)), ((), ())), preferred_element_type=F32)
        acc_q[side, rows, :] = total_q
        acc_kv[side, rows, :] = total_kv

        @pl.when(lax.rem(k, 4) == 3)
        def _():
            swap_kv(h).start()
            swap_q(h).start()

    def sum_y(d):
        return remote(sq.at[0], sq.at[d], sy_send.at[d - 1], sy_recv.at[d - 1], y_near[d - 1])

    def sum_z(d):
        return remote(sq.at[4], sq.at[4 + d], sz_send.at[d - 1], sz_recv.at[d - 1], z_near[d - 1])

    def piece(zs, xx, j):
        return wo.at[zs, xx, pl.ds(pl.multiple_of(j * PR, PR), PR), :]

    def wo_line(d, j):
        ahead = lax.rem(z_all + (1, jnp.where(lax.rem(j, 2) == 0, 2, 6), 7)[d - 1], 8)
        z_to = lax.rem(z + d, 4)
        col = pl.ds(pl.multiple_of(lax.rem(z_to, 2) * 2048, 2048), 2048)
        return remote(
            wo_hbm.at[x, pl.ds(pl.multiple_of(j * PR, PR), PR), col],
            piece(z, x, j), wz_send.at[d - 1, j], wz_recv.at[d - 1, j],
            {"grp": x * 2 + ahead // 4, "tp": lax.rem(ahead, 4) * 4 + y})

    def wo_sends(d):
        return lax.rem(z + d, 4) // 2 == core

    def wo_landed(d, j):
        zs = lax.rem(z + d, 4)
        return same(piece(zs, x, j), wz_send.at[3 - d, j], wz_recv.at[3 - d, j], z_near[d - 1])

    def wo_row(d, e, j):
        return same(piece(lax.rem(z + d, 4), x, j), wx_send.at[d - 1, e - 1, j],
                    wx_recv.at[d - 1, e - 1, j], x_near[e - 1])

    own_cols = pl.ds(pl.multiple_of(own_zz * 2048, 2048), 2048)

    def wo_local():
        return pltpu.make_async_copy(wo_hbm.at[:, :, own_cols], wo.at[z], wl_sem)

    def wo_cross(d):
        here = wo.at[lax.rem(z + d, 4)]
        return remote(wo_hbm.at[:, :, own_cols] if d == 0 else here, here,
                      wd_send.at[d], wd_recv.at[d], sibling)

    def redistribute(k):
        @pl.when((k >= WO_Z) & (k < WO_Z + PIECES))
        def _():
            for d in (1, 2, 3):
                @pl.when(wo_sends(d))
                def _():
                    wo_line(d, k - WO_Z).start()

        @pl.when(home & (k == WO_Z))
        def _():
            wo_local().start()
            wo_cross(0).start()

        @pl.when(home & (k >= WO_X) & (k < WO_X + PIECES))
        def _():
            for d in (1, 2, 3):
                wo_landed(d, k - WO_X).wait_recv()
                for e in (1, 2, 3):
                    wo_row(d, e, k - WO_X).start()

        for d in (1, 2, 3):
            @pl.when(home & (k == WO_D + d - 1))
            def _():
                for j in range(PIECES):
                    for e in (1, 2, 3):
                        wo_row(d, e, j).wait_recv()
                wo_cross(d).start()

    lax.fori_loop(0, NK, from_root, 0)
    line(0)
    for d in (1, 2, 3):
        sum_y(d).start()
    weights.wait()

    upper = lax.rem(y, 2) == 1
    left = lax.broadcasted_iota(jnp.int32, (RT, HD), 1) < KCOLS

    def trade(t):
        return remote(kv_own.at[chunk(t), :], kv_other.at[chunk(t), :], kv_send.at[t],
                      kv_recv.at[t], {"tp": z * 4 + y + 1 - 2 * lax.rem(y, 2)})

    def start_trade(t):
        @pl.when(t == 0)
        def _():
            for d in (1, 2, 3):
                sum_z(d).wait_recv()
            total = (sq[4] + sq[5] + sq[6] + sq[7]).T[:, :1]
            scale[...] = jnp.broadcast_to(lax.rsqrt(total * (1.0 / 8192.0) + EPS), (TOK, HD))
        swap_kv(t).wait()
        swap_q(t).wait()
        rows = chunk(t)
        mine = (acc_kv[core, rows, :] + got_kv[rows, :]) * scale[rows, :]
        got_kv[rows, :] = mine
        kv_own[rows, :] = mine.astype(BF16)
        trade(t).start()
        cosine = cos_ref[rows, :]
        sine = sin_ref[rows, :]
        for h in range(HEADS):
            cols = slice(h * HD, (h + 1) * HD)
            head = (acc_q[core, rows, cols] + got_q[rows, cols]) * scale[rows, :]
            heads[h, rows, :] = (head * cosine + pltpu.roll(head, HD // 2, 1) * sine).astype(BF16)

    def end_trade(t):
        trade(t).wait()
        rows = chunk(t)
        mine = got_kv[rows, :]
        theirs = kv_other[rows, :].astype(F32)
        low = jnp.where(upper, theirs, mine)
        high = jnp.where(upper, mine, theirs)
        k_full = jnp.where(left, low, pltpu.roll(high, KCOLS, 1))
        v_full = jnp.where(left, pltpu.roll(low, KCOLS, 1), high)
        k_full = k_full * cos_ref[rows, :] + pltpu.roll(k_full, HD // 2, 1) * sin_ref[rows, :]
        keys[rows, :] = k_full.astype(BF16)
        values[rows, :] = v_full.astype(BF16)
        kv_page[rows, :] = jnp.where(
            left,
            jnp.where(upper, pltpu.roll(k_full, KCOLS, 1), k_full),
            jnp.where(upper, v_full, pltpu.roll(v_full, KCOLS, 1)),
        ).astype(BF16)

    climb_to = z_near[0]
    descend_to = z_near[2]

    def climb(zs, t):
        return same(ctx.at[zs, t], cu_send.at[zs, t], cu_recv.at[zs, t], climb_to)

    def descend(zs, t):
        return same(ctx.at[zs, t], cd_send.at[zs, t], cd_recv.at[zs, t], descend_to)

    def attend(t):
        query = heads[:, pl.ds(pl.multiple_of(t * RT, RT), RT), :].reshape(HEADS * RT, HD)
        scores = lax.dot_general(
            query, keys[...], (((1,), (1,)), ((), ())), preferred_element_type=F32
        ) / jnp.sqrt(F32(HD))
        shape = (HEADS * RT, TOK)
        place = t * RT + lax.rem(lax.broadcasted_iota(jnp.int32, shape, 0), RT)
        scores = jnp.where(lax.broadcasted_iota(jnp.int32, shape, 1) <= place, scores, -1e30)
        weight = jnp.exp(scores - jnp.max(scores, axis=-1, keepdims=True))
        share = weight / jnp.sum(weight, axis=-1, keepdims=True)
        out = jnp.dot(share.astype(BF16), values[...], preferred_element_type=F32).astype(BF16)
        for h in range(HEADS):
            ctx[z, t, :, h * HD:(h + 1) * HD] = out[h * RT:(h + 1) * RT]

        @pl.when(z < 3)
        def _():
            climb(z, t).start()

        @pl.when(z > 0)
        def _():
            descend(z, t).start()

    def page(o):
        return remote(pages.at[o], pool_in.at[grp], p_send.at[o], p_recv.at[grp], owners[o])

    def page_id(o):
        return remote(ids.at[o], ids_in.at[grp], i_send.at[o], i_recv.at[grp], owners[o])

    def hand_over():
        live = 1.0 - shared_ref[...].astype(F32)
        owner = owner_ref[...]
        named = lax.broadcasted_iota(jnp.int32, (8, 32), 0) == owner
        onehot = jnp.where(named, live, 0.0)
        upto = (
            lax.broadcasted_iota(jnp.int32, (32, 32), 0)
            <= lax.broadcasted_iota(jnp.int32, (32, 32), 1)
        ).astype(F32)
        count = jnp.dot(onehot, upto, preferred_element_type=F32)
        rank = jnp.sum(count * onehot, axis=0, keepdims=True) - 1.0
        slot = jnp.where(live > 0.5, owner.astype(F32) * 6.0 + rank, -1.0)
        spread = (
            lax.broadcasted_iota(jnp.int32, (32, TOK), 0)
            == lax.broadcasted_iota(jnp.int32, (32, TOK), 1) // PAGE
        ).astype(F32)
        slots = jnp.dot(jnp.broadcast_to(slot, (8, 32)), spread, preferred_element_type=F32)
        inside = lax.rem(lax.broadcasted_iota(jnp.int32, (1, TOK), 1), PAGE)
        row = slots[:1] * float(PAGE) + inside.astype(F32)
        for o in range(8):
            at = (lax.broadcasted_iota(jnp.int32, (96, TOK), 0) + o * 96).astype(F32)
            picks = jnp.where(at == row, 1.0, 0.0).astype(BF16)
            pages[o] = jnp.dot(picks, kv_page[...], preferred_element_type=F32).astype(BF16)
            rank_of = lax.broadcasted_iota(jnp.int32, (8, 32), 0)
            chosen = (slot == (rank_of + o * 6).astype(F32)) & (rank_of < 6)
            found = jnp.sum(jnp.where(chosen, page_id_ref[...] + 1, 0), axis=1, keepdims=True) - 1
            ids[o] = jnp.broadcast_to(found, (8, 128))
            page(o).start()
            page_id(o).start()

    def take_over():
        for o in range(8):
            remote(pages.at[o], pool_in.at[o], p_send.at[o], p_recv.at[o], owners[o]).wait_recv()
            remote(ids.at[o], ids_in.at[o], i_send.at[o], i_recv.at[o], owners[o]).wait_recv()
        token = lax.broadcasted_iota(jnp.int32, (PAGE, 48, 768), 0)
        slot = lax.broadcasted_iota(jnp.int32, (PAGE, 48, 768), 1)
        source = lax.broadcasted_iota(jnp.int32, (PAGE, 48, 768), 2)
        picks = jnp.where(source == slot * PAGE + token, 1.0, 0.0).astype(BF16)
        moved = jnp.dot(
            picks.reshape(768, 768), pool_in[...].reshape(768, 128),
            preferred_element_type=F32).astype(BF16)
        for i in range(PAGE):
            pool_ref[:, i * 128:(i + 1) * 128] = moved[i * 48:(i + 1) * 48]
        line_ids = jnp.zeros((1, 128), jnp.int32)
        lane = lax.broadcasted_iota(jnp.int32, (1, 128), 1)
        for o in range(8):
            for r in range(6):
                line_ids = jnp.where(lane == o * 6 + r, ids_in[o, r:r + 1, :], line_ids)
        pool_ids_ref[...] = line_ids

    def opposite(t, way):
        return remote(opp_out.at[t, way], opp_in.at[t, way], a_send.at[t, way],
                      a_recv.at[t, way], (yp, ym)[way])

    def neighbour(t, way):
        return remote(near_out.at[t, way], near_in.at[t, way], b_send.at[t, way],
                      b_recv.at[t, way], (yp, ym)[way])

    def fetch(t, d):
        if True:
            @pl.when(z - d >= 0)
            def _():
                climb(z - d, t).wait_recv()

                @pl.when(z < 3)
                def _():
                    climb(z - d, t).start()

            @pl.when(z + d <= 3)
            def _():
                descend(z + d, t).wait_recv()

                @pl.when(z > 0)
                def _():
                    descend(z + d, t).start()

    def product(t, r):
        cols = pl.ds(pl.multiple_of(lax.rem(y + r, 4) * COLS, COLS), COLS)
        total = None
        for zs in range(4):
            part = jnp.dot(
                ctx[zs, t], wo[zs, :, :, cols].reshape(COLS, COLS), preferred_element_type=F32)
            total = part if total is None else total + part
        return total

    def compute(t):
        far = product(t, 2).astype(BF16)
        for way in (0, 1):
            opp_out[t, way] = far[way * HT:(way + 1) * HT]
            opposite(t, way).start()
        near_part[t, 0] = product(t, 1)
        near_part[t, 1] = product(t, 3)
        own_part[t] = product(t, 0)

    def pass_on(t):
        for way in (0, 1):
            opposite(t, way).wait_recv()
            with_sum = slice(way * HT, (way + 1) * HT)
            without = slice((1 - way) * HT, (2 - way) * HT)
            near_out[t, way, with_sum, :] = (
                near_part[t, way, with_sum, :] + opp_in[t, way].astype(F32)
            ).astype(BF16)
            near_out[t, way, without, :] = near_part[t, way, without, :].astype(BF16)
            neighbour(t, way).start()

    def finish(t):
        neighbour(t, 0).wait_recv()
        neighbour(t, 1).wait_recv()
        total = own_part[t] + near_in[t, 0].astype(F32) + near_in[t, 1].astype(F32)
        rows = pl.ds(pl.multiple_of(t * RT, RT), RT)
        mixed_ref[rows, :] = (tok_ref[rows, :].astype(F32) + total).astype(BF16)

    def wo_ready():
        @pl.when(home)
        def _():
            wo_local().wait()

        @pl.when(jnp.logical_not(home))
        def _():
            for d in range(4):
                wo_cross(d).wait_recv()

    def step(k, carry):
        @pl.when(k < NK)
        def _():
            spread(k)

        @pl.when(k < NK - AHEAD)
        def _():
            line(k + AHEAD)

        @pl.when((k >= LAG) & (k < NK + LAG))
        def _():
            ring(k - LAG)

        @pl.when((k >= LAG + 1) & (k < NK + LAG + 1))
        def _():
            multiply(k - LAG - 1)

        redistribute(k)

        @pl.when(k == 3)
        def _():
            for d in (1, 2, 3):
                sum_y(d).wait_recv()
            sq[4] = sq[0] + sq[1] + sq[2] + sq[3]
            for d in (1, 2, 3):
                sum_z(d).start()

        def at(offset):
            since = k - (LAG + 1) - offset
            return (since >= 0) & (since <= 4 * (NT - 1)) & (lax.rem(since, 4) == 0), since // 4

        turn, t1 = at(TRADE)

        @pl.when(turn)
        def _():
            start_trade(t1)

        turn, t2 = at(ATTEND)

        @pl.when(turn)
        def _():
            end_trade(t2)
            attend(t2)

        for d in (1, 2, 3):
            turn, t3 = at(FETCH[d - 1])

            @pl.when(turn)
            def _():
                fetch(t3, d)

        @pl.when(k == LAG + 1 + COMPUTE)
        def _():
            wo_ready()

        turn, t4 = at(COMPUTE)

        @pl.when(turn)
        def _():
            compute(t4)

        @pl.when(k == LAG + 2 + 4 * (NT - 1) + ATTEND)
        def _():
            hand_over()

        turn, t5 = at(PASS_ON)

        @pl.when(turn)
        def _():
            pass_on(t5)

        @pl.when(k == LAG + 2 + 4 * (NT - 1) + PASS_ON)
        def _():
            take_over()

        turn, t6 = at(FINISH)

        @pl.when(turn)
        def _():
            finish(t6)
        return carry

    for k in range(1, AHEAD):
        line(k)
    lax.fori_loop(0, STEPS, step, 0)

    def drain(k, carry):
        b, zz, side, h = unit(k)
        ref = blocks.at[zz, y, side, h]

        @pl.when((m >= b) & (m < 3))
        def _():
            same(ref, up_send.at[k], up_recv.at[k], up).wait_send()

        @pl.when((m == 1) & (b == 1))
        def _():
            same(ref, dn_send.at[k], dn_recv.at[k], down).wait_send()

        same(ref, yp_send.at[k], yp_recv.at[k], yp).wait_send()
        same(ref, ym_send.at[k], ym_recv.at[k], ym).wait_send()
        same(ref, fw_send.at[k], fw_recv.at[k], yp).wait_send()
        return carry

    lax.fori_loop(0, NK, drain, 0)

    def drain_out(t, carry):
        for zs in range(4):
            @pl.when((z < 3) & (zs <= z))
            def _():
                climb(zs, t).wait_send()

            @pl.when((z > 0) & (zs >= z))
            def _():
                descend(zs, t).wait_send()

        for way in (0, 1):
            opposite(t, way).wait_send()
            neighbour(t, way).wait_send()
        return carry

    lax.fori_loop(0, NT, drain_out, 0)

    @pl.when(jnp.logical_not(home))
    def _():
        for h in range(NH):
            to_root(h).wait_send()

    for d in (1, 2, 3):
        sum_y(d).wait_send()
        sum_z(d).wait_send()

    def drain_wo(j, carry):
        for d in (1, 2, 3):
            @pl.when(wo_sends(d))
            def _():
                wo_line(d, j).wait_send()

        @pl.when(home)
        def _():
            for d in (1, 2, 3):
                for e in (1, 2, 3):
                    wo_row(d, e, j).wait_send()
        return carry

    lax.fori_loop(0, PIECES, drain_wo, 0)

    @pl.when(home)
    def _():
        for d in range(4):
            wo_cross(d).wait_send()

    for o in range(8):
        page(o).wait_send()
        page_id(o).wait_send()


def layer(tokens, gain, wq, wk, wv, wo, cosine, sine, shared, owner, page_ids):
    sem = pltpu.SemaphoreType.DMA
    vm = pl.BlockSpec(memory_space=VMEM)
    hbm = pl.BlockSpec(memory_space=pl.ANY)
    return pl.pallas_call(
        layer_kernel,
        out_shape=(
            jax.ShapeDtypeStruct((TOK, COLS), BF16),
            jax.ShapeDtypeStruct((48, 2048), BF16),
            jax.ShapeDtypeStruct((1, 128), jnp.int32),
        ),
        in_specs=[vm, vm, hbm, vm, vm, hbm, vm, vm, vm, vm, vm],
        out_specs=(vm, vm, vm),
        scratch_shapes=[
            VMEM((8, 8, TOK), F32),
            VMEM((2, 4, 2, NH, RH, COLS), BF16),
            VMEM((NH, RH, COLS), BF16),
            VMEM((2, 4, COLS, COLS), BF16),
            VMEM((2, 4, 2 * KCOLS, COLS), BF16),
            VMEM((2, TOK, COLS), F32),
            VMEM((2, TOK, 2 * KCOLS), F32),
            VMEM((TOK, COLS), F32),
            VMEM((TOK, 2 * KCOLS), F32),
            VMEM((HEADS, TOK, HD), BF16),
            VMEM((TOK, HD), BF16),
            VMEM((TOK, HD), BF16),
            VMEM((TOK, HD), BF16),
            VMEM((TOK, HD), BF16),
            VMEM((TOK, HD), BF16),
            VMEM((TOK, HD), F32),
            VMEM((8, 96, 128), BF16),
            VMEM((8, 8, 128), jnp.int32),
            VMEM((8, 96, 128), BF16),
            VMEM((8, 8, 128), jnp.int32),
            VMEM((TOK, HD), F32),
            VMEM((TOK, HD), F32),
            VMEM((4, NT, RT, COLS), BF16),
            VMEM((4, 4, 128, 2048), BF16),
            VMEM((NT, 2, HT, COLS), BF16),
            VMEM((NT, 2, HT, COLS), BF16),
            VMEM((NT, 2, RT, COLS), BF16),
            VMEM((NT, 2, RT, COLS), BF16),
            VMEM((NT, 2, RT, COLS), F32),
            VMEM((NT, RT, COLS), F32),
            sem, sem((NH,)), sem((NH,)),
        ] + [sem((NK,))] * 10 + [
            sem((2, NT)), sem((2, NT)), sem((3,)), sem((3,)), sem((3,)), sem((3,)),
            sem((3, PIECES)), sem((3, PIECES)), sem((3, 3, PIECES)), sem((3, 3, PIECES)),
            sem((4,)), sem((4,)), sem, sem((NT,)), sem((NT,)),
            sem((4, NT)), sem((4, NT)), sem((4, NT)), sem((4, NT)),
            sem((NT, 2)), sem((NT, 2)), sem((NT, 2)), sem((NT, 2)),
            sem((8,)), sem((8,)), sem((8,)), sem((8,)),
        ],
        compiler_params=pltpu.CompilerParams(
            collective_id=0, has_side_effects=True, vmem_limit_bytes=56 * 2**20
        ),
    )(
        tokens, gain, wq.reshape(2, 4, COLS, COLS), wk.T, wv.T,
        wo.reshape(4, 128, 4096), cosine, sine, shared, owner, page_ids,
    )


def shards(tokens, norm_gain, wq, wk, wv, wo, span_offsets, shared_pages, page_owner, page_ids):
    half = HD // 2
    freq = jnp.exp(-jnp.log(500000.0) * (2.0 * jnp.arange(half, dtype=F32)) / HD)
    marks = jnp.concatenate(
        [span_offsets[0] + PAGE * jnp.arange(TOK // PAGE, dtype=jnp.int32),
         jnp.arange(PAGE, dtype=jnp.int32)])
    angle = marks.astype(F32)[:, None] * jnp.concatenate([freq, freq])[None, :]
    cosine = jnp.cos(angle)
    sine = jnp.sin(angle)
    mixed, pool, pool_ids = layer(
        tokens, norm_gain, wq, wk, wv, wo, cosine, sine,
        shared_pages, page_owner.reshape(1, 32), page_ids,
    )
    return mixed, pool, pool_ids[0, :48]


def solution(mesh):
    in_specs = (
        P(("side", "grp"), "tp"),
        P("tp"),
        P("side", "tp"),
        P("side", "tp"),
        P("side", "tp"),
        P("tp", "side"),
        P(("side", "grp")),
        P(("side", "grp"), None),
        P(("side", "grp"), None, None),
        P(("side", "grp"), None),
    )
    out_specs = (P(("side", "grp"), "tp"), P(("side", "grp"), "tp"), P(("side", "grp")))
    return jax.shard_map(shards, mesh=mesh, in_specs=in_specs, out_specs=out_specs, check_vma=False)
```
